32 devices in a mesh: seq: 8 (over z, x), rows: 4 (over y, core).
Axes of the slice: x: 2, y: 2, z: 4, core: 2. Of those that a mesh axis runs over, the one named last changes fastest.
Arguments:
- states: bfloat16 [8, 4096, 768], P('rows', 'seq'), may hold values from -6 to 6
- cotangent: bfloat16 [8, 4096, 768], P('rows', 'seq'), may hold values from -6 to 6
- subsets: int32 [8], P('rows'), may hold values from 0 to 21
- subset_weight: float32 [22], replicated, may hold values from 0.5 to 2
- gain_attn: float32 [768], replicated, may hold values from 0.1 to 1.9
- shift_attn: float32 [768], replicated, may hold values from -3 to 3
- gain_ffn: float32 [768], replicated, may hold values from 0.1 to 1.9
- shift_ffn: float32 [768], replicated, may hold values from -3 to 3
- query_projection: bfloat16 [768, 768], P(('seq', 'rows')), may hold values from -0.21875 to 0.21875
- pair_projection: bfloat16 [768, 128], P(('seq', 'rows')), may hold values from -0.21875 to 0.21875
- output_projection: bfloat16 [768, 768], P(('seq', 'rows')), may hold values from -6 to 6
- up_projection: bfloat16 [768, 3072], P(('seq', 'rows')), may hold values from -0.21875 to 0.21875
- down_projection: bfloat16 [3072, 768], P(('seq', 'rows')), may hold values from -0.109375 to 0.109375
Outputs:
- layer_out: bfloat16 [8, 4096, 768], P('rows', 'seq')
- grad_states: bfloat16 [8, 4096, 768], P('rows', 'seq')
- grad_gain_attn: float32 [768], P(('seq', 'rows'))
- grad_shift_attn: float32 [768], P(('seq', 'rows'))
- grad_gain_ffn: float32 [768], P(('seq', 'rows'))
- grad_shift_ffn: float32 [768], P(('seq', 'rows'))
- grad_query: float32 [768, 768], P(('seq', 'rows'))
- grad_pair: float32 [768, 128], P(('seq', 'rows'))
- grad_output: float32 [768, 768], P(('seq', 'rows'))
- grad_up: float32 [768, 3072], P(('seq', 'rows'))
- grad_down: float32 [3072, 768], P(('seq', 'rows'))
The draws below stay inside these ranges and needn't reach their ends.
Inputs may be any that keep to these rules, and one draw needn't show every extreme that they name: `subsets`: a sequence's Pile subset, one of 22.
All inputs are finite; a program needn't handle non-finite values.
Results may differ from the reference program's by a relative error of at most 0.011.
Values may be sent and summed in bfloat16 or wider, within the bound.
A program may use at most 192 MiB of HBM per device.

```python
import math
import jax
import jax.numpy as jnp
import numpy as np
from jax import lax

D = 768
H = 12
HD = 64
ROT = 16
FF = 3072
NSUB = 22
LEN = 4096
SEQS = 8


def place_ends(values, stream_key, smallest, high):
    longest = values.shape.index(max(values.shape))
    spots = []
    for shift in (0, 1):
        where = [jax.random.randint(jax.random.fold_in(stream_key, axis), (), 0, length) for axis, length in enumerate(values.shape)]
        where[longest] = (where[longest] + shift) % values.shape[longest]
        spots.append(tuple(where))
    return values.at[spots[0]].set(smallest).at[spots[1]].set(high)


def shard_levels(rng, extent, cuts, least, high):
    loudness, own = 1.0, jax.random.fold_in(rng, 6)
    for axis_at, shards_of in cuts:
        steps = jnp.exp(jax.random.uniform(jax.random.fold_in(own, axis_at), (shards_of,), jnp.float32, least / len(cuts), high / len(cuts)))
        loudness = loudness * jnp.repeat(steps, extent[axis_at] // shards_of).reshape([-1 if axis == axis_at else 1 for axis in range(len(extent))])
    return loudness


def rank_bounds(count, skew):
    weights = [(1 << 20) // math.isqrt(grade ** skew) + 1 for grade in range(1, count + 1)]
    deviation = 1 + sum(weights) // (1 << 30)
    return np.cumsum(np.array([max(1, weight // deviation) for weight in weights]))


def ranked(own_key, dims, amount, lean):
    listing = rank_bounds(amount, lean)
    pick = jax.random.randint(jax.random.fold_in(own_key, 1), dims, 0, int(listing[amount - 1]))
    grade = jnp.searchsorted(jnp.asarray(listing, jnp.int32), pick, side="right")
    return jax.random.permutation(jax.random.fold_in(own_key, 2), amount)[grade].astype(jnp.int32)


def noise(stream_key, shape, scale, reach, cuts=(), held_as=jnp.bfloat16):
    result = scale * jax.random.normal(stream_key, shape, jnp.float32)
    if cuts:
        result = result * shard_levels(stream_key, shape, cuts, -0.22, 0.18)
    return jnp.clip(result, -reach, reach).astype(held_as)


def setup_inputs(seed: int = 0) -> dict:
    key_list = jax.random.split(jax.random.key(seed), 14)
    return {
        "states": noise(key_list[0], (SEQS, LEN, D), 1.0, 6.0, ((0, 4), (1, 8))),
        "cotangent": noise(key_list[1], (SEQS, LEN, D), 1.0, 6.0, ((0, 4), (1, 8))),
        "subsets": place_ends(ranked(key_list[2], (SEQS,), NSUB, 2), jax.random.fold_in(key_list[2], 3), 0, NSUB - 1).astype(jnp.int32),
        "subset_weight": jnp.clip(jnp.exp(jax.random.uniform(key_list[3], (NSUB,), jnp.float32, math.log(0.5), math.log(2.0))), 0.5, 2.0),
        "gain_attn": jnp.clip(1.0 + 0.18 * jax.random.normal(key_list[4], (D,), jnp.float32), 0.1, 1.9),
        "shift_attn": noise(key_list[5], (D,), 0.5, 3.0, (), jnp.float32),
        "gain_ffn": jnp.clip(1.0 + 0.18 * jax.random.normal(key_list[6], (D,), jnp.float32), 0.1, 1.9),
        "shift_ffn": noise(key_list[7], (D,), 0.5, 3.0, (), jnp.float32),
        "query_projection": noise(key_list[8], (D, D), D ** -0.5, 0.21875, ((0, 32),)),
        "pair_projection": noise(key_list[9], (D, 2 * HD), D ** -0.5, 0.21875, ((0, 32),)),
        "output_projection": noise(key_list[10], (D, D), ((LEN // 8) ** 0.5 * D ** -0.5), 6.0, ((0, 32),)),
        "up_projection": noise(key_list[11], (D, FF), D ** -0.5, 0.21875, ((0, 32),)),
        "down_projection": noise(key_list[12], (FF, D), FF ** -0.5, 0.109375, ((0, 32),)),
    }


FULL_PRECISION = lax.Precision.HIGHEST
masked_value = -1e+30

@jax.custom_vjp
def low(v):
    return lax.optimization_barrier(v.astype(jnp.bfloat16)).astype(jnp.float32)

@jax.custom_vjp
def low_back(v):
    return v

def low_keep(v):
    return (low(v), None)

def low_pass(kept, grad):
    return (grad,)

def back_keep(v):
    return (v, None)

def back_low(kept, grad):
    return (low(grad),)
low.defvjp(low_keep, low_pass)
low_back.defvjp(back_keep, back_low)

def layer_norm(values, gain, shift):
    center = values - lax.optimization_barrier(jnp.mean(values, axis=-1, keepdims=True))
    spread = lax.optimization_barrier(jnp.mean(center * center, axis=-1, keepdims=True))
    return center * lax.rsqrt(spread + 1e-05) * gain + shift

def rotary_tables(length):
    half_rot = ROT // 2
    frequency = 10000.0 ** (-2.0 * jnp.arange(half_rot, dtype=jnp.float32) / ROT)
    angles = jnp.arange(length, dtype=jnp.float32)[:, None] * frequency[None, :]
    cosine = jnp.concatenate([jnp.cos(angles), jnp.cos(angles)], axis=-1)
    sine_vals = jnp.concatenate([jnp.sin(angles), jnp.sin(angles)], axis=-1)
    return (cosine, sine_vals)

def rotate(vector, cosine, sine_vals):
    half_rot = ROT // 2
    rotary_part = vector[..., :ROT]
    turned = jnp.concatenate([-rotary_part[..., half_rot:], rotary_part[..., :half_rot]], axis=-1)
    return jnp.concatenate([rotary_part * cosine + turned * sine_vals, vector[..., ROT:]], axis=-1)

def attend_block(query_block, anchor, key_values):
    key_part = key_values[:, :HD]
    values = key_values[:, HD:]
    scores = jnp.einsum('qhd,kd->hqk', query_block, key_part, precision=FULL_PRECISION) * HD ** (-0.5)
    scores = low_back(scores)
    query_rows = anchor + jnp.arange(query_block.shape[0], dtype=jnp.int32)
    key_rows = jnp.arange(key_part.shape[0], dtype=jnp.int32)
    allowed = key_rows[None, :] <= query_rows[:, None]
    scores = jnp.where(allowed[None], scores, masked_value)
    logsum = jax.nn.logsumexp(scores, axis=-1, keepdims=True)
    weights = low(jnp.exp(scores - logsum))
    return jnp.einsum('hqk,kd->qhd', weights, values, precision=FULL_PRECISION)

def attend_sequence(seq_pair):
    queries, key_values = seq_pair
    length = queries.shape[0]
    query_block = min(length, 512)
    block_count = length // query_block
    blocks = queries.reshape(block_count, query_block, queries.shape[1], queries.shape[2])
    starts = jnp.arange(block_count, dtype=jnp.int32) * query_block
    checked = jax.checkpoint(attend_block)
    results = lax.map(lambda element: checked(element[0], element[1], key_values), (blocks, starts))
    return results.reshape(length, queries.shape[1] * queries.shape[2])

def forward(states, gain_attn, shift_attn, gain_ffn, shift_ffn, query_projection, pair_projection, output_projection, up_projection, down_projection):
    seq_count, length, model_width = states.shape
    cosine, sine_vals = rotary_tables(length)
    attention_input = low(layer_norm(states, gain_attn, shift_attn))
    feedforward_input = low(layer_norm(states, gain_ffn, shift_ffn))
    query_preactivation = low_back(jnp.einsum('gvq,qh->gvh', attention_input, query_projection, precision=FULL_PRECISION))
    pair_preactivation = low_back(jnp.einsum('gvq,qh->gvh', attention_input, pair_projection, precision=FULL_PRECISION))
    queries = low(rotate(query_preactivation.reshape(seq_count, length, H, HD), cosine[:, None, :], sine_vals[:, None, :]))
    key_part = rotate(pair_preactivation[..., :HD], cosine, sine_vals)
    key_values = low(jnp.concatenate([key_part, pair_preactivation[..., HD:]], axis=-1))
    attention_output = lax.map(attend_sequence, (queries, key_values))
    attention_output = low(low_back(attention_output))
    up_preactivation = low_back(jnp.einsum('jez,zn->jen', feedforward_input, up_projection, precision=FULL_PRECISION))
    gelu_output = low(jax.nn.gelu(up_preactivation, approximate=False))
    residual_branch = jnp.einsum('iex,xg->ieg', attention_output, output_projection, precision=FULL_PRECISION)
    residual_branch = residual_branch + jnp.einsum('otg,gy->oty', gelu_output, down_projection, precision=FULL_PRECISION)
    return states + low_back(residual_branch)

def reference(states, cotangent, subsets, subset_weight, gain_attn, shift_attn, gain_ffn, shift_ffn, query_projection, pair_projection, output_projection, up_projection, down_projection):
    layer_out, pullback = jax.vjp(forward, states.astype(jnp.float32), gain_attn, shift_attn, gain_ffn, shift_ffn, query_projection.astype(jnp.float32), pair_projection.astype(jnp.float32), output_projection.astype(jnp.float32), up_projection.astype(jnp.float32), down_projection.astype(jnp.float32))
    row_scale = subset_weight[subsets]
    gradients = pullback(cotangent.astype(jnp.float32) * row_scale[:, None, None])
    return (layer_out.astype(jnp.bfloat16), gradients[0].astype(jnp.bfloat16), gradients[1], gradients[2], gradients[3], gradients[4], gradients[5], gradients[6], gradients[7], gradients[8], gradients[9])
```

```python
import functools
import jax
import jax.numpy as jnp
from jax import lax
from jax.experimental import pallas as pl
from jax.experimental.pallas import tpu as pltpu

H = 12
HD = 64
LN2 = 0.6931471805599453


def dot(a, b, ca, cb):
    return lax.dot_general(a, b, (((ca,), (cb,)), ((), ())), preferred_element_type=jnp.float32)


def three_parts(x):
    hi = x.astype(jnp.bfloat16)
    rest = x - hi.astype(jnp.float32)
    mid = rest.astype(jnp.bfloat16)
    low = (rest - mid.astype(jnp.float32)).astype(jnp.bfloat16)
    return hi, mid, low


def attn_kernel(
    M, tk, G,
    seq_ref, row_ref, wide_ref,
    q_ref, g_ref, ka_ref, va_ref,
    o_ref, dq_ref, dkv_ref,
    qs, gs, qt, gt, stash, oacc, dqacc, top,
):
    t = pl.program_id(0)
    seq = seq_ref[t]
    row0 = row_ref[t]
    rows_all = H * M
    f32, bf16 = jnp.float32, jnp.bfloat16

    @pl.when(t == 0)
    def _():
        qs[...] = jnp.zeros_like(qs)
        dkv_ref[...] = jnp.zeros_like(dkv_ref)

    for h in range(H):
        qs[h * M:(h + 1) * M, :HD] = q_ref[:, h * HD:(h + 1) * HD]
    oacc[...] = jnp.zeros_like(oacc)
    dqacc[...] = jnp.zeros_like(dqacc)
    n_full = row0 // tk

    def keys(ref, kt):
        return ref[seq, pl.ds(pl.multiple_of(kt * tk, tk), tk), :]

    def allowed(kt):
        row = row0 + (lax.broadcasted_iota(jnp.int32, (G, tk), 0) & (M - 1))
        col = kt * tk + lax.broadcasted_iota(jnp.int32, (G, tk), 1)
        return col <= row

    def scores(kt, g, masked):
        s = dot(qs[g * G:(g + 1) * G, :], keys(ka_ref, kt), 1, 1)
        if masked:
            s = jnp.where(allowed(kt), s, -1e30)
        return s

    @pl.when(wide_ref[0] != 0)
    def _():
        for h in range(H):
            qs[h * M:(h + 1) * M, HD:] = jnp.zeros((M, 128 - HD), bf16)
        top[...] = jnp.full_like(top, -1e30)

        def peak(kt, masked):
            for g in range(rows_all // G):
                s = scores(kt, g, masked)
                part = s[:, :128]
                for j in range(1, tk // 128):
                    part = jnp.maximum(part, s[:, j * 128:(j + 1) * 128])
                r = slice(g * G, (g + 1) * G)
                top[r, :] = jnp.maximum(top[r, :], part)

        lax.fori_loop(0, n_full, lambda kt, _: (peak(kt, False), 0)[1], 0)
        peak(n_full, True)
        for h in range(H):
            r = slice(h * M, (h + 1) * M)
            best = -jnp.max(top[r, :], axis=1, keepdims=True)
            for j, part in enumerate(three_parts(best)):
                qs[r, HD + j:HD + j + 1] = part

    def first(kt, masked):
        v = keys(va_ref, kt)
        for g in range(rows_all // G):
            r = slice(g * G, (g + 1) * G)
            e = jnp.exp2(scores(kt, g, masked)).astype(bf16)
            stash[kt, r, :] = e
            oacc[r, :] += dot(e, v, 1, 0)

    lax.fori_loop(0, n_full, lambda kt, _: (first(kt, False), 0)[1], 0)
    first(n_full, True)

    for p in range(H // 2):
        outs = []
        for h in (2 * p, 2 * p + 1):
            r = slice(h * M, (h + 1) * M)
            acc = oacc[r, :]
            inverse = 1.0 / acc[:, HD:HD + 1]
            out = acc[:, :HD] * inverse
            outs.append(out)
            low = (g_ref[:, h * HD:(h + 1) * HD].astype(f32) * inverse).astype(bf16)
            delta = -jnp.sum(low.astype(f32) * out, axis=1, keepdims=True)
            parts = three_parts(delta)
            gs[r, :] = jnp.concatenate(
                [low, *parts, jnp.zeros((M, 128 - HD - 3), bf16)], axis=1)
        o_ref[:, p * 128:(p + 1) * 128] = jnp.concatenate(outs, axis=1).astype(bf16)
    qt[...] = qs[...].T
    gt[...] = gs[...].T

    def second(kt):
        k = keys(ka_ref, kt)
        v = keys(va_ref, kt)
        dk = jnp.zeros((HD, tk), f32)
        dv = jnp.zeros((HD, tk), f32)
        for g in range(rows_all // G):
            r = slice(g * G, (g + 1) * G)
            e = stash[kt, r, :]
            slope = (e.astype(f32) * dot(gs[r, :], v, 1, 1)).astype(bf16)
            dqacc[r, :] += dot(slope, k, 1, 0)
            dk = dk + dot(qt[:HD, r], slope, 1, 0)
            dv = dv + dot(gt[:HD, r], e, 1, 0)
        c = pl.ds(pl.multiple_of(kt * tk, tk), tk)
        dkv_ref[seq, :HD, c] += dk
        dkv_ref[seq, HD:, c] += dv

    lax.fori_loop(0, n_full + 1, lambda kt, _: (second(kt), 0)[1], 0)
    for p in range(H // 2):
        both = [dqacc[h * M:(h + 1) * M, :HD] for h in (2 * p, 2 * p + 1)]
        dq_ref[:, p * 128:(p + 1) * 128] = jnp.concatenate(both, axis=1)


def attention(seqs, rows, wide, q, g, ka, va, M, tk=512):
    G = 4 * M
    slots = q.shape[0] // M
    S, L, _ = ka.shape
    width = H * HD
    grid_spec = pltpu.PrefetchScalarGridSpec(
        num_scalar_prefetch=3,
        grid=(slots,),
        in_specs=[
            pl.BlockSpec((M, width), lambda t, *_: (t, 0)),
            pl.BlockSpec((M, width), lambda t, *_: (t, 0)),
            pl.BlockSpec((S, L, 128), lambda t, *_: (0, 0, 0), pipeline_mode=pl.Buffered(1)),
            pl.BlockSpec((S, L, 128), lambda t, *_: (0, 0, 0), pipeline_mode=pl.Buffered(1)),
        ],
        out_specs=[
            pl.BlockSpec((M, width), lambda t, *_: (t, 0)),
            pl.BlockSpec((M, width), lambda t, *_: (t, 0)),
            pl.BlockSpec((S, 128, L), lambda t, *_: (0, 0, 0), pipeline_mode=pl.Buffered(1)),
        ],
        scratch_shapes=[
            pltpu.VMEM((H * M, 128), jnp.bfloat16),
            pltpu.VMEM((H * M, 128), jnp.bfloat16),
            pltpu.VMEM((128, H * M), jnp.bfloat16),
            pltpu.VMEM((128, H * M), jnp.bfloat16),
            pltpu.VMEM((L // tk, H * M, tk), jnp.bfloat16),
            pltpu.VMEM((H * M, 128), jnp.float32),
            pltpu.VMEM((H * M, 128), jnp.float32),
            pltpu.VMEM((H * M, 128), jnp.float32),
        ],
    )
    pairs = slots * M * H * L // 2
    return pl.pallas_call(
        functools.partial(attn_kernel, M, tk, G),
        grid_spec=grid_spec,
        out_shape=[
            jax.ShapeDtypeStruct((slots * M, width), jnp.bfloat16),
            jax.ShapeDtypeStruct((slots * M, width), jnp.float32),
            jax.ShapeDtypeStruct((S, 128, L), jnp.float32),
        ],
        compiler_params=pltpu.CompilerParams(vmem_limit_bytes=56 << 20),
        cost_estimate=pl.CostEstimate(flops=12 * pairs * 64, bytes_accessed=16 << 20, transcendentals=pairs),
        name="attention",
    )(seqs, rows, wide, q, g, ka, va)


def gelu_both(x):
    z = jnp.abs(x) * 0.7071067811865476
    s = 1.0 / (1.0 + 0.3275911 * z)
    poly = s * (0.127414796 + s * (-0.142248368 + s * (0.710706871 + s * (-0.7265760135 + s * 0.5307027145))))
    bell = jnp.exp(-z * z)
    tail = poly * bell
    phi = jnp.where(x >= 0.0, 1.0 - tail, tail)
    return x * phi, phi + x * (bell * 0.3989422804014327)


def ffn_kernel(C, x_ref, b_ref, up_ref, down_ref, out_ref, dx_ref, gup_ref, gdown_ref, act_s, ug_s):
    f = pl.program_id(0)
    T = x_ref.shape[0]

    @pl.when(f == 0)
    def _():
        out_ref[...] = jnp.zeros_like(out_ref)
        dx_ref[...] = jnp.zeros_like(dx_ref)

    up = up_ref[...]
    down = down_ref[...]
    for c in range(T // C):
        r = slice(c * C, (c + 1) * C)
        u = dot(x_ref[r, :], up, 1, 0)
        a = dot(b_ref[r, :], down, 1, 1)
        act, slope = gelu_both(u)
        act = act.astype(jnp.bfloat16)
        ug = (a * slope).astype(jnp.bfloat16)
        act_s[r, :] = act
        ug_s[r, :] = ug
        out_ref[r, :] += dot(act, down, 1, 0)
        dx_ref[r, :] += dot(ug, up, 1, 1)
    gup_ref[...] = dot(x_ref[...], ug_s[...], 0, 0).astype(gup_ref.dtype)
    gdown_ref[...] = dot(act_s[...], b_ref[...], 0, 0).astype(gdown_ref.dtype)


def ffn(x, b, up, down, F=512, C=256, wire=jnp.bfloat16):
    T, D = x.shape
    FF = up.shape[1]
    C = min(C, T)
    f32, bf16 = jnp.float32, jnp.bfloat16
    whole = lambda f: (0, 0)
    return pl.pallas_call(
        functools.partial(ffn_kernel, C),
        grid=(FF // F,),
        in_specs=[
            pl.BlockSpec((T, D), whole, pipeline_mode=pl.Buffered(1)),
            pl.BlockSpec((T, D), whole, pipeline_mode=pl.Buffered(1)),
            pl.BlockSpec((D, F), lambda f: (0, f)),
            pl.BlockSpec((F, D), lambda f: (f, 0)),
        ],
        out_specs=[
            pl.BlockSpec((T, D), whole, pipeline_mode=pl.Buffered(1)),
            pl.BlockSpec((T, D), whole, pipeline_mode=pl.Buffered(1)),
            pl.BlockSpec((D, F), lambda f: (0, f)),
            pl.BlockSpec((F, D), lambda f: (f, 0)),
        ],
        out_shape=[
            jax.ShapeDtypeStruct((T, D), f32),
            jax.ShapeDtypeStruct((T, D), f32),
            jax.ShapeDtypeStruct((D, FF), wire),
            jax.ShapeDtypeStruct((FF, D), wire),
        ],
        scratch_shapes=[pltpu.VMEM((T, F), bf16), pltpu.VMEM((T, F), bf16)],
        compiler_params=pltpu.CompilerParams(vmem_limit_bytes=56 << 20),
        cost_estimate=pl.CostEstimate(flops=12 * T * D * FF, bytes_accessed=32 << 20, transcendentals=T * FF),
        name="feedforward",
    )(x, b, up, down)


ROT = 16


def layer_norm(values):
    center = values - jnp.mean(values, axis=-1, keepdims=True)
    inverse = lax.rsqrt(jnp.mean(center * center, axis=-1, keepdims=True) + 1e-05)
    return center * inverse, inverse


def norm_back(incoming, normed, inverse, gain):
    scaled = incoming * gain
    return inverse * (
        scaled
        - jnp.mean(scaled, axis=-1, keepdims=True)
        - normed * jnp.mean(scaled * normed, axis=-1, keepdims=True)
    )


def rotary_tables(positions):
    half_rot = ROT // 2
    frequency = 10000.0 ** (-2.0 * jnp.arange(half_rot, dtype=jnp.float32) / ROT)
    angles = positions[:, None] * frequency[None, :]
    cosine = jnp.concatenate([jnp.cos(angles), jnp.cos(angles)], axis=-1)
    sine_vals = jnp.concatenate([jnp.sin(angles), jnp.sin(angles)], axis=-1)
    return (cosine, sine_vals)


def rotate(vector, cosine, sine_vals):
    half_rot = ROT // 2
    rotary_part = vector[..., :ROT]
    turned = jnp.concatenate([-rotary_part[..., half_rot:], rotary_part[..., :half_rot]], axis=-1)
    return jnp.concatenate([rotary_part * cosine + turned * sine_vals, vector[..., ROT:]], axis=-1)


def scatter_sum(part, dims=("seq", "rows")):
    for axis in dims:
        part = lax.psum_scatter(part, axis, scatter_dimension=0, tiled=True)
    return part


def local(
    states, cotangent, subsets, subset_weight, gain_attn, shift_attn, gain_ffn, shift_ffn,
    query_projection, pair_projection, output_projection, up_projection, down_projection,
):
    f32, bf16 = jnp.float32, jnp.bfloat16
    both = ("seq", "rows")
    here, length_here, D = states.shape
    T = here * length_here
    n_seq, n = lax.axis_size("seq"), lax.axis_size("seq") * lax.axis_size("rows")
    length = length_here * n_seq
    offset = lax.axis_index("seq") * length_here
    M = min(128, length_here)
    FF = up_projection.shape[1]
    scale = HD ** -0.5

    small = jnp.concatenate([query_projection, pair_projection, output_projection], axis=1)
    small = lax.all_gather(small, both, axis=0, tiled=True)
    big = jnp.stack([up_projection, down_projection.reshape(up_projection.shape)])
    big = lax.all_gather(big, both, axis=1, tiled=True)
    full_query, full_pair, full_output = small[:, :D], small[:, D:D + 2 * HD], small[:, D + 2 * HD:]
    full_up, full_down = big[0], big[1].reshape(FF, D)

    source = states.astype(f32).reshape(T, D)
    unit, inverse = layer_norm(source)
    attention_input = (unit * gain_attn + shift_attn).astype(bf16)
    feedforward_input = (unit * gain_ffn + shift_ffn).astype(bf16)
    table_rows = jnp.arange(subset_weight.shape[0], dtype=jnp.int32)
    row_scale = jnp.sum(
        jnp.where(table_rows[None, :] == subsets[:, None], subset_weight[None, :], 0.0), axis=1
    )
    upstream = (cotangent.astype(f32) * row_scale[:, None, None]).reshape(T, D)
    branch_grad = upstream.astype(bf16)

    rows_here = offset + jnp.arange(length_here, dtype=jnp.int32)
    cosine, sine_vals = rotary_tables(rows_here.astype(f32))
    query_pre = jnp.dot(attention_input, full_query, preferred_element_type=f32)
    pair_pre = jnp.dot(attention_input, full_pair, preferred_element_type=f32)
    pair_pre = pair_pre.reshape(here, length_here, 2 * HD)
    queries = rotate(
        query_pre.reshape(here, length_here, H, HD) * (scale / LN2),
        cosine[None, :, None, :], sine_vals[None, :, None, :],
    ).astype(bf16).reshape(T, D)
    key_values = jnp.concatenate(
        [rotate(pair_pre[..., :HD], cosine[None], sine_vals[None]), pair_pre[..., HD:]], axis=2
    ).astype(bf16)
    out_grad = lax.dot_general(
        branch_grad, full_output, (((1,), (1,)), ((), ())), preferred_element_type=f32
    ).astype(bf16)

    all_kv = lax.all_gather(key_values, "seq", axis=1, tiled=True)
    ones = jnp.ones((here, length, 3), bf16)
    zeros = jnp.zeros((here, length, HD - 3), bf16)
    ka = jnp.concatenate([all_kv[..., :HD], ones, zeros], axis=-1)
    va = jnp.concatenate([all_kv[..., HD:], ones, zeros], axis=-1)
    q_norm = jnp.max(jnp.sum(jnp.square(queries.astype(f32).reshape(T, H, HD)), axis=-1))
    k_norm = jnp.max(jnp.sum(jnp.square(all_kv[..., :HD].astype(f32)), axis=-1))
    wide = (q_norm * k_norm > 60.0 ** 2).astype(jnp.int32).reshape(1)

    tiles = length_here // M
    slot = jnp.arange(here * tiles, dtype=jnp.int32)
    attended, query_grad, pair_terms = attention(
        slot // tiles, offset + (slot % tiles) * M, wide, queries, out_grad, ka, va, M,
        tk=min(512, length))

    ffn_out, ffn_input_grad, grad_up, grad_down = ffn(
        feedforward_input, branch_grad, full_up, full_down)

    ffn_grads = jnp.concatenate(
        [grad_up.reshape(n, -1, D), grad_down.reshape(n, -1, D)], axis=1)
    ffn_grads = scatter_sum(ffn_grads)[0]
    half = ffn_grads.shape[0] // 2
    grad_up = ffn_grads[:half].reshape(-1, FF).astype(f32)
    grad_down = ffn_grads[half:].astype(f32)

    pair_terms = pair_terms.astype(bf16).reshape(here, 2 * HD, n_seq, length_here)
    pair_terms = jnp.moveaxis(pair_terms, 2, 0)
    arrived = lax.all_to_all(pair_terms, "seq", split_axis=0, concat_axis=0, tiled=True)
    pair_grad = jnp.swapaxes(arrived.astype(f32).sum(axis=0), 1, 2)

    residual = jnp.dot(attended, full_output, preferred_element_type=f32) + ffn_out
    layer_out = (source + residual).astype(bf16).reshape(here, length_here, D)
    grad_output = lax.dot_general(
        attended, branch_grad, (((0,), (0,)), ((), ())), preferred_element_type=f32)

    query_pre_grad = rotate(
        query_grad.reshape(here, length_here, H, HD) * scale,
        cosine[None, :, None, :], -sine_vals[None, :, None, :],
    ).reshape(T, D).astype(bf16)
    pair_pre_grad = jnp.concatenate(
        [rotate(pair_grad[..., :HD] * LN2, cosine[None], -sine_vals[None]), pair_grad[..., HD:]], axis=2
    ).reshape(T, 2 * HD).astype(bf16)
    pre_grad = jnp.concatenate([query_pre_grad, pair_pre_grad], axis=1)
    grad_qp = lax.dot_general(
        attention_input, pre_grad, (((0,), (0,)), ((), ())), preferred_element_type=f32)
    attn_input_grad = lax.dot_general(
        pre_grad, small[:, :D + 2 * HD], (((1,), (1,)), ((), ())), preferred_element_type=f32)

    sums = jnp.stack([
        jnp.sum(attn_input_grad * unit, axis=0), jnp.sum(attn_input_grad, axis=0),
        jnp.sum(ffn_input_grad * unit, axis=0), jnp.sum(ffn_input_grad, axis=0)], axis=1)
    sums = jnp.concatenate([sums, jnp.zeros((D, 124), f32)], axis=1)
    grad_states = upstream + norm_back(attn_input_grad, unit, inverse, gain_attn)
    grad_states = grad_states + norm_back(ffn_input_grad, unit, inverse, gain_ffn)
    grad_states = grad_states.astype(bf16).reshape(here, length_here, D)

    last = jnp.concatenate([grad_qp, grad_output, sums], axis=1).astype(bf16)
    last = lax.psum_scatter(last, both, scatter_dimension=0, tiled=True).astype(f32)
    at = D + 2 * HD
    vectors = last[:, at + D:]
    return (
        layer_out, grad_states,
        vectors[:, 0], vectors[:, 1], vectors[:, 2], vectors[:, 3],
        last[:, :D], last[:, D:at], last[:, at:at + D], grad_up, grad_down,
    )


def solution(mesh):
    from jax.sharding import PartitionSpec as P

    blocks, owned = P("rows", "seq", None), P(("seq", "rows"), None)
    vector = P(("seq", "rows"))
    return jax.shard_map(
        local,
        mesh=mesh,
        in_specs=(blocks, blocks, P("rows"), P(), P(), P(), P(), P()) + (owned,) * 5,
        out_specs=(blocks, blocks) + (vector,) * 4 + (owned,) * 5,
        check_vma=False,
    )
```

```python
import functools
import jax
import jax.numpy as jnp
import numpy as np
from jax import lax
from jax.experimental import pallas as pl
from jax.experimental.pallas import tpu as pltpu

H = 12
HD = 64
LN2 = 0.6931471805599453


def dot(a, b, ca, cb):
    return lax.dot_general(a, b, (((ca,), (cb,)), ((), ())), preferred_element_type=jnp.float32)


def three_parts(x):
    hi = x.astype(jnp.bfloat16)
    rest = x - hi.astype(jnp.float32)
    mid = rest.astype(jnp.bfloat16)
    low = (rest - mid.astype(jnp.float32)).astype(jnp.bfloat16)
    return hi, mid, low


ROT = 16


def turn_tables(length, M):
    frequency = 10000.0 ** (-2.0 * np.arange(ROT // 2) / ROT)
    lanes = np.zeros(HD)
    lanes[:ROT] = np.concatenate([frequency, frequency])
    lanes = np.concatenate([lanes, lanes])

    def table(places):
        angles = places[:, None] * lanes[None, :]
        return np.concatenate([np.cos(angles), np.sin(angles)], axis=1).astype(np.float32)

    return table(np.arange(M)), table(np.arange(0, length, M))


def turn_factors(near, far):
    cn, sn, cf, sf = near[:, :128], near[:, 128:], far[:, :128], far[:, 128:]
    sine = sf * cn + cf * sn
    lane = lax.broadcasted_iota(jnp.int32, sine.shape, 1) & (HD - 1)
    low = jnp.where(lane < ROT // 2, sine, 0.0)
    high = jnp.where((lane >= ROT // 2) & (lane < ROT), sine, 0.0)
    return cf * cn - sf * sn, low, high


def turn(z, cosine, low, high):
    return z * cosine - pltpu.roll(z, 120, 1) * low + pltpu.roll(z, 8, 1) * high


def turn_back(z, cosine, low, high):
    return z * cosine + pltpu.roll(z, 120, 1) * low - pltpu.roll(z, 8, 1) * high


def attn_kernel(
    M, tk, own, first_call,
    slot_ref, seq_ref, row_ref, on_ref,
    q_ref, g_ref, other_ref, near_ref, far_ref, kv_ref, *refs,
):
    if not first_call:
        refs = refs[2:]
        before_ref, refs = refs[0], refs[1:]
    o_ref, dq_ref, dkv_ref = refs[:3]
    ka, va, qs, gs, qt, gt, stash, oacc, dqacc, top, limit = refs[3:]
    t = pl.program_id(0)
    seq = seq_ref[t]
    row0 = row_ref[t]
    G = 4 * M
    groups = [slice(g * G, (g + 1) * G) for g in range(H // 4)]
    heads = [slice(h * M, (h + 1) * M) for h in range(H)]
    f32, bf16 = jnp.float32, jnp.bfloat16
    parts_, count, block, _ = kv_ref.shape

    @pl.when(t == 0)
    def _():
        if first_call:
            dkv_ref[...] = jnp.zeros_like(dkv_ref)
        else:
            dkv_ref[...] = before_ref[...]
        lane = lax.broadcasted_iota(jnp.int32, (block, HD), 1)
        ones = jnp.where(lane < 3, 1.0, 0.0).astype(bf16)

        def arrange(i, most):
            for s in range(count):
                kv = kv_ref[i, s]
                rows = pl.ds(pl.multiple_of(i * block, block), block)
                ka[s, rows, :] = jnp.concatenate([kv[:, :HD], ones], axis=1)
                va[s, rows, :] = jnp.concatenate([kv[:, HD:], ones], axis=1)
                k = kv[:, :HD].astype(f32)
                most = jnp.maximum(most, jnp.max(jnp.sum(k * k, axis=1, keepdims=True)))
            return most

        limit[0] = lax.fori_loop(0, parts_, arrange, jnp.float32(0.0))

    @pl.when(on_ref[t] != 0)
    def _():
        taken = slot_ref[t] >= own
        q_in = q_ref[...] if other_ref is None else jnp.where(taken, other_ref[0, 0], q_ref[...])
        g_in = g_ref[...] if other_ref is None else jnp.where(taken, other_ref[0, 1], g_ref[...])
        for h in range(H):
            qs[heads[h], :HD] = q_in[:, h * HD:(h + 1) * HD]
            qs[heads[h], HD:] = jnp.zeros((M, 128 - HD), bf16)
        oacc[...] = jnp.zeros_like(oacc)
        dqacc[...] = jnp.zeros_like(dqacc)
        n_full = row0 // tk

        def keys(ref, kt):
            return ref[seq, pl.ds(pl.multiple_of(kt * tk, tk), tk), :]

        def allowed(kt):
            row = row0 + (lax.broadcasted_iota(jnp.int32, (G, tk), 0) & (M - 1))
            col = kt * tk + lax.broadcasted_iota(jnp.int32, (G, tk), 1)
            return col <= row

        def scores(kt, r, masked):
            s = dot(qs[r, :], keys(ka, kt), 1, 1)
            if masked:
                s = jnp.where(allowed(kt), s, -1e30)
            return s

        most = jnp.float32(0.0)
        for r in groups:
            q = qs[r, :].astype(f32)
            most = jnp.maximum(most, jnp.max(jnp.sum(q * q, axis=1, keepdims=True)))

        @pl.when(most * limit[0] > 3600.0)
        def _():
            top[...] = jnp.full_like(top, -1e30)

            def peak(kt, masked):
                for r in groups:
                    s = scores(kt, r, masked)
                    part = s[:, :128]
                    for j in range(1, tk // 128):
                        part = jnp.maximum(part, s[:, j * 128:(j + 1) * 128])
                    top[r, :] = jnp.maximum(top[r, :], part)

            lax.fori_loop(0, n_full, lambda kt, _: (peak(kt, False), 0)[1], 0)
            peak(n_full, True)
            for r in heads:
                best = -jnp.max(top[r, :], axis=1, keepdims=True)
                for j, part in enumerate(three_parts(best)):
                    qs[r, HD + j:HD + j + 1] = part

        def first(kt, masked):
            v = keys(va, kt)
            for r in groups:
                e = jnp.exp2(scores(kt, r, masked)).astype(bf16)
                stash[kt, r, :] = e
                oacc[r, :] += dot(e, v, 1, 0)

        lax.fori_loop(0, n_full, lambda kt, _: (first(kt, False), 0)[1], 0)
        first(n_full, True)

        for p in range(H // 2):
            outs = []
            for h in (2 * p, 2 * p + 1):
                r = heads[h]
                acc = oacc[r, :]
                inverse = 1.0 / acc[:, HD:HD + 1]
                out = acc[:, :HD] * inverse
                outs.append(out)
                low = (g_in[:, h * HD:(h + 1) * HD].astype(f32) * inverse).astype(bf16)
                delta = -jnp.sum(low.astype(f32) * out, axis=1, keepdims=True)
                gs[r, :] = jnp.concatenate(
                    [low, *three_parts(delta), jnp.zeros((M, 128 - HD - 3), bf16)], axis=1)
            o_ref[:, p * 128:(p + 1) * 128] = jnp.concatenate(outs, axis=1).astype(bf16)
        qt[...] = qs[...].T
        gt[...] = gs[...].T

        def second(kt):
            k = keys(ka, kt)
            v = keys(va, kt)
            dk = jnp.zeros((HD, tk), f32)
            dv = jnp.zeros((HD, tk), f32)
            for r in groups:
                e = stash[kt, r, :]
                slope = (e.astype(f32) * dot(gs[r, :], v, 1, 1)).astype(bf16)
                dqacc[r, :] += dot(slope, k, 1, 0)
                dk = dk + dot(qt[:HD, r], slope, 1, 0)
                dv = dv + dot(gt[:HD, r], e, 1, 0)
            c = pl.ds(pl.multiple_of(kt * tk, tk), tk)
            dkv_ref[seq, :HD, c] += dk
            dkv_ref[seq, HD:, c] += dv

        lax.fori_loop(0, n_full + 1, lambda kt, _: (second(kt), 0)[1], 0)
        factors = turn_factors(near_ref[...], far_ref[pl.ds(row0 // M, 1), :])
        for p in range(H // 2):
            z = jnp.concatenate([dqacc[heads[h], :HD] for h in (2 * p, 2 * p + 1)], axis=1)
            dq_ref[:, p * 128:(p + 1) * 128] = (turn_back(z, *factors) * HD ** -0.5).astype(bf16)


def attention(tables, q, g, others, kv, M, tk, most, before=None):
    width = H * HD
    steps = tables[0].shape[0]
    own = q.shape[0] // M
    parts, S, block, _ = kv.shape
    L = parts * block
    near, far = turn_tables(L, M)
    whole = pl.Buffered(1)
    tile = pl.BlockSpec((M, width), lambda t, slot, *_: (slot[t], 0))
    near_spec = pl.BlockSpec(near.shape, lambda t, *_: (0, 0), pipeline_mode=whole)
    far_spec = pl.BlockSpec(far.shape, lambda t, *_: (0, 0), pipeline_mode=whole)
    mine = pl.BlockSpec((M, width), lambda t, slot, *_: (jnp.minimum(slot[t], own - 1), 0))
    taken = pl.BlockSpec((1, 2, M, width), lambda t, slot, *_: (jnp.maximum(slot[t] - own, 0), 0, 0, 0))
    sums = pl.BlockSpec((S, 128, L), lambda t, *_: (0, 0, 0), pipeline_mode=whole)
    anywhere = pl.BlockSpec(memory_space=pl.ANY)
    bf16, f32 = jnp.bfloat16, jnp.float32
    pairs = steps * M * H * L // 3
    kernel = functools.partial(attn_kernel, M, tk, own, before is None)
    operands, specs = [q, g], [mine, mine]
    if others is None:
        inner = kernel
        kernel = lambda a, b, c, d, q_ref, g_ref, *refs: inner(a, b, c, d, q_ref, g_ref, None, *refs)
    else:
        operands, specs = operands + [others], specs + [taken]
    operands += [near, far, kv]
    specs += [near_spec, far_spec, pl.BlockSpec(kv.shape, lambda t, *_: (0, 0, 0, 0), pipeline_mode=whole)]
    aliases = {}
    if before is not None:
        aliases = {4 + len(operands) + i: i for i in range(3)}
        operands, specs = operands + list(before), specs + [anywhere, anywhere, sums]
    slots = jax.ShapeDtypeStruct(((own + most) * M, width), bf16)
    return pl.pallas_call(
        kernel,
        grid_spec=pltpu.PrefetchScalarGridSpec(
            num_scalar_prefetch=4,
            grid=(steps,),
            in_specs=specs,
            out_specs=[tile, tile, sums],
            scratch_shapes=[
                pltpu.VMEM((S, L, 128), bf16),
                pltpu.VMEM((S, L, 128), bf16),
                pltpu.VMEM((H * M, 128), bf16),
                pltpu.VMEM((H * M, 128), bf16),
                pltpu.VMEM((128, H * M), bf16),
                pltpu.VMEM((128, H * M), bf16),
                pltpu.VMEM((L // tk, H * M, tk), bf16),
                pltpu.VMEM((H * M, 128), f32),
                pltpu.VMEM((H * M, 128), f32),
                pltpu.VMEM((H * M, 128), f32),
                pltpu.SMEM((1,), f32),
            ],
        ),
        out_shape=[slots, slots, jax.ShapeDtypeStruct((S, 128, L), f32)],
        input_output_aliases=aliases,
        compiler_params=pltpu.CompilerParams(vmem_limit_bytes=58 << 20),
        cost_estimate=pl.CostEstimate(flops=1 << 20, bytes_accessed=1 << 16, transcendentals=0),
        name="attention",
    )(*tables, *operands)


def gelu_both(x):
    z = jnp.abs(x) * 0.7071067811865476
    s = 1.0 / (1.0 + 0.3275911 * z)
    poly = s * (0.127414796 + s * (-0.142248368 + s * (0.710706871 + s * (-0.7265760135 + s * 0.5307027145))))
    bell = jnp.exp(-z * z)
    tail = poly * bell
    phi = jnp.where(x >= 0.0, 1.0 - tail, tail)
    return x * phi, phi + x * (bell * 0.3989422804014327)


def ffn_kernel(C, x_ref, b_ref, up_ref, down_ref, out_ref, dx_ref, gup_ref, gdown_ref, act_s, ug_s):
    f = pl.program_id(0)
    T = x_ref.shape[0]

    @pl.when(f == 0)
    def _():
        out_ref[...] = jnp.zeros_like(out_ref)
        dx_ref[...] = jnp.zeros_like(dx_ref)

    up = up_ref[...]
    down = down_ref[...]
    for c in range(T // C):
        r = slice(c * C, (c + 1) * C)
        u = dot(x_ref[r, :], up, 1, 0)
        a = dot(b_ref[r, :], down, 1, 1)
        act, slope = gelu_both(u)
        act = act.astype(jnp.bfloat16)
        ug = (a * slope).astype(jnp.bfloat16)
        act_s[r, :] = act
        ug_s[r, :] = ug
        out_ref[r, :] += dot(act, down, 1, 0)
        dx_ref[r, :] += dot(ug, up, 1, 1)
    gup_ref[...] = dot(x_ref[...], ug_s[...], 0, 0).astype(gup_ref.dtype)
    gdown_ref[...] = dot(act_s[...], b_ref[...], 0, 0).astype(gdown_ref.dtype)


def ffn(x, b, up, down, F=512, C=256, wire=jnp.bfloat16):
    T, D = x.shape
    FF = up.shape[1]
    C = min(C, T)
    f32, bf16 = jnp.float32, jnp.bfloat16
    whole = lambda f: (0, 0)
    return pl.pallas_call(
        functools.partial(ffn_kernel, C),
        grid=(FF // F,),
        in_specs=[
            pl.BlockSpec((T, D), whole, pipeline_mode=pl.Buffered(1)),
            pl.BlockSpec((T, D), whole, pipeline_mode=pl.Buffered(1)),
            pl.BlockSpec((D, F), lambda f: (0, f)),
            pl.BlockSpec((F, D), lambda f: (f, 0)),
        ],
        out_specs=[
            pl.BlockSpec((T, D), whole, pipeline_mode=pl.Buffered(1)),
            pl.BlockSpec((T, D), whole, pipeline_mode=pl.Buffered(1)),
            pl.BlockSpec((D, F), lambda f: (0, f)),
            pl.BlockSpec((F, D), lambda f: (f, 0)),
        ],
        out_shape=[
            jax.ShapeDtypeStruct((T, D), f32),
            jax.ShapeDtypeStruct((T, D), f32),
            jax.ShapeDtypeStruct((D, FF), wire),
            jax.ShapeDtypeStruct((FF, D), wire),
        ],
        scratch_shapes=[pltpu.VMEM((T, F), bf16), pltpu.VMEM((T, F), bf16)],
        compiler_params=pltpu.CompilerParams(vmem_limit_bytes=56 << 20),
        cost_estimate=pl.CostEstimate(flops=12 * T * D * FF, bytes_accessed=32 << 20, transcendentals=T * FF),
        name="feedforward",
    )(x, b, up, down)


def ffn_packed_kernel(C, n_rows, x_ref, b_ref, up_ref, down_ref, out_ref, dx_ref, grads_ref, act_s, ug_s, wide, ups):
    f = pl.program_id(0)
    T, D = x_ref.shape
    groups, each, _, count, _ = up_ref.shape
    tiles = ups.shape[0]
    n = groups * each
    owned = D // n
    f32, bf16 = jnp.float32, jnp.bfloat16

    @pl.when(f == 0)
    def _():
        out_ref[...] = jnp.zeros_like(out_ref)
        dx_ref[...] = jnp.zeros_like(dx_ref)

        def unpack(d, _):
            part = up_ref[d // each, lax.rem(d, each), 0].astype(f32)
            for j in range(tiles):
                at = pl.ds(pl.multiple_of(d * owned, 8), owned)
                wide[j, at, :] = part[j * owned:(j + 1) * owned]
            return 0

        lax.fori_loop(0, n, unpack, 0)
        for j in range(tiles):
            ups[j] = wide[j].astype(bf16)

    up = ups[f]
    down = down_ref[...].reshape(D, D)
    for c in range(T // C):
        r = slice(c * C, (c + 1) * C)
        u = dot(x_ref[r, :], up, 1, 0)
        a = dot(b_ref[r, :], down, 1, 1)
        act, slope = gelu_both(u)
        act = act.astype(bf16)
        ug = (a * slope).astype(bf16)
        act_s[r, :] = act
        ug_s[r, :] = ug
        out_ref[r, :] += dot(act, down, 1, 0)
        dx_ref[r, :] += dot(ug, up, 1, 1)
    wide[f] = dot(x_ref[...], ug_s[...], 0, 0)
    grad_down = dot(act_s[...], b_ref[...], 0, 0).astype(bf16)
    for k in range(each):
        at = f * each + k
        grads_ref[lax.rem(at, n_rows), at // n_rows, count:] = grad_down[k * count:(k + 1) * count]

    @pl.when(f == tiles - 1)
    def _():
        def pack(d, _):
            at = pl.ds(pl.multiple_of(d * owned, 8), owned)
            part = jnp.concatenate([wide[j, at, :] for j in range(tiles)], axis=0)
            grads_ref[lax.rem(d, n_rows), d // n_rows, :count] = part.astype(bf16)
            return 0

        lax.fori_loop(0, n, pack, 0)


def ffn_packed(x, b, packed, n_seq, n_rows, C=256):
    T, D = x.shape
    n, count = packed.shape[0], packed.shape[1] // 2
    FF = n * count
    tiles = FF // D
    each = n // tiles
    packed = packed.reshape(tiles, each, 2, count, D)
    f32, bf16 = jnp.float32, jnp.bfloat16
    once = pl.Buffered(1)
    whole = lambda f: (0, 0)
    return pl.pallas_call(
        functools.partial(ffn_packed_kernel, C, n_rows),
        grid=(tiles,),
        in_specs=[
            pl.BlockSpec((T, D), whole, pipeline_mode=once),
            pl.BlockSpec((T, D), whole, pipeline_mode=once),
            pl.BlockSpec((tiles, each, 1, count, D), lambda f: (0, 0, 0, 0, 0), pipeline_mode=once),
            pl.BlockSpec((1, each, 1, count, D), lambda f: (f, 0, 1, 0, 0)),
        ],
        out_specs=[
            pl.BlockSpec((T, D), whole, pipeline_mode=once),
            pl.BlockSpec((T, D), whole, pipeline_mode=once),
            pl.BlockSpec((n_rows, n_seq, 2 * count, D), lambda f: (0, 0, 0, 0), pipeline_mode=once),
        ],
        out_shape=[
            jax.ShapeDtypeStruct((T, D), f32),
            jax.ShapeDtypeStruct((T, D), f32),
            jax.ShapeDtypeStruct((n_rows, n_seq, 2 * count, D), bf16),
        ],
        scratch_shapes=[
            pltpu.VMEM((T, D), bf16), pltpu.VMEM((T, D), bf16),
            pltpu.VMEM((tiles, D, D), f32), pltpu.VMEM((tiles, D, D), bf16),
        ],
        compiler_params=pltpu.CompilerParams(vmem_limit_bytes=60 << 20),
        cost_estimate=pl.CostEstimate(flops=1 << 20, bytes_accessed=1 << 16, transcendentals=0),
        name="feedforward",
    )(x, b, packed, packed)


MESH = pl.DeviceIdType.MESH


def bits_of(n_seq, n_rows):
    high = [("seq", 1 << b) for b in reversed(range(n_seq.bit_length() - 1))]
    return high + [("rows", 1 << b) for b in reversed(range(n_rows.bit_length() - 1))]


def place(bits):
    return [lax.rem(lax.axis_index(axis) // weight, 2) for axis, weight in bits]


def partner(bit):
    axis, weight = bit
    mine = lax.axis_index(axis)
    return {axis: mine + weight - 2 * weight * lax.rem(mine // weight, 2)}


def greet(bits):
    barrier = pltpu.get_barrier_semaphore()
    for bit in bits:
        pl.semaphore_signal(barrier, inc=1, device_id=partner(bit), device_id_type=MESH)
    pl.semaphore_wait(barrier, len(bits))


def routes(bits):
    n = len(bits)
    one = list(range(n))
    other = list(range(n))
    near = max(i for i in range(n) if bits[i][0] == "seq")
    if near + 1 < n - 1:
        other[near], other[near + 1] = other[near + 1], other[near]
    return one, other


def gather_kernel(bits, count, *refs):
    shards, fulls = refs[:count], refs[count:2 * count]
    own_sem, send_sem, recv_sem = refs[2 * count:]
    me = place(bits)
    orders = routes(bits)
    locals_ = []
    for a in range(count):
        copy = pltpu.make_async_copy(shards[a], fulls[a].at[tuple(me)], own_sem.at[a])
        copy.start()
        locals_.append(copy)
    greet(bits)
    for copy in locals_:
        copy.wait()
    held = [set(), set()]
    for stage in range(len(bits)):
        copies = []
        for half in (0, 1):
            b = orders[half][stage]
            for a in range(count):
                rows = shards[a].shape[0] // 2
                where = tuple(slice(None) if i in held[half] else me[i] for i in range(len(bits)))
                piece = fulls[a].at[where + (pl.ds(half * rows, rows),)]
                copy = pltpu.make_async_remote_copy(
                    src_ref=piece, dst_ref=piece,
                    send_sem=send_sem.at[a, half, stage], recv_sem=recv_sem.at[a, half, stage],
                    device_id=partner(bits[b]), device_id_type=MESH)
                copy.start()
                copies.append(copy)
            held[half].add(b)
        for copy in copies:
            copy.wait()


def gather(shards, n_seq, n_rows, collective_id):
    bits = bits_of(n_seq, n_rows)
    count = len(shards)
    outs = pl.pallas_call(
        functools.partial(gather_kernel, bits, count),
        out_shape=[jax.ShapeDtypeStruct((2,) * len(bits) + s.shape, s.dtype) for s in shards],
        in_specs=[pl.BlockSpec(memory_space=pl.ANY)] * count,
        out_specs=[pl.BlockSpec(memory_space=pl.ANY)] * count,
        scratch_shapes=[
            pltpu.SemaphoreType.DMA((count,)),
            pltpu.SemaphoreType.DMA((count, 2, len(bits))),
            pltpu.SemaphoreType.DMA((count, 2, len(bits))),
        ],
        compiler_params=pltpu.CompilerParams(collective_id=collective_id, has_side_effects=True),
        name="gather",
    )(*shards)
    return [o.reshape((n_seq * n_rows,) + s.shape) for o, s in zip(outs, shards)]


def scatter_kernel(bits, width, x_ref, out_ref, *refs):
    n = len(bits)
    send = refs[:n]
    recv = refs[n:2 * n]
    acc = refs[2 * n:3 * n]
    send_sem, recv_sem = refs[3 * n:]
    rows = x_ref.shape[1]
    f32, bf16 = jnp.float32, jnp.bfloat16
    me = place(bits)
    orders = [list(reversed(o)) for o in routes(bits)]
    greet(bits)

    def spread(half, stage, j, own):
        left = sorted(orders[half][stage:])
        b = orders[half][stage]
        rest = [i for i in left if i != b]
        index = 0
        for i in left:
            if i == b:
                bit = me[b] if own else 1 - me[b]
            else:
                bit = lax.rem(j // (1 << (len(rest) - 1 - rest.index(i))), 2)
            index = index * 2 + bit
        return index

    def block(half, stage, at):
        if stage == 0:
            low = x_ref[at, :, half * 2 * width:half * 2 * width + width]
            high = x_ref[at, :, half * 2 * width + width:(half + 1) * 2 * width]
            return jnp.concatenate([low, high], axis=0)
        return acc[stage - 1][half, at]

    for stage in range(n):
        size = 1 << (n - 1 - stage)
        copies = []
        for half in (0, 1):
            def fill(j, _, half=half, stage=stage):
                send[stage][half, j] = block(half, stage, spread(half, stage, j, False)).astype(bf16)
                return 0
            lax.fori_loop(0, size, fill, 0)
            copy = pltpu.make_async_remote_copy(
                src_ref=send[stage].at[half], dst_ref=recv[stage].at[half],
                send_sem=send_sem.at[half, stage], recv_sem=recv_sem.at[half, stage],
                device_id=partner(bits[orders[half][stage]]), device_id_type=MESH)
            copy.start()
            copies.append(copy)
        for half in (0, 1):
            copies[half].wait()

            def add(j, _, half=half, stage=stage):
                own = block(half, stage, spread(half, stage, j, True))
                acc[stage][half, j] = own + recv[stage][half, j].astype(f32)
                return 0
            lax.fori_loop(0, size, add, 0)
    for half in (0, 1):
        total = acc[n - 1][half, 0]
        out_ref[:, half * 2 * width:half * 2 * width + width] = total[:rows]
        out_ref[:, half * 2 * width + width:(half + 1) * 2 * width] = total[rows:]


def scatter(x, n_seq, n_rows, collective_id):
    bits = bits_of(n_seq, n_rows)
    n, rows, columns = x.shape
    width = columns // 4
    shapes = [(2, 1 << (len(bits) - 1 - s), 2 * rows, width) for s in range(len(bits))]
    return pl.pallas_call(
        functools.partial(scatter_kernel, bits, width),
        out_shape=jax.ShapeDtypeStruct((rows, columns), jnp.float32),
        in_specs=[pl.BlockSpec(memory_space=pltpu.VMEM)],
        out_specs=pl.BlockSpec(memory_space=pltpu.VMEM),
        scratch_shapes=[pltpu.VMEM(s, jnp.bfloat16) for s in shapes]
        + [pltpu.VMEM(s, jnp.bfloat16) for s in shapes]
        + [pltpu.VMEM(s, jnp.float32) for s in shapes]
        + [pltpu.SemaphoreType.DMA((2, len(bits))), pltpu.SemaphoreType.DMA((2, len(bits)))],
        compiler_params=pltpu.CompilerParams(
            collective_id=collective_id, has_side_effects=True, vmem_limit_bytes=40 << 20),
        name="scatter",
    )(x)


def front_kernel(
    bits, here, M, chunk,
    x_ref, c_ref, scale_ref, norm_ref, near_ref, far_ref, sq_ref, pr_ref,
    q_ref, g_ref, kv_ref, xa_ref, xf_ref, b_ref, wide_ref, wp,
    sq_all, pr_all, stage_q, stage_o, stage_p,
    own_sem, send_sem, recv_sem, kv_send, kv_recv,
):
    f32, bf16 = jnp.float32, jnp.bfloat16
    T, D = x_ref.shape
    n = len(bits)
    me = place(bits)
    seq_bits = [i for i in range(n) if bits[i][0] == "seq"]
    own = [pltpu.make_async_copy(s, d.at[tuple(me)], own_sem.at[i])
           for i, (s, d) in enumerate(((sq_ref, sq_all), (pr_ref, pr_all)))]
    for copy in own:
        copy.start()
    greet(bits)
    for copy in own:
        copy.wait()

    def normalize(i):
        r = slice(i * chunk, (i + 1) * chunk)
        x = x_ref[r, :].astype(f32)
        x = x - jnp.mean(x, axis=1, keepdims=True)
        unit = x * lax.rsqrt(jnp.mean(x * x, axis=1, keepdims=True) + 1e-05)
        xa_ref[r, :] = (unit * norm_ref[0:1, :] + norm_ref[1:2, :]).astype(bf16)
        xf_ref[r, :] = (unit * norm_ref[2:3, :] + norm_ref[3:4, :]).astype(bf16)
        part = i * chunk // (T // here)
        b_ref[r, :] = (c_ref[r, :].astype(f32) * scale_ref[part:part + 1, :]).astype(bf16)

    orders = routes(bits)
    held = [set(), set()]
    chunks = T // chunk
    for stage in range(n):
        copies = []
        for half in (0, 1):
            b = orders[half][stage]
            for a, full in enumerate((pr_all, sq_all)):
                rows = full.shape[-2]
                if half == 0:
                    part = pl.ds(0, rows // 32 * 16)
                else:
                    part = pl.ds(rows // 32 * 16, rows - rows // 32 * 16)
                where = tuple(slice(None) if i in held[half] else me[i] for i in range(n))
                piece = full.at[where + (part,)]
                copy = pltpu.make_async_remote_copy(
                    src_ref=piece, dst_ref=piece,
                    send_sem=send_sem.at[a, half, stage], recv_sem=recv_sem.at[a, half, stage],
                    device_id=partner(bits[b]), device_id_type=MESH)
                copy.start()
                copies.append(copy)
            held[half].add(b)
        for i in range(chunks):
            if i % n == stage:
                normalize(i)
        for copy in copies:
            copy.wait()

    owned = D // (1 << n)
    for d in range(1 << n):
        at = tuple((d >> (n - 1 - i)) & 1 for i in range(n))
        r = slice(d * owned, (d + 1) * owned)
        squares = sq_all[at].astype(f32)
        stage_q[r, :] = squares[:owned]
        stage_o[r, :] = squares[owned:2 * owned]
        stage_p[r, :] = pr_all[at].astype(f32)[:owned]
    wp[...] = stage_p[...].astype(bf16)

    block = lax.axis_index("seq")
    per = T // here // M
    tables = []
    for j in range(per):
        tables.append(turn_factors(near_ref[...], far_ref[pl.ds(block * per + j, 1), :]))

    first = lax.broadcasted_iota(jnp.int32, (M, 128), 1) < HD
    at = tuple(me[i] for i in seq_bits)
    for s in range(here):
        for j in range(per):
            r = slice((s * per + j) * M, (s * per + j + 1) * M)
            kv = dot(xa_ref[r, :], wp[...], 1, 0)
            turned = turn(kv, *tables[j])
            kv_ref[at + (s, pl.ds(j * M, M))] = jnp.where(first, turned, kv).astype(bf16)

    def kv_stage(k, held):
        copies = []
        for half in (0, 1):
            order = seq_bits if half == 0 else seq_bits[-1:] + seq_bits[:-1]
            b = order[k]
            rows = T // here // 2
            where = tuple(slice(None) if i in held[half] else me[i] for i in seq_bits)
            piece = kv_ref.at[where + (slice(None), pl.ds(half * rows, rows))]
            copy = pltpu.make_async_remote_copy(
                src_ref=piece, dst_ref=piece, send_sem=kv_send.at[half, k], recv_sem=kv_recv.at[half, k],
                device_id=partner(bits[b]), device_id_type=MESH)
            copy.start()
            copies.append(copy)
            held[half].add(b)
        return copies

    def queries(i):
        r = slice(i * chunk, (i + 1) * chunk)
        z = dot(xa_ref[r, :], wide_ref[0], 1, 0)
        for j in range(chunk // M):
            tab = tables[(i * chunk // M + j) % per]
            for p in range(D // 128):
                c = slice(p * 128, (p + 1) * 128)
                part = turn(z[j * M:(j + 1) * M, c], *tab) * (HD ** -0.5 / LN2)
                q_ref[i * chunk + j * M:i * chunk + (j + 1) * M, c] = part.astype(bf16)

    def gradients(i):
        r = slice(i * chunk, (i + 1) * chunk)
        g_ref[r, :] = dot(b_ref[r, :], wide_ref[1], 1, 1).astype(bf16)

    held = [set(), set()]
    jobs = [functools.partial(f, i) for f in (queries, gradients) for i in range(chunks)]
    for k in range(len(seq_bits)):
        copies = kv_stage(k, held)
        if k == 0:
            wide_ref[0] = stage_q[...].astype(bf16)
            wide_ref[1] = stage_o[...].astype(bf16)
        for i, job in enumerate(jobs):
            if i * len(seq_bits) // len(jobs) == k:
                job()
        for copy in copies:
            copy.wait()


def front(x, c, scale, norms, squares, pairs, here, length, M, n_seq, n_rows, collective_id, chunk=256):
    bits = bits_of(n_seq, n_rows)
    n = len(bits)
    n_s = n_seq.bit_length() - 1
    T, D = x.shape
    f32, bf16 = jnp.float32, jnp.bfloat16
    near, far = turn_tables(length, M)
    vmem = pl.BlockSpec(memory_space=pltpu.VMEM)
    token = jax.ShapeDtypeStruct((T, D), bf16)
    outs = pl.pallas_call(
        functools.partial(front_kernel, bits, here, M, chunk),
        out_shape=[token, token, jax.ShapeDtypeStruct((2,) * n_s + (here, T // here, 128), bf16), token, token, token,
                   jax.ShapeDtypeStruct((2, D, D), bf16), jax.ShapeDtypeStruct((D, 128), bf16)],
        in_specs=[vmem] * 8,
        out_specs=[vmem] * 8,
        scratch_shapes=[
            pltpu.VMEM((2,) * n + squares.shape, bf16),
            pltpu.VMEM((2,) * n + pairs.shape, bf16),
            pltpu.VMEM((D, D), f32),
            pltpu.VMEM((D, D), f32),
            pltpu.VMEM((D, 128), f32),
            pltpu.SemaphoreType.DMA((2,)),
            pltpu.SemaphoreType.DMA((2, 2, n)),
            pltpu.SemaphoreType.DMA((2, 2, n)),
            pltpu.SemaphoreType.DMA((2, n_s)),
            pltpu.SemaphoreType.DMA((2, n_s)),
        ],
        compiler_params=pltpu.CompilerParams(
            collective_id=collective_id, has_side_effects=True, vmem_limit_bytes=56 << 20),
        name="front",
    )(x, c, scale, norms, near, far, squares, pairs)
    q, g, kv, xa, xf, b, wide, pair = outs
    return q, g, kv.reshape(n_seq, here, T // here, 128), xa, xf, b, wide, pair


def layer_norm(values):
    center = values - jnp.mean(values, axis=-1, keepdims=True)
    inverse = lax.rsqrt(jnp.mean(center * center, axis=-1, keepdims=True) + 1e-05)
    return center * inverse, inverse


def norm_back(incoming, normed, inverse, gain):
    scaled = incoming * gain
    return inverse * (
        scaled
        - jnp.mean(scaled, axis=-1, keepdims=True)
        - normed * jnp.mean(scaled * normed, axis=-1, keepdims=True)
    )


def rotary_tables(positions):
    half_rot = ROT // 2
    frequency = 10000.0 ** (-2.0 * jnp.arange(half_rot, dtype=jnp.float32) / ROT)
    angles = positions[:, None] * frequency[None, :]
    cosine = jnp.concatenate([jnp.cos(angles), jnp.cos(angles)], axis=-1)
    sine_vals = jnp.concatenate([jnp.sin(angles), jnp.sin(angles)], axis=-1)
    return (cosine, sine_vals)


def rotate(vector, cosine, sine_vals):
    half_rot = ROT // 2
    rotary_part = vector[..., :ROT]
    turned = jnp.concatenate([-rotary_part[..., half_rot:], rotary_part[..., :half_rot]], axis=-1)
    return jnp.concatenate([rotary_part * cosine + turned * sine_vals, vector[..., ROT:]], axis=-1)


def plan(n, here, per, M, tk):
    order = [(s, j) for j in reversed(range(per)) for s in range(here)]
    row = lambda i, j: (i * per + j) * M
    price = lambda first: first // tk + 1.4
    moved = [0] * n
    for i in range(n // 2, n):
        load = lambda k: max(
            sum(price(row(i, j)) for _, j in order[k:]),
            sum(price(row(n - 1 - i, j)) for _, j in order) + sum(price(row(i, j)) for _, j in order[:k]))
        moved[i] = min(range(len(order)), key=load)
    most = max(moved)
    takes = [[(here * per + k, s, row(n - 1 - i, j)) for k, (s, j) in enumerate(order[:moved[n - 1 - i]])] if i < n // 2 else []
             for i in range(n)]
    keeps = [[(s * per + j, s, row(i, j)) for s, j in order[moved[i]:]] for i in range(n)]
    cost = lambda steps: sum(price(x[2]) for x in steps)
    mean = sum(cost(t) + cost(k) for t, k in zip(takes, keeps)) / n
    lists = ([], [], [])
    for take, keep in zip(takes, keeps):
        keep = list(keep)
        head, middle = [], list(take)
        while keep and cost(head) + price(keep[0][2]) / 2 < 0.22 * mean:
            head.append(keep.pop(0))
        while keep and cost(middle) + price(keep[0][2]) / 2 < 0.56 * mean and cost(keep) > 0.22 * mean:
            middle.append(keep.pop(0))
        for part, steps in zip(lists, (head, middle, keep)):
            part.append(steps)
    tables = []
    for part in lists:
        size = max(1, max(len(w) for w in part))
        full = [[x + (1,) for x in w] + [(w[-1] if w else (0, 0, 0)) + (0,)] * (size - len(w)) for w in part]
        tables.append(np.array(full, np.int32))
    return order, moved, most, tables


def local(
    mesh, states, cotangent, subsets, subset_weight, gain_attn, shift_attn, gain_ffn, shift_ffn,
    query_projection, pair_projection, output_projection, up_projection, down_projection,
):
    f32, bf16 = jnp.float32, jnp.bfloat16
    both = ("seq", "rows")
    here, length_here, D = states.shape
    T = here * length_here
    n_seq, n_rows = mesh.shape["seq"], mesh.shape["rows"]
    n = n_seq * n_rows
    length = length_here * n_seq
    block = lax.axis_index("seq")
    offset = block * length_here
    M = min(128, length_here)
    per = length_here // M
    tk = min(512, length)
    FF = up_projection.shape[1]
    P = 2 * HD
    scale = HD ** -0.5
    own_rows = query_projection.shape[0]
    aligned = (2 * own_rows) % 16 == 0 and own_rows % 8 == 0

    rows_here = offset + jnp.arange(length_here, dtype=jnp.int32)
    cosine, sine_vals = rotary_tables(rows_here.astype(f32))
    source = states.astype(f32).reshape(T, D)
    unit, inverse = layer_norm(source)
    table_rows = jnp.arange(subset_weight.shape[0], dtype=jnp.int32)
    row_scale = jnp.sum(
        jnp.where(table_rows[None, :] == subsets[:, None], subset_weight[None, :], 0.0), axis=1
    )
    upstream = (cotangent.astype(f32) * row_scale[:, None, None]).reshape(T, D)

    if aligned:
        tiles = FF // D
        packed = jnp.concatenate([
            jnp.swapaxes(up_projection.reshape(own_rows, tiles, D), 0, 1).reshape(-1, D), down_projection])
        packed = lax.all_gather(packed, both, axis=0)
        squares = jnp.concatenate([query_projection, output_projection], axis=0)
        pairs = jnp.pad(pair_projection, ((0, -own_rows % 32), (0, 0)))
        norms = jnp.stack([gain_attn, shift_attn, gain_ffn, shift_ffn])
        scales = jnp.broadcast_to(row_scale[:, None], (here, D))
        queries, out_grad, all_kv, attention_input, feedforward_input, branch_grad, squares, full_pair = front(
            states.reshape(T, D), cotangent.reshape(T, D), scales, norms, squares, pairs,
            here, length, M, n_seq, n_rows, 1)
        full_query, full_output = squares[0], squares[1]
    else:
        big = jnp.stack([up_projection, down_projection.reshape(up_projection.shape)])
        big = lax.all_gather(big, both, axis=1, tiled=True)
        full_up, full_down = big[0], big[1].reshape(FF, D)
        small = jnp.concatenate([query_projection, pair_projection, output_projection], axis=1)
        small = lax.all_gather(small, both, axis=0, tiled=True)
        full_query, full_pair, full_output = small[:, :D], small[:, D:D + P], small[:, D + P:]
        attention_input = (unit * gain_attn + shift_attn).astype(bf16)
        feedforward_input = (unit * gain_ffn + shift_ffn).astype(bf16)
        branch_grad = upstream.astype(bf16)
        pair_pre = jnp.dot(attention_input, full_pair, preferred_element_type=f32)
        pair_pre = pair_pre.reshape(here, length_here, P)
        key_values = jnp.concatenate(
            [rotate(pair_pre[..., :HD], cosine[None], sine_vals[None]), pair_pre[..., HD:]], axis=2
        ).astype(bf16)
        query_pre = jnp.dot(attention_input, full_query, preferred_element_type=f32)
        queries = rotate(
            query_pre.reshape(here, length_here, H, HD) * (scale / LN2),
            cosine[None, :, None, :], sine_vals[None, :, None, :],
        ).astype(bf16).reshape(T, D)
        out_grad = lax.dot_general(
            branch_grad, full_output, (((1,), (1,)), ((), ())), preferred_element_type=f32
        ).astype(bf16)
        all_kv = lax.all_gather(key_values, "seq", axis=0)

    order, moved, most, tables = plan(n_seq, here, per, M, tk)
    own = here * per
    q_tiles, g_tiles = queries.reshape(own, M, D), out_grad.reshape(own, M, D)
    others = []
    for k in range(most):
        s, j = order[k]
        pairs_of = [(i, n_seq - 1 - i) for i in range(n_seq) if moved[i] > k]
        others.append(lax.ppermute(jnp.stack([q_tiles[s * per + j], g_tiles[s * per + j]]), "seq", pairs_of))
    steps = []
    for table in tables:
        mine = jnp.asarray(table)[block]
        steps.append(tuple(mine[:, c] for c in range(4)))
    done = attention(steps[0], queries, out_grad, None, all_kv, M, tk, most)

    ffn_x, done = lax.optimization_barrier((feedforward_input, done))
    if aligned:
        ffn_out, ffn_input_grad, ffn_grads = ffn_packed(ffn_x, branch_grad, packed, n_seq, n_rows)
    else:
        ffn_out, ffn_input_grad, grad_up, grad_down = ffn(ffn_x, branch_grad, full_up, full_down)
        ffn_grads = jnp.concatenate(
            [grad_up.reshape(n_seq, n_rows, -1, D), grad_down.reshape(n_seq, n_rows, -1, D)], axis=2)
        ffn_grads = jnp.swapaxes(ffn_grads, 0, 1)
    done, ffn_out = lax.optimization_barrier((done, ffn_out))
    ffn_grads = lax.psum_scatter(ffn_grads, "rows", scatter_dimension=0, tiled=True)[0]
    ffn_grads = lax.psum_scatter(ffn_grads, "seq", scatter_dimension=0, tiled=True)[0]
    half = ffn_grads.shape[0] // 2
    final_up = ffn_grads[:half]
    if aligned:
        final_up = jnp.swapaxes(final_up.reshape(FF // D, own_rows, D), 0, 1)
    final_up = final_up.reshape(-1, FF).astype(f32)
    final_down = ffn_grads[half:].astype(f32)

    done = attention(steps[1], queries, out_grad, jnp.stack(others), all_kv, M, tk, most, done)
    backs = []
    for k in range(most):
        pairs_of = [(n_seq - 1 - i, i) for i in range(n_seq) if moved[i] > k]
        tile = slice((own + k) * M, (own + k + 1) * M)
        backs.append(lax.ppermute(jnp.stack([done[0][tile], done[1][tile]]), "seq", pairs_of))
    attended, query_pre_grad, pair_terms = attention(steps[2], queries, out_grad, None, all_kv, M, tk, most, done)
    a_own, d_own = list(attended.reshape(-1, M, D)[:own]), list(query_pre_grad.reshape(-1, M, D)[:own])
    count = jnp.asarray(np.array(moved, np.int32))[block]
    for k in range(most):
        s, j = order[k]
        at = s * per + j
        a_own[at] = jnp.where(count > k, backs[k][0], a_own[at])
        d_own[at] = jnp.where(count > k, backs[k][1], d_own[at])
    attended, query_pre_grad = jnp.concatenate(a_own), jnp.concatenate(d_own)

    pair_terms = pair_terms.astype(bf16).reshape(here, P, n_seq, length_here)
    pair_terms = jnp.moveaxis(pair_terms, 2, 0)
    arrived = lax.all_to_all(pair_terms, "seq", split_axis=0, concat_axis=0, tiled=True)
    pair_grad = jnp.swapaxes(arrived.astype(f32).sum(axis=0), 1, 2)

    residual = jnp.dot(attended, full_output, preferred_element_type=f32) + ffn_out
    layer_out = (source + residual).astype(bf16).reshape(here, length_here, D)
    grad_output = lax.dot_general(
        attended, branch_grad, (((0,), (0,)), ((), ())), preferred_element_type=f32)
    grad_query = lax.dot_general(
        attention_input, query_pre_grad, (((0,), (0,)), ((), ())), preferred_element_type=f32)
    attn_input_grad = lax.dot_general(
        query_pre_grad, full_query, (((1,), (1,)), ((), ())), preferred_element_type=f32)

    pair_pre_grad = jnp.concatenate(
        [rotate(pair_grad[..., :HD] * LN2, cosine[None], -sine_vals[None]), pair_grad[..., HD:]], axis=2
    ).reshape(T, P).astype(bf16)
    grad_pair = lax.dot_general(
        attention_input, pair_pre_grad, (((0,), (0,)), ((), ())), preferred_element_type=f32)
    attn_input_grad = attn_input_grad + lax.dot_general(
        pair_pre_grad, full_pair, (((1,), (1,)), ((), ())), preferred_element_type=f32)

    sums = jnp.stack([
        jnp.sum(attn_input_grad * unit, axis=0), jnp.sum(attn_input_grad, axis=0),
        jnp.sum(ffn_input_grad * unit, axis=0), jnp.sum(ffn_input_grad, axis=0)], axis=1)
    grad_states = upstream + norm_back(attn_input_grad, unit, inverse, gain_attn)
    grad_states = grad_states + norm_back(ffn_input_grad, unit, inverse, gain_ffn)
    grad_states = grad_states.astype(bf16).reshape(here, length_here, D)

    last = jnp.concatenate([grad_query, grad_pair, jnp.pad(sums, ((0, 0), (0, 124))), grad_output], axis=1)
    if aligned:
        last = jnp.pad(last, ((0, 0), (0, -last.shape[1] % 512)))
        last = scatter(last.reshape(n, own_rows, -1), n_seq, n_rows, 3)
    else:
        last = lax.psum_scatter(last.astype(bf16), both, scatter_dimension=0, tiled=True).astype(f32)
    vectors = last[:, D + P:]
    at = D + P + 128
    return (
        layer_out, grad_states,
        vectors[:, 0], vectors[:, 1], vectors[:, 2], vectors[:, 3],
        last[:, :D], last[:, D:D + P], last[:, at:at + D], final_up, final_down,
    )


def solution(mesh):
    from jax.sharding import PartitionSpec as P

    blocks, owned = P("rows", "seq", None), P(("seq", "rows"), None)
    vector = P(("seq", "rows"))
    return jax.shard_map(
        functools.partial(local, mesh),
        mesh=mesh,
        in_specs=(blocks, blocks, P("rows"), P(), P(), P(), P(), P()) + (owned,) * 5,
        out_specs=(blocks, blocks) + (vector,) * 4 + (owned,) * 5,
        check_vma=False,
    )
```

```python
import functools
import jax
import jax.numpy as jnp
import numpy as np
from jax import lax
from jax.experimental import pallas as pl
from jax.experimental.pallas import tpu as pltpu

H = 12
HD = 64
LN2 = 0.6931471805599453


def dot(a, b, ca, cb):
    return lax.dot_general(a, b, (((ca,), (cb,)), ((), ())), preferred_element_type=jnp.float32)


def three_parts(x):
    hi = x.astype(jnp.bfloat16)
    rest = x - hi.astype(jnp.float32)
    mid = rest.astype(jnp.bfloat16)
    low = (rest - mid.astype(jnp.float32)).astype(jnp.bfloat16)
    return hi, mid, low


ROT = 16


def turn_tables(length, M):
    frequency = 10000.0 ** (-2.0 * np.arange(ROT // 2) / ROT)
    lanes = np.zeros(HD)
    lanes[:ROT] = np.concatenate([frequency, frequency])
    lanes = np.concatenate([lanes, lanes])

    def table(places):
        angles = places[:, None] * lanes[None, :]
        return np.concatenate([np.cos(angles), np.sin(angles)], axis=1).astype(np.float32)

    return table(np.arange(M)), table(np.arange(0, length, M))


def turn_factors(near, far):
    cn, sn, cf, sf = near[:, :128], near[:, 128:], far[:, :128], far[:, 128:]
    sine = sf * cn + cf * sn
    lane = lax.broadcasted_iota(jnp.int32, sine.shape, 1) & (HD - 1)
    low = jnp.where(lane < ROT // 2, sine, 0.0)
    high = jnp.where((lane >= ROT // 2) & (lane < ROT), sine, 0.0)
    return cf * cn - sf * sn, low, high


def turn(z, cosine, low, high):
    return z * cosine - pltpu.roll(z, 120, 1) * low + pltpu.roll(z, 8, 1) * high


def turn_back(z, cosine, low, high):
    return z * cosine + pltpu.roll(z, 120, 1) * low - pltpu.roll(z, 8, 1) * high


def attn_kernel(
    M, tk, own, first_call,
    slot_ref, seq_ref, row_ref, on_ref,
    q_ref, g_ref, other_ref, near_ref, far_ref, kv_ref, *refs,
):
    if not first_call:
        refs = refs[2:]
        before_ref, refs = refs[0], refs[1:]
    o_ref, dq_ref, dkv_ref = refs[:3]
    ka, va, qs, gs, qt, gt, stash, oacc, dqacc, top, limit = refs[3:]
    t = pl.program_id(0)
    seq = seq_ref[t]
    row0 = row_ref[t]
    G = 4 * M
    groups = [slice(g * G, (g + 1) * G) for g in range(H // 4)]
    heads = [slice(h * M, (h + 1) * M) for h in range(H)]
    f32, bf16 = jnp.float32, jnp.bfloat16
    parts_, count, block, _ = kv_ref.shape

    @pl.when(t == 0)
    def _():
        if first_call:
            dkv_ref[...] = jnp.zeros_like(dkv_ref)
        else:
            dkv_ref[...] = before_ref[...]
        lane = lax.broadcasted_iota(jnp.int32, (block, HD), 1)
        ones = jnp.where(lane < 3, 1.0, 0.0).astype(bf16)

        def arrange(i, most):
            for s in range(count):
                kv = kv_ref[i, s]
                rows = pl.ds(pl.multiple_of(i * block, block), block)
                ka[s, rows, :] = jnp.concatenate([kv[:, :HD], ones], axis=1)
                va[s, rows, :] = jnp.concatenate([kv[:, HD:], ones], axis=1)
                k = kv[:, :HD].astype(f32)
                most = jnp.maximum(most, jnp.max(jnp.sum(k * k, axis=1, keepdims=True)))
            return most

        limit[0] = lax.fori_loop(0, parts_, arrange, jnp.float32(0.0))

    @pl.when(on_ref[t] != 0)
    def _():
        taken = slot_ref[t] >= own
        q_in = q_ref[...] if other_ref is None else jnp.where(taken, other_ref[0, 0], q_ref[...])
        g_in = g_ref[...] if other_ref is None else jnp.where(taken, other_ref[0, 1], g_ref[...])
        for h in range(H):
            qs[heads[h], :HD] = q_in[:, h * HD:(h + 1) * HD]
            qs[heads[h], HD:] = jnp.zeros((M, 128 - HD), bf16)
        oacc[...] = jnp.zeros_like(oacc)
        dqacc[...] = jnp.zeros_like(dqacc)
        n_full = row0 // tk

        def keys(ref, kt):
            return ref[seq, pl.ds(pl.multiple_of(kt * tk, tk), tk), :]

        def allowed(kt):
            row = row0 + (lax.broadcasted_iota(jnp.int32, (G, tk), 0) & (M - 1))
            col = kt * tk + lax.broadcasted_iota(jnp.int32, (G, tk), 1)
            return col <= row

        def scores(kt, r, masked):
            s = dot(qs[r, :], keys(ka, kt), 1, 1)
            if masked:
                s = jnp.where(allowed(kt), s, -1e30)
            return s

        most = jnp.float32(0.0)
        for r in groups:
            q = qs[r, :].astype(f32)
            most = jnp.maximum(most, jnp.max(jnp.sum(q * q, axis=1, keepdims=True)))

        @pl.when(most * limit[0] > 3600.0)
        def _():
            top[...] = jnp.full_like(top, -1e30)

            def peak(kt, masked):
                for r in groups:
                    s = scores(kt, r, masked)
                    part = s[:, :128]
                    for j in range(1, tk // 128):
                        part = jnp.maximum(part, s[:, j * 128:(j + 1) * 128])
                    top[r, :] = jnp.maximum(top[r, :], part)

            lax.fori_loop(0, n_full, lambda kt, _: (peak(kt, False), 0)[1], 0)
            peak(n_full, True)
            for r in heads:
                best = -jnp.max(top[r, :], axis=1, keepdims=True)
                for j, part in enumerate(three_parts(best)):
                    qs[r, HD + j:HD + j + 1] = part

        def first(kt, masked):
            v = keys(va, kt)
            for r in groups:
                e = jnp.exp2(scores(kt, r, masked)).astype(bf16)
                stash[kt, r, :] = e
                oacc[r, :] += dot(e, v, 1, 0)

        lax.fori_loop(0, n_full, lambda kt, _: (first(kt, False), 0)[1], 0)
        first(n_full, True)

        for p in range(H // 2):
            outs = []
            for h in (2 * p, 2 * p + 1):
                r = heads[h]
                acc = oacc[r, :]
                inverse = 1.0 / acc[:, HD:HD + 1]
                out = acc[:, :HD] * inverse
                outs.append(out)
                low = (g_in[:, h * HD:(h + 1) * HD].astype(f32) * inverse).astype(bf16)
                delta = -jnp.sum(low.astype(f32) * out, axis=1, keepdims=True)
                gs[r, :] = jnp.concatenate(
                    [low, *three_parts(delta), jnp.zeros((M, 128 - HD - 3), bf16)], axis=1)
            o_ref[:, p * 128:(p + 1) * 128] = jnp.concatenate(outs, axis=1).astype(bf16)
        qt[...] = qs[...].T
        gt[...] = gs[...].T

        def second(kt):
            k = keys(ka, kt)
            v = keys(va, kt)
            dk = jnp.zeros((HD, tk), f32)
            dv = jnp.zeros((HD, tk), f32)
            for r in groups:
                e = stash[kt, r, :]
                slope = (e.astype(f32) * dot(gs[r, :], v, 1, 1)).astype(bf16)
                dqacc[r, :] += dot(slope, k, 1, 0)
                dk = dk + dot(qt[:HD, r], slope, 1, 0)
                dv = dv + dot(gt[:HD, r], e, 1, 0)
            c = pl.ds(pl.multiple_of(kt * tk, tk), tk)
            dkv_ref[seq, :HD, c] += dk
            dkv_ref[seq, HD:, c] += dv

        lax.fori_loop(0, n_full + 1, lambda kt, _: (second(kt), 0)[1], 0)
        factors = turn_factors(near_ref[...], far_ref[pl.ds(row0 // M, 1), :])
        for p in range(H // 2):
            z = jnp.concatenate([dqacc[heads[h], :HD] for h in (2 * p, 2 * p + 1)], axis=1)
            dq_ref[:, p * 128:(p + 1) * 128] = (turn_back(z, *factors) * HD ** -0.5).astype(bf16)


def attention(tables, q, g, others, skip, kv, M, tk, most, before=None):
    width = H * HD
    steps = tables[0].shape[0]
    own = q.shape[0] // M
    parts, S, block, _ = kv.shape
    L = parts * block
    near, far = turn_tables(L, M)
    whole = pl.Buffered(1)
    tile = pl.BlockSpec((M, width), lambda t, slot, *_: (slot[t], 0))
    near_spec = pl.BlockSpec(near.shape, lambda t, *_: (0, 0), pipeline_mode=whole)
    far_spec = pl.BlockSpec(far.shape, lambda t, *_: (0, 0), pipeline_mode=whole)
    mine = pl.BlockSpec((M, width), lambda t, slot, *_: (jnp.minimum(slot[t], own - 1), 0))
    taken = pl.BlockSpec((1, 2, M, width), lambda t, slot, *_: (jnp.maximum(slot[t] - own - skip, 0), 0, 0, 0))
    sums = pl.BlockSpec((S, 128, L), lambda t, *_: (0, 0, 0), pipeline_mode=whole)
    anywhere = pl.BlockSpec(memory_space=pl.ANY)
    bf16, f32 = jnp.bfloat16, jnp.float32
    pairs = steps * M * H * L // 3
    kernel = functools.partial(attn_kernel, M, tk, own, before is None)
    operands, specs = [q, g], [mine, mine]
    if others is None:
        inner = kernel
        kernel = lambda a, b, c, d, q_ref, g_ref, *refs: inner(a, b, c, d, q_ref, g_ref, None, *refs)
    else:
        operands, specs = operands + [others], specs + [taken]
    operands += [near, far, kv]
    specs += [near_spec, far_spec, pl.BlockSpec(kv.shape, lambda t, *_: (0, 0, 0, 0), pipeline_mode=whole)]
    aliases = {}
    if before is not None:
        aliases = {4 + len(operands) + i: i for i in range(3)}
        operands, specs = operands + list(before), specs + [anywhere, anywhere, sums]
    slots = jax.ShapeDtypeStruct(((own + most) * M, width), bf16)
    return pl.pallas_call(
        kernel,
        grid_spec=pltpu.PrefetchScalarGridSpec(
            num_scalar_prefetch=4,
            grid=(steps,),
            in_specs=specs,
            out_specs=[tile, tile, sums],
            scratch_shapes=[
                pltpu.VMEM((S, L, 128), bf16),
                pltpu.VMEM((S, L, 128), bf16),
                pltpu.VMEM((H * M, 128), bf16),
                pltpu.VMEM((H * M, 128), bf16),
                pltpu.VMEM((128, H * M), bf16),
                pltpu.VMEM((128, H * M), bf16),
                pltpu.VMEM((L // tk, H * M, tk), bf16),
                pltpu.VMEM((H * M, 128), f32),
                pltpu.VMEM((H * M, 128), f32),
                pltpu.VMEM((H * M, 128), f32),
                pltpu.SMEM((1,), f32),
            ],
        ),
        out_shape=[slots, slots, jax.ShapeDtypeStruct((S, 128, L), f32)],
        input_output_aliases=aliases,
        compiler_params=pltpu.CompilerParams(vmem_limit_bytes=58 << 20),
        cost_estimate=pl.CostEstimate(flops=1 << 20, bytes_accessed=1 << 16, transcendentals=0),
        name="attention",
    )(*tables, *operands)


MESH = pl.DeviceIdType.MESH


def bits_of(n_seq, n_rows):
    high = [("seq", 1 << b) for b in reversed(range(n_seq.bit_length() - 1))]
    return high + [("rows", 1 << b) for b in reversed(range(n_rows.bit_length() - 1))]


def place(bits):
    return [lax.rem(lax.axis_index(axis) // weight, 2) for axis, weight in bits]


def partner(bit):
    axis, weight = bit
    mine = lax.axis_index(axis)
    return {axis: mine + weight - 2 * weight * lax.rem(mine // weight, 2)}


def greet(bits):
    barrier = pltpu.get_barrier_semaphore()
    for bit in bits:
        pl.semaphore_signal(barrier, inc=1, device_id=partner(bit), device_id_type=MESH)
    pl.semaphore_wait(barrier, len(bits))


def routes(bits):
    n = len(bits)
    one = list(range(n))
    other = list(range(n))
    near = max(i for i in range(n) if bits[i][0] == "seq")
    if near + 1 < n - 1:
        other[near], other[near + 1] = other[near + 1], other[near]
    return one, other


def gelu_both(x):
    z = jnp.abs(x) * 0.7071067811865476
    s = 1.0 / (1.0 + 0.3275911 * z)
    poly = s * (0.127414796 + s * (-0.142248368 + s * (0.710706871 + s * (-0.7265760135 + s * 0.5307027145))))
    bell = jnp.exp(-z * z)
    tail = poly * bell
    phi = jnp.where(x >= 0.0, 1.0 - tail, tail)
    return x * phi, phi + x * (bell * 0.3989422804014327)


def ffn_kernel(C, x_ref, b_ref, up_ref, down_ref, out_ref, dx_ref, gup_ref, gdown_ref, act_s, ug_s):
    f = pl.program_id(0)
    T = x_ref.shape[0]

    @pl.when(f == 0)
    def _():
        out_ref[...] = jnp.zeros_like(out_ref)
        dx_ref[...] = jnp.zeros_like(dx_ref)

    up = up_ref[...]
    down = down_ref[...]
    for c in range(T // C):
        r = slice(c * C, (c + 1) * C)
        u = dot(x_ref[r, :], up, 1, 0)
        a = dot(b_ref[r, :], down, 1, 1)
        act, slope = gelu_both(u)
        act = act.astype(jnp.bfloat16)
        ug = (a * slope).astype(jnp.bfloat16)
        act_s[r, :] = act
        ug_s[r, :] = ug
        out_ref[r, :] += dot(act, down, 1, 0)
        dx_ref[r, :] += dot(ug, up, 1, 1)
    gup_ref[...] = dot(x_ref[...], ug_s[...], 0, 0).astype(gup_ref.dtype)
    gdown_ref[...] = dot(act_s[...], b_ref[...], 0, 0).astype(gdown_ref.dtype)


def ffn(x, b, up, down, F=512, C=256, wire=jnp.bfloat16):
    T, D = x.shape
    FF = up.shape[1]
    C = min(C, T)
    f32, bf16 = jnp.float32, jnp.bfloat16
    whole = lambda f: (0, 0)
    return pl.pallas_call(
        functools.partial(ffn_kernel, C),
        grid=(FF // F,),
        in_specs=[
            pl.BlockSpec((T, D), whole, pipeline_mode=pl.Buffered(1)),
            pl.BlockSpec((T, D), whole, pipeline_mode=pl.Buffered(1)),
            pl.BlockSpec((D, F), lambda f: (0, f)),
            pl.BlockSpec((F, D), lambda f: (f, 0)),
        ],
        out_specs=[
            pl.BlockSpec((T, D), whole, pipeline_mode=pl.Buffered(1)),
            pl.BlockSpec((T, D), whole, pipeline_mode=pl.Buffered(1)),
            pl.BlockSpec((D, F), lambda f: (0, f)),
            pl.BlockSpec((F, D), lambda f: (f, 0)),
        ],
        out_shape=[
            jax.ShapeDtypeStruct((T, D), f32),
            jax.ShapeDtypeStruct((T, D), f32),
            jax.ShapeDtypeStruct((D, FF), wire),
            jax.ShapeDtypeStruct((FF, D), wire),
        ],
        scratch_shapes=[pltpu.VMEM((T, F), bf16), pltpu.VMEM((T, F), bf16)],
        compiler_params=pltpu.CompilerParams(vmem_limit_bytes=56 << 20),
        cost_estimate=pl.CostEstimate(flops=12 * T * D * FF, bytes_accessed=32 << 20, transcendentals=T * FF),
        name="feedforward",
    )(x, b, up, down)


def ffn_packed_kernel(
    C, bits, M, order, moved,
    x_ref, b_ref, up_ref, down_ref, kv_ref, q_ref, g_ref,
    out_ref, dx_ref, grads_ref, all_kv, others,
    act_s, ug_s, wide, ups, own_sem, kv_send, kv_recv, tile_send, tile_recv,
):
    f = pl.program_id(0)
    T, D = x_ref.shape
    groups, each, _, count, _ = up_ref.shape
    tiles = ups.shape[0]
    n = groups * each
    owned = D // n
    f32, bf16 = jnp.float32, jnp.bfloat16
    stages = len(bits)
    me = place(bits)
    block = lax.axis_index("seq")
    n_seq = len(moved)
    local = kv_ref.shape[1]

    def kv_copies(stage):
        copies = []
        for half in (0, 1):
            route = list(range(stages)) if half == 0 else [stages - 1] + list(range(stages - 1))
            at = tuple(slice(None) if i in route[:stage] else me[i] for i in range(stages))
            piece = all_kv.at[at + (slice(None), pl.ds(half * (local // 2), local // 2))]
            copies.append(pltpu.make_async_remote_copy(
                src_ref=piece, dst_ref=piece, send_sem=kv_send.at[half, stage], recv_sem=kv_recv.at[half, stage],
                device_id=partner(bits[route[stage]]), device_id_type=MESH))
        return copies

    def tile_copies(k):
        r = pl.ds(order[k] * M, M)
        return [pltpu.make_async_remote_copy(
            src_ref=ref.at[r], dst_ref=others.at[k, i], send_sem=tile_send.at[k, i], recv_sem=tile_recv.at[k, i],
            device_id={"seq": n_seq - 1 - block}, device_id_type=MESH) for i, ref in enumerate((q_ref, g_ref))]

    def among(devices):
        return functools.reduce(jnp.logical_or, [block == i for i in devices])

    @pl.when(f == 0)
    def _():
        own = pltpu.make_async_copy(kv_ref, all_kv.at[tuple(me)], own_sem)
        own.start()
        barrier = pltpu.get_barrier_semaphore()
        for bit in bits:
            pl.semaphore_signal(barrier, inc=1, device_id=partner(bit), device_id_type=MESH)
        pl.semaphore_signal(barrier, inc=1, device_id={"seq": n_seq - 1 - block}, device_id_type=MESH)
        pl.semaphore_wait(barrier, stages + 1)
        own.wait()

    for stage in range(stages):
        @pl.when(f == min(stage, tiles - 1))
        def _(stage=stage):
            if stage > 0:
                for copy in kv_copies(stage - 1):
                    copy.wait()
            for copy in kv_copies(stage):
                copy.start()

    @pl.when(f == 1)
    def _():
        for k in range(len(order)):
            @pl.when(among([i for i in range(n_seq) if moved[i] > k]))
            def _(k=k):
                for copy in tile_copies(k):
                    copy.start()

    @pl.when(f == 0)
    def _():
        out_ref[...] = jnp.zeros_like(out_ref)
        dx_ref[...] = jnp.zeros_like(dx_ref)

        def unpack(d, _):
            part = up_ref[d // each, lax.rem(d, each), 0].astype(f32)
            for j in range(tiles):
                at = pl.ds(pl.multiple_of(d * owned, 8), owned)
                wide[j, at, :] = part[j * owned:(j + 1) * owned]
            return 0

        lax.fori_loop(0, n, unpack, 0)
        for j in range(tiles):
            ups[j] = wide[j].astype(bf16)

    up = ups[f]
    down = down_ref[...].reshape(D, D)
    for c in range(T // C):
        r = slice(c * C, (c + 1) * C)
        u = dot(x_ref[r, :], up, 1, 0)
        a = dot(b_ref[r, :], down, 1, 1)
        act, slope = gelu_both(u)
        act = act.astype(bf16)
        ug = (a * slope).astype(bf16)
        act_s[r, :] = act
        ug_s[r, :] = ug
        out_ref[r, :] += dot(act, down, 1, 0)
        dx_ref[r, :] += dot(ug, up, 1, 1)
    wide[f] = dot(x_ref[...], ug_s[...], 0, 0)
    grad_down = dot(act_s[...], b_ref[...], 0, 0).astype(bf16)
    for k in range(each):
        at = f * each + k
        grads_ref[at, count:] = grad_down[k * count:(k + 1) * count]

    @pl.when(f == tiles - 1)
    def _():
        def pack(d, _):
            at = pl.ds(pl.multiple_of(d * owned, 8), owned)
            part = jnp.concatenate([wide[j, at, :] for j in range(tiles)], axis=0)
            grads_ref[d, :count] = part.astype(bf16)
            return 0

        lax.fori_loop(0, n, pack, 0)
        for copy in kv_copies(stages - 1):
            copy.wait()
        for k in range(len(order)):
            @pl.when(among([i for i in range(n_seq) if moved[i] > k]))
            def _(k=k):
                for copy in tile_copies(k):
                    copy.wait_send()

            @pl.when(among([n_seq - 1 - i for i in range(n_seq) if moved[i] > k]))
            def _(k=k):
                for copy in tile_copies(k):
                    copy.wait_recv()


def ffn_packed(x, b, packed, kv, q, g, order, moved, M, n_seq, collective_id, C=256):
    T, D = x.shape
    n, count = packed.shape[0], packed.shape[1] // 2
    FF = n * count
    tiles = FF // D
    each = n // tiles
    packed = packed.reshape(tiles, each, 2, count, D)
    f32, bf16 = jnp.float32, jnp.bfloat16
    once = pl.Buffered(1)
    whole = lambda f: (0, 0)
    bits = bits_of(n_seq, 1)
    anywhere = pl.BlockSpec(memory_space=pl.ANY)
    out, dx, grads, all_kv, others = pl.pallas_call(
        functools.partial(ffn_packed_kernel, C, bits, M, tuple(order), tuple(moved)),
        grid=(tiles,),
        in_specs=[
            pl.BlockSpec((T, D), whole, pipeline_mode=once),
            pl.BlockSpec((T, D), whole, pipeline_mode=once),
            pl.BlockSpec((tiles, each, 1, count, D), lambda f: (0, 0, 0, 0, 0), pipeline_mode=once),
            pl.BlockSpec((1, each, 1, count, D), lambda f: (f, 0, 1, 0, 0)),
            anywhere, anywhere, anywhere,
        ],
        out_specs=[
            pl.BlockSpec((T, D), whole, pipeline_mode=once),
            pl.BlockSpec((T, D), whole, pipeline_mode=once),
            pl.BlockSpec((n, 2 * count, D), lambda f: (0, 0, 0), pipeline_mode=once),
            anywhere, anywhere,
        ],
        out_shape=[
            jax.ShapeDtypeStruct((T, D), f32),
            jax.ShapeDtypeStruct((T, D), f32),
            jax.ShapeDtypeStruct((n, 2 * count, D), bf16),
            jax.ShapeDtypeStruct((2,) * len(bits) + kv.shape, bf16),
            jax.ShapeDtypeStruct((len(order), 2, M, D), bf16),
        ],
        scratch_shapes=[
            pltpu.VMEM((T, D), bf16), pltpu.VMEM((T, D), bf16),
            pltpu.VMEM((tiles, D, D), f32), pltpu.VMEM((tiles, D, D), bf16),
            pltpu.SemaphoreType.DMA,
            pltpu.SemaphoreType.DMA((2, len(bits))), pltpu.SemaphoreType.DMA((2, len(bits))),
            pltpu.SemaphoreType.DMA((len(order), 2)), pltpu.SemaphoreType.DMA((len(order), 2)),
        ],
        compiler_params=pltpu.CompilerParams(
            collective_id=collective_id, has_side_effects=True, vmem_limit_bytes=60 << 20),
        cost_estimate=pl.CostEstimate(flops=1 << 20, bytes_accessed=1 << 16, transcendentals=0),
        name="feedforward",
    )(x, b, packed, packed, kv, q, g)
    return out, dx, grads, all_kv.reshape((n_seq,) + kv.shape), others


def streams_of(bits, squares, hidden):
    n = len(bits)
    one, other = routes(bits)
    near = max(i for i in range(n) if bits[i][0] == "seq")
    last = [i for i in (near, near + 1) if i < n - 1]
    last += [i for i in range(n - 1) if i not in last] + [n - 1]
    early, late = list(range(n)), list(range(2, n + 2))
    split = list(range(2)) + list(range(4, n + 2))
    unit = squares // 48 * 16
    head = hidden // 12 // 16 * 16
    tail = hidden // 6 // 16 * 16
    rest = (hidden - 2 * head - tail) // 2
    return [
        (0, 0, 16, one, early), (0, 16, 16, other, early),
        (1, 0, unit, one, early), (1, unit, squares - unit, other, early),
        (2, 0, head, one, early), (2, head, head, other, early),
        (2, 2 * head, rest, one, late), (2, 2 * head + rest, rest, other, late),
        (2, 2 * head + 2 * rest, tail, last, split),
    ]


def front_kernel(
    bits, here, M, chunk, streams,
    x_ref, c_ref, scale_ref, norm_ref, near_ref, far_ref, query_ref, pair_ref, output_ref, up_ref, down_ref,
    q_ref, g_ref, kv_ref, xa_ref, xf_ref, b_ref, wide_ref, wp, hidden_ref,
    pr_all, sq_all, hidden_own, stage_q, stage_o, stage_p,
    own_sem, send_sem, recv_sem,
):
    f32, bf16 = jnp.float32, jnp.bfloat16
    T, D = x_ref.shape
    n = len(bits)
    me = place(bits)
    owned = query_ref.shape[0]
    tiles = up_ref.shape[1] // D
    rows = hidden_own.shape[0] // 2
    up = up_ref[...].astype(f32)
    hidden_own[:rows, :] = jnp.concatenate([up[:, j * D:(j + 1) * D] for j in range(tiles)], axis=0).astype(bf16)
    hidden_own[rows:, :] = down_ref[...]
    own = pltpu.make_async_copy(hidden_own, hidden_ref.at[tuple(me)], own_sem)
    own.start()
    squares = jnp.concatenate([query_ref[...].astype(f32), output_ref[...].astype(f32)], axis=0)
    sq_all[tuple(me)] = squares.astype(bf16)
    pairs = jnp.concatenate([pair_ref[...].astype(f32), jnp.zeros((pr_all.shape[-2] - owned, 128), f32)], axis=0)
    pr_all[tuple(me)] = pairs.astype(bf16)
    greet(bits)
    own.wait()

    def normalize(i):
        r = slice(i * chunk, (i + 1) * chunk)
        x = x_ref[r, :].astype(f32)
        x = x - jnp.mean(x, axis=1, keepdims=True)
        unit = x * lax.rsqrt(jnp.mean(x * x, axis=1, keepdims=True) + 1e-05)
        xa_ref[r, :] = (unit * norm_ref[0:1, :] + norm_ref[1:2, :]).astype(bf16)
        xf_ref[r, :] = (unit * norm_ref[2:3, :] + norm_ref[3:4, :]).astype(bf16)
        part = i * chunk // (T // here)
        b_ref[r, :] = (c_ref[r, :].astype(f32) * scale_ref[part:part + 1, :]).astype(bf16)

    def unpack():
        for d in range(1 << n):
            at = tuple((d >> (n - 1 - i)) & 1 for i in range(n))
            r = slice(d * owned, (d + 1) * owned)
            both = sq_all[at].astype(f32)
            stage_q[r, :] = both[:owned]
            stage_o[r, :] = both[owned:2 * owned]
            stage_p[r, :] = pr_all[at].astype(f32)[:owned]
        wp[...] = stage_p[...].astype(bf16)
        wide_ref[0] = stage_q[...].astype(bf16)
        wide_ref[1] = stage_o[...].astype(bf16)

    block = lax.axis_index("seq")
    per = T // here // M
    tables = []
    for j in range(per):
        tables.append(turn_factors(near_ref[...], far_ref[pl.ds(block * per + j, 1), :]))
    first = lax.broadcasted_iota(jnp.int32, (M, 128), 1) < HD

    def keys(i):
        r = slice(i * chunk, (i + 1) * chunk)
        kv = dot(xa_ref[r, :], wp[...], 1, 0)
        for j in range(chunk // M):
            part = kv[j * M:(j + 1) * M]
            turned = turn(part, *tables[(i * chunk // M + j) % per])
            kv_ref[i * chunk + j * M:i * chunk + (j + 1) * M, :] = jnp.where(first, turned, part).astype(bf16)

    def queries(i):
        r = slice(i * chunk, (i + 1) * chunk)
        z = dot(xa_ref[r, :], wide_ref[0], 1, 0)
        for j in range(chunk // M):
            tab = tables[(i * chunk // M + j) % per]
            for p in range(D // 128):
                c = slice(p * 128, (p + 1) * 128)
                part = turn(z[j * M:(j + 1) * M, c], *tab) * (HD ** -0.5 / LN2)
                q_ref[i * chunk + j * M:i * chunk + (j + 1) * M, c] = part.astype(bf16)

    def gradients(i):
        r = slice(i * chunk, (i + 1) * chunk)
        g_ref[r, :] = dot(b_ref[r, :], wide_ref[1], 1, 1).astype(bf16)

    chunks = T // chunk
    rounds = max(s[4][-1] for s in streams) + 1
    jobs = [[] for _ in range(rounds)]
    for i in range(chunks):
        jobs[min(i, n - 1)].append(functools.partial(normalize, i))
    jobs[min(n, rounds - 1)] += [unpack] + [functools.partial(f, i) for f in (keys, queries, gradients) for i in range(chunks)]
    arrays = (pr_all, sq_all, hidden_ref)
    held = [set() for _ in streams]
    for now in range(rounds):
        copies = []
        for i, (a, start, size, order, when) in enumerate(streams):
            if now not in when:
                continue
            stage = when.index(now)
            where = tuple(slice(None) if b in held[i] else me[b] for b in range(n))
            piece = arrays[a].at[where + (pl.ds(start, size),)]
            copy = pltpu.make_async_remote_copy(
                src_ref=piece, dst_ref=piece, send_sem=send_sem.at[i, stage], recv_sem=recv_sem.at[i, stage],
                device_id=partner(bits[order[stage]]), device_id_type=MESH)
            copy.start()
            copies.append(copy)
            held[i].add(order[stage])
        for job in jobs[now]:
            job()
        for copy in copies:
            copy.wait()


def front(x, c, scale, norms, query, pair, output, up, down, here, length, M, n_seq, n_rows, collective_id, chunk=256):
    bits = bits_of(n_seq, n_rows)
    n = len(bits)
    T, D = x.shape
    owned, hidden = query.shape[0], 2 * down.shape[0]
    f32, bf16 = jnp.float32, jnp.bfloat16
    near, far = turn_tables(length, M)
    vmem = pl.BlockSpec(memory_space=pltpu.VMEM)
    token = jax.ShapeDtypeStruct((T, D), bf16)
    streams = streams_of(bits, 2 * owned, hidden)
    q, g, kv, xa, xf, b, wide, wp, packed = pl.pallas_call(
        functools.partial(front_kernel, bits, here, M, chunk, streams),
        out_shape=[token, token, jax.ShapeDtypeStruct((T, 128), bf16), token, token, token,
                   jax.ShapeDtypeStruct((2, D, D), bf16), jax.ShapeDtypeStruct((D, 128), bf16),
                   jax.ShapeDtypeStruct((2,) * n + (hidden, D), bf16)],
        in_specs=[vmem] * 11,
        out_specs=[vmem] * 8 + [pl.BlockSpec(memory_space=pl.ANY)],
        scratch_shapes=[
            pltpu.VMEM((2,) * n + (32, 128), bf16),
            pltpu.VMEM((2,) * n + (2 * owned, D), bf16),
            pltpu.VMEM((hidden, D), bf16),
            pltpu.VMEM((D, D), f32),
            pltpu.VMEM((D, D), f32),
            pltpu.VMEM((D, 128), f32),
            pltpu.SemaphoreType.DMA,
            pltpu.SemaphoreType.DMA((len(streams), n)),
            pltpu.SemaphoreType.DMA((len(streams), n)),
        ],
        compiler_params=pltpu.CompilerParams(
            collective_id=collective_id, has_side_effects=True, vmem_limit_bytes=56 << 20),
        name="front",
    )(x, c, scale, norms, near, far, query, pair, output, up, down)
    return q, g, kv, xa, xf, b, wide, wp, packed.reshape(1 << n, hidden, D)


class Halving:
    def __init__(self, bits, order, me, first, send, recv, acc, send_sem, recv_sem):
        self.bits, self.order, self.me, self.first = bits, order, me, first
        self.send, self.recv, self.acc = send, recv, acc
        self.send_sem, self.recv_sem = send_sem, recv_sem
        self.copy = None

    def spot(self, stage, j, own):
        left = sorted(self.order[stage:])
        b = self.order[stage]
        rest = [i for i in left if i != b]
        index = 0
        for i in left:
            if i == b:
                bit = self.me[b] if own else 1 - self.me[b]
            else:
                bit = lax.rem(j // (1 << (len(rest) - 1 - rest.index(i))), 2)
            index = index * 2 + bit
        return index

    def block(self, stage, at):
        return self.first(at) if stage == 0 else self.acc[stage - 1][at]

    def start(self, stage):
        def fill(j, _):
            self.send[stage][j] = self.block(stage, self.spot(stage, j, False)).astype(jnp.bfloat16)
            return 0

        lax.fori_loop(0, 1 << (len(self.order) - 1 - stage), fill, 0)
        self.copy = pltpu.make_async_remote_copy(
            src_ref=self.send[stage], dst_ref=self.recv[stage],
            send_sem=self.send_sem.at[stage], recv_sem=self.recv_sem.at[stage],
            device_id=partner(self.bits[self.order[stage]]), device_id_type=MESH)
        self.copy.start()

    def finish(self, stage):
        self.copy.wait()

        def add(j, _):
            own = self.block(stage, self.spot(stage, j, True))
            self.acc[stage][j] = own + self.recv[stage][j].astype(jnp.float32)
            return 0

        lax.fori_loop(0, 1 << (len(self.order) - 1 - stage), add, 0)


def halving_shapes(stages, rows, columns):
    sizes = [(1 << (stages - 1 - s), rows, columns) for s in range(stages)]
    half = [pltpu.VMEM(s, jnp.bfloat16) for s in sizes]
    return half + half + [pltpu.VMEM(s, jnp.float32) for s in sizes] + [
        pltpu.SemaphoreType.DMA((stages,)), pltpu.SemaphoreType.DMA((stages,))]


def post_kernel(bits, here, M, order, moved, chunk, *refs):
    (sums_ref, o_hbm, dq_hbm, *refs) = refs
    backs, refs = refs[:len(order)], refs[len(order):]
    (xa_ref, b_ref, x_hbm, c_hbm, out_hbm, dx_hbm, wide_ref, wp_ref, norm_ref, scale_ref, near_ref, far_ref,
     layer_ref, states_ref, square_ref, small_ref, *refs) = refs
    f32, bf16 = jnp.float32, jnp.bfloat16
    T, D = xa_ref.shape
    n = len(bits)
    seq_bits = [i for i in range(n) if bits[i][0] == "seq"]
    n_s = len(seq_bits)
    me = place(bits)
    o_ref, dq_ref, x_ref, c_ref, out_ref, dx_ref, ai_ref, gq, go, gs, load_sem, *refs = refs

    def take(stages):
        nonlocal refs
        mine, refs = refs[:3 * stages + 2], refs[3 * stages + 2:]
        return mine[:stages], mine[stages:2 * stages], mine[2 * stages:3 * stages], mine[-2], mine[-1]

    loads = [pltpu.make_async_copy(s, d, load_sem.at[i])
             for i, (s, d) in enumerate((
                 (dq_hbm.at[:T], dq_ref), (o_hbm.at[:T], o_ref), (out_hbm, out_ref),
                 (x_hbm, x_ref), (dx_hbm, dx_ref), (c_hbm, c_ref)))]
    for load in loads:
        load.start()
    greet(bits)

    owned = D >> n
    local = T // here
    per = local // M
    wide = sums_ref.shape[2] >> n_s

    def keys_first(s):
        return lambda at: sums_ref[s, :, pl.ds(pl.multiple_of(at * wide, 128), wide)]

    def square_first(ref):
        def get(at):
            r = pl.ds(pl.multiple_of(at * owned, 8), owned)
            return jnp.concatenate([ref[r, :D // 2], ref[r, D // 2:]], axis=0)
        return get

    def small_first(at):
        r = pl.ds(pl.multiple_of(at * owned, 8), owned)
        return jnp.concatenate([gs[r, :128], gs[r, 128:]], axis=0)

    x_first = seq_bits[::-1]
    z_first = x_first[1:] + x_first[:1]
    kv = [Halving(bits, z_first if s % 2 else x_first, me, keys_first(s), *take(n_s)) for s in range(here)]
    routes_back = [list(reversed(o)) for o in routes(bits)]
    squares = [Halving(bits, routes_back[i], me, square_first(ref), *take(n)) for i, ref in enumerate((gq, go))]
    small = Halving(bits, routes_back[0], me, small_first, *take(n))

    for h in kv:
        h.start(0)

    block = lax.axis_index("seq")
    loads[0].wait()
    loads[1].wait()
    for k, at in enumerate(order):
        r = slice(at * M, (at + 1) * M)
        away = functools.reduce(jnp.logical_or, [block == i for i in range(len(moved)) if moved[i] > k])
        o_ref[r, :] = jnp.where(away, backs[k][0], o_ref[r, :])
        dq_ref[r, :] = jnp.where(away, backs[k][1], dq_ref[r, :])

    gq[...] = dot(xa_ref[...], dq_ref[...], 0, 0)
    squares[0].start(0)
    go[...] = dot(o_ref[...], b_ref[...], 0, 0)
    squares[1].start(0)
    for h in kv:
        h.finish(0)
        h.start(1)
    loads[2].wait()
    loads[3].wait()
    chunks = T // chunk

    def forward(i):
        r = slice(i * chunk, (i + 1) * chunk)
        total = x_ref[r, :].astype(f32) + (dot(o_ref[r, :], wide_ref[1], 1, 0) + out_ref[r, :])
        layer_ref[r, :] = total.astype(bf16)

    def backward(i):
        r = slice(i * chunk, (i + 1) * chunk)
        ai_ref[r, :] = dot(dq_ref[r, :], wide_ref[0], 1, 1)

    jobs = [functools.partial(f, i) for f in (forward, backward) for i in range(chunks)]
    gaps = n - 1
    for stage in range(n):
        for h in squares:
            h.finish(stage)
            if stage + 1 < n:
                h.start(stage + 1)
        for i, job in enumerate(jobs):
            if i * gaps // len(jobs) == stage:
                job()
        if 0 < stage < n_s:
            for h in kv:
                h.finish(stage)
                if stage + 1 < n_s:
                    h.start(stage + 1)
    for i, h in enumerate(squares):
        total = h.acc[n - 1][0]
        square_ref[i, :, :D // 2] = total[:owned]
        square_ref[i, :, D // 2:] = total[owned:]

    first = lax.broadcasted_iota(jnp.int32, (M, 128), 1) < HD
    grads = []
    for s in range(here):
        home = kv[s].acc[n_s - 1][0].T
        for j in range(per):
            factors = turn_factors(near_ref[...], far_ref[pl.ds(block * per + j, 1), :])
            part = home[j * M:(j + 1) * M]
            turned = turn_back(part, *factors) * LN2
            grads.append(jnp.where(first, turned, part).astype(bf16))
    pairs = jnp.concatenate(grads, axis=0)
    gs[:, :128] = dot(xa_ref[...], pairs, 0, 0)
    loads[4].wait()
    loads[5].wait()
    totals = [jnp.zeros((1, D), f32) for _ in range(4)]
    for i in range(chunks):
        r = slice(i * chunk, (i + 1) * chunk)
        x = x_ref[r, :].astype(f32)
        x = x - jnp.mean(x, axis=1, keepdims=True)
        inverse = lax.rsqrt(jnp.mean(x * x, axis=1, keepdims=True) + 1e-05)
        unit = x * inverse
        ai = ai_ref[r, :] + dot(pairs[r], wp_ref[...], 1, 1)
        fi = dx_ref[r, :]
        for k, part in enumerate((ai * unit, ai, fi * unit, fi)):
            totals[k] = totals[k] + jnp.sum(part, axis=0, keepdims=True)
        both = ai * norm_ref[0:1, :] + fi * norm_ref[2:3, :]
        middle = jnp.mean(both, axis=1, keepdims=True)
        slope = jnp.mean(both * unit, axis=1, keepdims=True)
        part = i * chunk // local
        up = c_ref[r, :].astype(f32) * scale_ref[part:part + 1, :]
        states_ref[r, :] = (up + inverse * (both - middle - unit * slope)).astype(bf16)
    rows = jnp.concatenate(totals + [jnp.zeros((124, D), f32)], axis=0)
    gs[:, 128:] = rows.T
    for stage in range(n):
        small.start(stage)
        small.finish(stage)
    total = small.acc[n - 1][0]
    small_ref[:, :128] = total[:owned]
    small_ref[:, 128:] = total[owned:]


def post(sums, o, dq, backs, order, moved, xa, b, x, c, out, dx, wide, wp, norms, scales,
         here, length, M, n_seq, n_rows, collective_id, chunk=256):
    bits = bits_of(n_seq, n_rows)
    n, n_s = len(bits), n_seq.bit_length() - 1
    T, D = xa.shape
    owned = D >> n
    f32, bf16 = jnp.float32, jnp.bfloat16
    near, far = turn_tables(length, M)
    vmem, anywhere = pl.BlockSpec(memory_space=pltpu.VMEM), pl.BlockSpec(memory_space=pl.ANY)
    token = jax.ShapeDtypeStruct((T, D), bf16)
    scratch = [
        *[pltpu.VMEM((T, D), bf16)] * 4, *[pltpu.VMEM((T, D), f32)] * 3,
        pltpu.VMEM((D, D), f32), pltpu.VMEM((D, D), f32), pltpu.VMEM((D, 256), f32),
        pltpu.SemaphoreType.DMA((6,)),
    ]
    for _ in range(here):
        scratch += halving_shapes(n_s, 128, length // n_seq)
    for _ in range(2):
        scratch += halving_shapes(n, 2 * owned, D // 2)
    scratch += halving_shapes(n, 2 * owned, 128)
    return pl.pallas_call(
        functools.partial(post_kernel, bits, here, M, tuple(order), tuple(moved), chunk),
        out_shape=[token, token, jax.ShapeDtypeStruct((2, owned, D), f32), jax.ShapeDtypeStruct((owned, 256), f32)],
        in_specs=[vmem, anywhere, anywhere] + [vmem] * len(backs) + [vmem] * 2 + [anywhere] * 4 + [vmem] * 6,
        out_specs=[vmem] * 4,
        scratch_shapes=scratch,
        compiler_params=pltpu.CompilerParams(
            collective_id=collective_id, has_side_effects=True, vmem_limit_bytes=60 << 20),
        name="post",
    )(sums, o, dq, *backs, xa, b, x, c, out, dx, wide, wp, norms, scales, near, far)


def layer_norm(values):
    center = values - jnp.mean(values, axis=-1, keepdims=True)
    inverse = lax.rsqrt(jnp.mean(center * center, axis=-1, keepdims=True) + 1e-05)
    return center * inverse, inverse


def norm_back(incoming, normed, inverse, gain):
    scaled = incoming * gain
    return inverse * (
        scaled
        - jnp.mean(scaled, axis=-1, keepdims=True)
        - normed * jnp.mean(scaled * normed, axis=-1, keepdims=True)
    )


def rotary_tables(positions):
    half_rot = ROT // 2
    frequency = 10000.0 ** (-2.0 * jnp.arange(half_rot, dtype=jnp.float32) / ROT)
    angles = positions[:, None] * frequency[None, :]
    cosine = jnp.concatenate([jnp.cos(angles), jnp.cos(angles)], axis=-1)
    sine_vals = jnp.concatenate([jnp.sin(angles), jnp.sin(angles)], axis=-1)
    return (cosine, sine_vals)


def rotate(vector, cosine, sine_vals):
    half_rot = ROT // 2
    rotary_part = vector[..., :ROT]
    turned = jnp.concatenate([-rotary_part[..., half_rot:], rotary_part[..., :half_rot]], axis=-1)
    return jnp.concatenate([rotary_part * cosine + turned * sine_vals, vector[..., ROT:]], axis=-1)


def plan(n, here, per, M, tk):
    order = [(s, j) for j in reversed(range(per)) for s in range(here)]
    row = lambda i, j: (i * per + j) * M
    price = lambda first: first // tk + 1.4
    moved = [0] * n
    for i in range(n // 2, n):
        load = lambda k: max(
            sum(price(row(i, j)) for _, j in order[k:]),
            sum(price(row(n - 1 - i, j)) for _, j in order) + sum(price(row(i, j)) for _, j in order[:k]))
        moved[i] = min(range(len(order)), key=load)
    most = max(moved)
    takes = [[(here * per + k, s, row(n - 1 - i, j)) for k, (s, j) in enumerate(order[:moved[n - 1 - i]])] if i < n // 2 else []
             for i in range(n)]
    keeps = [[(s * per + j, s, row(i, j)) for s, j in order[moved[i]:]] for i in range(n)]
    cost = lambda steps: sum(price(x[2]) for x in steps)
    mean = sum(cost(t) + cost(k) for t, k in zip(takes, keeps)) / n
    lists = ([], [], [])
    for take, keep in zip(takes, keeps):
        keep, head, middle = list(keep), list(take[:1]), list(take[1:])
        while len(keep) > 1 and cost(head) + price(keep[0][2]) / 2 < 0.32 * mean:
            head.append(keep.pop(0))
        while len(keep) > 1 and cost(middle) + price(keep[0][2]) / 2 < 0.42 * mean and cost(keep) > 0.24 * mean:
            middle.append(keep.pop(0))
        for part, steps in zip(lists, (head, middle, keep)):
            part.append(steps)
    tables = []
    for part in lists:
        size = max(1, max(len(w) for w in part))
        full = [[x + (1,) for x in w] + [(w[-1] if w else (0, 0, 0)) + (0,)] * (size - len(w)) for w in part]
        tables.append(np.array(full, np.int32))
    return order, moved, most, tables


def local(
    mesh, states, cotangent, subsets, subset_weight, gain_attn, shift_attn, gain_ffn, shift_ffn,
    query_projection, pair_projection, output_projection, up_projection, down_projection,
):
    f32, bf16 = jnp.float32, jnp.bfloat16
    both = ("seq", "rows")
    here, length_here, D = states.shape
    T = here * length_here
    n_seq, n_rows = mesh.shape["seq"], mesh.shape["rows"]
    n = n_seq * n_rows
    length = length_here * n_seq
    block = lax.axis_index("seq")
    offset = block * length_here
    M = min(128, length_here)
    per = length_here // M
    tk = min(512, length)
    FF = up_projection.shape[1]
    P = 2 * HD
    scale = HD ** -0.5
    own_rows = query_projection.shape[0]
    aligned = own_rows % 8 == 0 and here % 2 == 0

    rows_here = offset + jnp.arange(length_here, dtype=jnp.int32)
    cosine, sine_vals = rotary_tables(rows_here.astype(f32))
    table_rows = jnp.arange(subset_weight.shape[0], dtype=jnp.int32)
    row_scale = jnp.sum(
        jnp.where(table_rows[None, :] == subsets[:, None], subset_weight[None, :], 0.0), axis=1
    )
    if aligned:
        norms = jnp.stack([gain_attn, shift_attn, gain_ffn, shift_ffn])
        scales = jnp.broadcast_to(row_scale[:, None], (here, D))
        queries, out_grad, own_kv, attention_input, feedforward_input, branch_grad, wide, full_pair, packed = front(
            states.reshape(T, D), cotangent.reshape(T, D), scales, norms, query_projection, pair_projection,
            output_projection, up_projection, down_projection, here, length, M, n_seq, n_rows, 1)
    else:
        source = states.astype(f32).reshape(T, D)
        unit, inverse = layer_norm(source)
        upstream = (cotangent.astype(f32) * row_scale[:, None, None]).reshape(T, D)
        big = jnp.stack([up_projection, down_projection.reshape(up_projection.shape)])
        big = lax.all_gather(big, both, axis=1, tiled=True)
        full_up, full_down = big[0], big[1].reshape(FF, D)
        small = jnp.concatenate([query_projection, pair_projection, output_projection], axis=1)
        small = lax.all_gather(small, both, axis=0, tiled=True)
        full_query, full_pair, full_output = small[:, :D], small[:, D:D + P], small[:, D + P:]
        attention_input = (unit * gain_attn + shift_attn).astype(bf16)
        feedforward_input = (unit * gain_ffn + shift_ffn).astype(bf16)
        branch_grad = upstream.astype(bf16)
        pair_pre = jnp.dot(attention_input, full_pair, preferred_element_type=f32)
        pair_pre = pair_pre.reshape(here, length_here, P)
        key_values = jnp.concatenate(
            [rotate(pair_pre[..., :HD], cosine[None], sine_vals[None]), pair_pre[..., HD:]], axis=2
        ).astype(bf16)
        query_pre = jnp.dot(attention_input, full_query, preferred_element_type=f32)
        queries = rotate(
            query_pre.reshape(here, length_here, H, HD) * (scale / LN2),
            cosine[None, :, None, :], sine_vals[None, :, None, :],
        ).astype(bf16).reshape(T, D)
        out_grad = lax.dot_general(
            branch_grad, full_output, (((1,), (1,)), ((), ())), preferred_element_type=f32
        ).astype(bf16)
        all_kv = lax.all_gather(key_values, "seq", axis=0)

    order, moved, most, tables = plan(n_seq, here, per, M, tk)
    own = here * per
    at_slots = [s * per + j for s, j in order[:most]]
    steps = []
    for table in tables:
        mine = jnp.asarray(table)[block]
        steps.append(tuple(mine[:, c] for c in range(4)))
    q_tiles, g_tiles = queries.reshape(own, M, D), out_grad.reshape(own, M, D)

    def send(k):
        pairs_of = [(i, n_seq - 1 - i) for i in range(n_seq) if moved[i] > k]
        return lax.ppermute(jnp.stack([q_tiles[at_slots[k]], g_tiles[at_slots[k]]]), "seq", pairs_of)

    def send_back(done, k):
        pairs_of = [(n_seq - 1 - i, i) for i in range(n_seq) if moved[i] > k]
        tile = slice((own + k) * M, (own + k + 1) * M)
        return lax.ppermute(jnp.stack([done[0][tile], done[1][tile]]), "seq", pairs_of)

    if aligned:
        ffn_out, ffn_input_grad, ffn_grads, all_kv, first_taken = ffn_packed(
            feedforward_input, branch_grad, packed, own_kv.reshape(here, length_here, P), queries, out_grad,
            at_slots[:1], moved, M, n_seq, 3)
    else:
        first_taken = send(0)[None]
        ffn_out, ffn_input_grad, grad_up, grad_down = ffn(feedforward_input, branch_grad, full_up, full_down)
        ffn_grads = jnp.concatenate([grad_up.reshape(n, -1, D), grad_down.reshape(n, -1, D)], axis=1)
    ffn_grads = lax.psum_scatter(ffn_grads, both, scatter_dimension=0, tiled=True)[0]
    done = attention(steps[0], queries, out_grad, first_taken, 0, all_kv, M, tk, most)
    backs = [send_back(done, 0)]
    if most > 1:
        taken = jnp.stack([send(k) for k in range(1, most)])
        done = attention(steps[1], queries, out_grad, taken, 1, all_kv, M, tk, most, done)
    else:
        done = attention(steps[1], queries, out_grad, None, 0, all_kv, M, tk, most, done)
    backs += [send_back(done, k) for k in range(1, most)]
    half = ffn_grads.shape[0] // 2
    final_up = ffn_grads[:half]
    if aligned:
        final_up = jnp.swapaxes(final_up.reshape(FF // D, own_rows, D), 0, 1)
    final_up = final_up.reshape(-1, FF).astype(f32)
    final_down = ffn_grads[half:].astype(f32)
    attended, query_pre_grad, pair_terms = attention(steps[2], queries, out_grad, None, 0, all_kv, M, tk, most, done)
    if aligned:
        layer_out, grad_states, squares, small = post(
            pair_terms, attended, query_pre_grad, backs, at_slots, moved, attention_input, branch_grad,
            states.reshape(T, D), cotangent.reshape(T, D), ffn_out, ffn_input_grad, wide, full_pair, norms, scales,
            here, length, M, n_seq, n_rows, 2)
        vectors = small[:, P:]
        return (
            layer_out.reshape(states.shape), grad_states.reshape(states.shape),
            vectors[:, 0], vectors[:, 1], vectors[:, 2], vectors[:, 3],
            squares[0], small[:, :P], squares[1], final_up, final_down,
        )

    a_own, d_own = list(attended.reshape(-1, M, D)[:own]), list(query_pre_grad.reshape(-1, M, D)[:own])
    count = jnp.asarray(np.array(moved, np.int32))[block]
    for k in range(most):
        s, j = order[k]
        at = s * per + j
        a_own[at] = jnp.where(count > k, backs[k][0], a_own[at])
        d_own[at] = jnp.where(count > k, backs[k][1], d_own[at])
    attended, query_pre_grad = jnp.concatenate(a_own), jnp.concatenate(d_own)

    pair_terms = pair_terms.astype(bf16).reshape(here, P, n_seq, length_here)
    pair_terms = jnp.moveaxis(pair_terms, 2, 0)
    arrived = lax.all_to_all(pair_terms, "seq", split_axis=0, concat_axis=0, tiled=True)
    pair_grad = jnp.swapaxes(arrived.astype(f32).sum(axis=0), 1, 2)

    residual = jnp.dot(attended, full_output, preferred_element_type=f32) + ffn_out
    layer_out = (source + residual).astype(bf16).reshape(here, length_here, D)
    grad_output = lax.dot_general(
        attended, branch_grad, (((0,), (0,)), ((), ())), preferred_element_type=f32)
    grad_query = lax.dot_general(
        attention_input, query_pre_grad, (((0,), (0,)), ((), ())), preferred_element_type=f32)
    attn_input_grad = lax.dot_general(
        query_pre_grad, full_query, (((1,), (1,)), ((), ())), preferred_element_type=f32)

    pair_pre_grad = jnp.concatenate(
        [rotate(pair_grad[..., :HD] * LN2, cosine[None], -sine_vals[None]), pair_grad[..., HD:]], axis=2
    ).reshape(T, P).astype(bf16)
    grad_pair = lax.dot_general(
        attention_input, pair_pre_grad, (((0,), (0,)), ((), ())), preferred_element_type=f32)
    attn_input_grad = attn_input_grad + lax.dot_general(
        pair_pre_grad, full_pair, (((1,), (1,)), ((), ())), preferred_element_type=f32)

    sums = jnp.stack([
        jnp.sum(attn_input_grad * unit, axis=0), jnp.sum(attn_input_grad, axis=0),
        jnp.sum(ffn_input_grad * unit, axis=0), jnp.sum(ffn_input_grad, axis=0)], axis=1)
    grad_states = upstream + norm_back(attn_input_grad, unit, inverse, gain_attn)
    grad_states = grad_states + norm_back(ffn_input_grad, unit, inverse, gain_ffn)
    grad_states = grad_states.astype(bf16).reshape(here, length_here, D)

    last = jnp.concatenate([grad_query, grad_pair, jnp.pad(sums, ((0, 0), (0, 124))), grad_output], axis=1)
    last = lax.psum_scatter(last.astype(bf16), both, scatter_dimension=0, tiled=True).astype(f32)
    vectors = last[:, D + P:]
    at = D + P + 128
    return (
        layer_out, grad_states,
        vectors[:, 0], vectors[:, 1], vectors[:, 2], vectors[:, 3],
        last[:, :D], last[:, D:D + P], last[:, at:at + D], final_up, final_down,
    )


def solution(mesh):
    from jax.sharding import PartitionSpec as P

    blocks, owned = P("rows", "seq", None), P(("seq", "rows"), None)
    vector = P(("seq", "rows"))
    return jax.shard_map(
        functools.partial(local, mesh),
        mesh=mesh,
        in_specs=(blocks, blocks, P("rows"), P(), P(), P(), P(), P()) + (owned,) * 5,
        out_specs=(blocks, blocks) + (vector,) * 4 + (owned,) * 5,
        check_vma=False,
    )
```

```python
import functools
import jax
import jax.numpy as jnp
import numpy as np
from jax import lax
from jax.experimental import pallas as pl
from jax.experimental.pallas import tpu as pltpu

H = 12
HD = 64
LN2 = 0.6931471805599453


def dot(a, b, ca, cb):
    return lax.dot_general(a, b, (((ca,), (cb,)), ((), ())), preferred_element_type=jnp.float32)


def three_parts(x):
    hi = x.astype(jnp.bfloat16)
    rest = x - hi.astype(jnp.float32)
    mid = rest.astype(jnp.bfloat16)
    low = (rest - mid.astype(jnp.float32)).astype(jnp.bfloat16)
    return hi, mid, low


ROT = 16


def turn_tables(length, M):
    frequency = 10000.0 ** (-2.0 * np.arange(ROT // 2) / ROT)
    lanes = np.zeros(HD)
    lanes[:ROT] = np.concatenate([frequency, frequency])
    lanes = np.concatenate([lanes, lanes])

    def table(places):
        angles = places[:, None] * lanes[None, :]
        return np.concatenate([np.cos(angles), np.sin(angles)], axis=1).astype(np.float32)

    return table(np.arange(M)), table(np.arange(0, length, M))


def turn_factors(near, far):
    cn, sn, cf, sf = near[:, :128], near[:, 128:], far[:, :128], far[:, 128:]
    sine = sf * cn + cf * sn
    lane = lax.broadcasted_iota(jnp.int32, sine.shape, 1) & (HD - 1)
    low = jnp.where(lane < ROT // 2, sine, 0.0)
    high = jnp.where((lane >= ROT // 2) & (lane < ROT), sine, 0.0)
    return cf * cn - sf * sn, low, high


def turn(z, cosine, low, high):
    return z * cosine - pltpu.roll(z, 120, 1) * low + pltpu.roll(z, 8, 1) * high


def turn_back(z, cosine, low, high):
    return z * cosine + pltpu.roll(z, 120, 1) * low - pltpu.roll(z, 8, 1) * high


def attn_kernel(
    M, tk, own, first_call,
    slot_ref, seq_ref, row_ref, on_ref,
    q_ref, g_ref, other_ref, near_ref, far_ref, kv_ref, *refs,
):
    if not first_call:
        before_ref, refs = refs[2], refs[3:]
    o_ref, dq_ref, sums_ref, *refs = refs
    given_ref = None
    if other_ref is not None:
        given_ref, *refs = refs
    ka, va, qs, gs, qt, gt, stash, oacc, dqacc, top, delta, dkv_ref, limit, sum_sem = refs
    t = pl.program_id(0)
    seq = seq_ref[t]
    row0 = row_ref[t]
    G = 4 * M
    groups = [slice(g * G, (g + 1) * G) for g in range(H // 4)]
    heads = [slice(h * M, (h + 1) * M) for h in range(H)]
    f32, bf16 = jnp.float32, jnp.bfloat16
    parts_, count, block, _ = kv_ref.shape

    row_head = lax.broadcasted_iota(jnp.int32, (128, 128), 0) // HD
    spread = (row_head == lax.broadcasted_iota(jnp.int32, (128, 128), 1) // HD).astype(bf16)
    only_keys = (row_head == 0).astype(bf16)

    @pl.when(t == 0)
    def _():
        if first_call:
            dkv_ref[...] = jnp.zeros_like(dkv_ref)
        else:
            pltpu.make_async_copy(before_ref, dkv_ref, sum_sem).start()
        lower = lax.broadcasted_iota(jnp.int32, (block, 128), 1) < HD
        one = jnp.ones((block, 128), bf16)

        def arrange(i, most):
            for s in range(count):
                kv = kv_ref[i, s]
                rows = pl.ds(pl.multiple_of(i * block, block), block)
                ka[s, rows, :] = jnp.where(lower, kv, one)
                va[s, rows, :] = jnp.where(lower, one, kv)
                most = jnp.maximum(most, dot(kv * kv, only_keys, 1, 0))
            return most

        limit[0] = jnp.max(lax.fori_loop(0, parts_, arrange, jnp.zeros((block, 128), f32)))

    @pl.when(on_ref[t] != 0)
    def _():
        taken = slot_ref[t] >= own
        q_in = q_ref[...] if other_ref is None else jnp.where(taken, other_ref[0, 0], q_ref[...])
        g_in = g_ref[...] if other_ref is None else jnp.where(taken, other_ref[0, 1], g_ref[...])
        lane = lax.broadcasted_iota(jnp.int32, (M, 128), 1)
        low_half = lane < HD
        most = jnp.zeros((M, 128), f32)
        for p in range(H // 2):
            pair = q_in[:, p * 128:(p + 1) * 128]
            most = jnp.maximum(most, dot(pair * pair, spread, 1, 0))
            pair = pair.astype(f32)
            qs[heads[2 * p], :] = jnp.where(low_half, pair, 0.0).astype(bf16)
            qs[heads[2 * p + 1], :] = jnp.where(low_half, pltpu.roll(pair, HD, 1), 0.0).astype(bf16)
        oacc[...] = jnp.zeros_like(oacc)
        dqacc[...] = jnp.zeros_like(dqacc)
        n_full = row0 // tk

        def keys(ref, kt, size=tk):
            return ref[seq, pl.ds(pl.multiple_of(kt * tk, tk), size), :]

        def allowed(kt, size):
            row = row0 + (lax.broadcasted_iota(jnp.int32, (G, size), 0) & (M - 1))
            col = kt * tk + lax.broadcasted_iota(jnp.int32, (G, size), 1)
            return col <= row

        def scores(kt, r, masked, size=tk):
            s = dot(qs[r, :], keys(ka, kt, size), 1, 1)
            if masked:
                s = jnp.where(allowed(kt, size), s, -1e30)
            return s

        short = row0 + M - n_full * tk <= tk // 2

        def last(step):
            @pl.when(short)
            def _():
                step(tk // 2)

            @pl.when(jnp.logical_not(short))
            def _():
                step(tk)

        @pl.when(jnp.max(most) * limit[0] > 3600.0)
        def _():
            top[...] = jnp.full_like(top, -1e30)

            def peak(kt, masked):
                for r in groups:
                    s = scores(kt, r, masked)
                    part = s[:, :128]
                    for j in range(1, tk // 128):
                        part = jnp.maximum(part, s[:, j * 128:(j + 1) * 128])
                    top[r, :] = jnp.maximum(top[r, :], part)

            lax.fori_loop(0, n_full, lambda kt, _: (peak(kt, False), 0)[1], 0)
            peak(n_full, True)
            for r in heads:
                best = -jnp.max(top[r, :], axis=1, keepdims=True)
                for j, part in enumerate(three_parts(best)):
                    qs[r, HD + j:HD + j + 1] = part

        def first(kt, masked, size=tk):
            v = keys(va, kt, size)
            for r in groups:
                e = jnp.exp2(scores(kt, r, masked, size)).astype(bf16)
                stash[kt, r, :size] = e
                oacc[r, :] += dot(e, v, 1, 0)

        lax.fori_loop(0, n_full, lambda kt, _: (first(kt, False), 0)[1], 0)
        last(lambda size: first(n_full, True, size))

        ones = jnp.ones((3 * 128, 128), bf16)
        for p in range(H // 2):
            grads = g_in[:, p * 128:(p + 1) * 128].astype(f32)
            outs = []
            for h in (2 * p, 2 * p + 1):
                r = heads[h]
                acc = oacc[r, :]
                inverse = pltpu.roll(1.0 / acc, HD, 1)
                out = acc * inverse
                outs.append(out)
                grad = grads if h % 2 == 1 else pltpu.roll(grads, HD, 1)
                low = jnp.where(low_half, 0.0, grad * inverse).astype(bf16).astype(f32)
                delta[r, :] = dot(jnp.concatenate(three_parts(low * out), axis=1), ones, 1, 0)
                gs[r, :] = low.astype(bf16)
            out = jnp.where(low_half, pltpu.roll(outs[0], HD, 1), outs[1]).astype(bf16)
            o_ref[:, p * 128:(p + 1) * 128] = out
            if given_ref is not None:
                @pl.when(taken)
                def _(p=p, out=out):
                    given_ref[0, 0, :, p * 128:(p + 1) * 128] = out
        qt[...] = qs[...].T
        gt[...] = gs[...].T

        if not first_call:
            @pl.when(t == 0)
            def _():
                pltpu.make_async_copy(before_ref, dkv_ref, sum_sem).wait()

        def second(kt, size=tk):
            k = keys(ka, kt, size)
            v = keys(va, kt, size)
            dk = jnp.zeros((HD, size), f32)
            dv = jnp.zeros((HD, size), f32)
            for r in groups:
                e = stash[kt, r, :size]
                slope = e.astype(f32) * (dot(gs[r, :], v, 1, 1) - jnp.tile(delta[r, :], (1, size // 128)))
                slope = slope.astype(bf16)
                dqacc[r, :] += dot(slope, k, 1, 0)
                dk = dk + dot(qt[:HD, r], slope, 1, 0)
                dv = dv + dot(gt[HD:, r], e, 1, 0)
            c = pl.ds(pl.multiple_of(kt * tk, tk), size)
            dkv_ref[seq, :HD, c] += dk
            dkv_ref[seq, HD:, c] += dv

        lax.fori_loop(0, n_full, lambda kt, _: (second(kt), 0)[1], 0)
        last(lambda size: second(n_full, size))
        factors = turn_factors(near_ref[...], far_ref[pl.ds(row0 // M, 1), :])
        for p in range(H // 2):
            z = jnp.where(low_half, dqacc[heads[2 * p], :], pltpu.roll(dqacc[heads[2 * p + 1], :], HD, 1))
            z = (turn_back(z, *factors) * HD ** -0.5).astype(bf16)
            dq_ref[:, p * 128:(p + 1) * 128] = z
            if given_ref is not None:
                @pl.when(taken)
                def _(p=p, z=z):
                    given_ref[0, 1, :, p * 128:(p + 1) * 128] = z

    @pl.when(t == pl.num_programs(0) - 1)
    def _():
        copy = pltpu.make_async_copy(dkv_ref, sums_ref, sum_sem)
        copy.start()
        copy.wait()


def attention(tables, q, g, others, skip, kv, M, tk, before=None):
    width = H * HD
    steps = tables[0].shape[0]
    own = q.shape[0] // M
    parts, S, block, _ = kv.shape
    L = parts * block
    near, far = turn_tables(L, M)
    whole = pl.Buffered(1)
    tile = pl.BlockSpec((M, width), lambda t, slot, *_: (jnp.minimum(slot[t], own), 0))
    near_spec = pl.BlockSpec(near.shape, lambda t, *_: (0, 0), pipeline_mode=whole)
    far_spec = pl.BlockSpec(far.shape, lambda t, *_: (0, 0), pipeline_mode=whole)
    mine = pl.BlockSpec((M, width), lambda t, slot, *_: (jnp.minimum(slot[t], own - 1), 0))
    taken = pl.BlockSpec((1, 2, M, width), lambda t, slot, *_: (jnp.maximum(slot[t] - own - skip, 0), 0, 0, 0))
    anywhere = pl.BlockSpec(memory_space=pl.ANY)
    bf16, f32 = jnp.bfloat16, jnp.float32
    pairs = steps * M * H * L // 3
    kernel = functools.partial(attn_kernel, M, tk, own, before is None)
    operands, specs = [q, g], [mine, mine]
    if others is None:
        inner = kernel
        kernel = lambda a, b, c, d, q_ref, g_ref, *refs: inner(a, b, c, d, q_ref, g_ref, None, *refs)
    else:
        operands, specs = operands + [others], specs + [taken]
    operands += [near, far, kv]
    specs += [near_spec, far_spec, pl.BlockSpec(kv.shape, lambda t, *_: (0, 0, 0, 0), pipeline_mode=whole)]
    aliases = {}
    if before is not None:
        aliases = {4 + len(operands) + i: i for i in range(3)}
        operands, specs = operands + list(before), specs + [anywhere] * 3
    slots = jax.ShapeDtypeStruct(((own + 1) * M, width), bf16)
    out_shape, out_specs = [slots, slots, jax.ShapeDtypeStruct((S, 128, L), f32)], [tile, tile, anywhere]
    if others is not None:
        count = others.shape[0]
        out_shape.append(jax.ShapeDtypeStruct(others.shape, bf16))
        out_specs.append(pl.BlockSpec(
            (1, 2, M, width),
            lambda t, slot, *_: (jnp.where(slot[t] < own, count - 1, jnp.minimum(slot[t] - own - skip, count - 1)), 0, 0, 0)))
    return pl.pallas_call(
        kernel,
        grid_spec=pltpu.PrefetchScalarGridSpec(
            num_scalar_prefetch=4,
            grid=(steps,),
            in_specs=specs,
            out_specs=out_specs,
            scratch_shapes=[
                pltpu.VMEM((S, L, 128), bf16),
                pltpu.VMEM((S, L, 128), bf16),
                pltpu.VMEM((H * M, 128), bf16),
                pltpu.VMEM((H * M, 128), bf16),
                pltpu.VMEM((128, H * M), bf16),
                pltpu.VMEM((128, H * M), bf16),
                pltpu.VMEM((L // tk, H * M, tk), bf16),
                pltpu.VMEM((H * M, 128), f32),
                pltpu.VMEM((H * M, 128), f32),
                pltpu.VMEM((H * M, 128), f32),
                pltpu.VMEM((H * M, 128), f32),
                pltpu.VMEM((S, 128, L), f32),
                pltpu.SMEM((1,), f32),
                pltpu.SemaphoreType.DMA,
            ],
        ),
        out_shape=out_shape,
        input_output_aliases=aliases,
        compiler_params=pltpu.CompilerParams(vmem_limit_bytes=58 << 20),
        cost_estimate=pl.CostEstimate(flops=1 << 20, bytes_accessed=1 << 16, transcendentals=0),
        name="attention",
    )(*tables, *operands)


MESH = pl.DeviceIdType.MESH


def bits_of(n_seq, n_rows):
    high = [("seq", 1 << b) for b in reversed(range(n_seq.bit_length() - 1))]
    return high + [("rows", 1 << b) for b in reversed(range(n_rows.bit_length() - 1))]


def place(bits):
    return [lax.rem(lax.axis_index(axis) // weight, 2) for axis, weight in bits]


def partner(bit):
    axis, weight = bit
    mine = lax.axis_index(axis)
    return {axis: mine + weight - 2 * weight * lax.rem(mine // weight, 2)}


def greet(bits):
    barrier = pltpu.get_barrier_semaphore()
    for bit in bits:
        pl.semaphore_signal(barrier, inc=1, device_id=partner(bit), device_id_type=MESH)
    pl.semaphore_wait(barrier, len(bits))


def routes(bits):
    n = len(bits)
    one = list(range(n))
    other = list(range(n))
    near = max(i for i in range(n) if bits[i][0] == "seq")
    if near + 1 < n - 1:
        other[near], other[near + 1] = other[near + 1], other[near]
    return one, other


def gelu_both(x):
    z = jnp.abs(x) * 0.7071067811865476
    s = 1.0 / (1.0 + 0.3275911 * z)
    poly = s * (0.127414796 + s * (-0.142248368 + s * (0.710706871 + s * (-0.7265760135 + s * 0.5307027145))))
    bell = jnp.exp(-z * z)
    tail = poly * bell
    phi = jnp.where(x >= 0.0, 1.0 - tail, tail)
    return x * phi, phi + x * (bell * 0.3989422804014327)


def ffn_kernel(C, x_ref, b_ref, up_ref, down_ref, out_ref, dx_ref, gup_ref, gdown_ref, act_s, ug_s):
    f = pl.program_id(0)
    T = x_ref.shape[0]

    @pl.when(f == 0)
    def _():
        out_ref[...] = jnp.zeros_like(out_ref)
        dx_ref[...] = jnp.zeros_like(dx_ref)

    up = up_ref[...]
    down = down_ref[...]
    for c in range(T // C):
        r = slice(c * C, (c + 1) * C)
        u = dot(x_ref[r, :], up, 1, 0)
        a = dot(b_ref[r, :], down, 1, 1)
        act, slope = gelu_both(u)
        act = act.astype(jnp.bfloat16)
        ug = (a * slope).astype(jnp.bfloat16)
        act_s[r, :] = act
        ug_s[r, :] = ug
        out_ref[r, :] += dot(act, down, 1, 0)
        dx_ref[r, :] += dot(ug, up, 1, 1)
    gup_ref[...] = dot(x_ref[...], ug_s[...], 0, 0).astype(gup_ref.dtype)
    gdown_ref[...] = dot(act_s[...], b_ref[...], 0, 0).astype(gdown_ref.dtype)


def ffn(x, b, up, down, F=512, C=256, wire=jnp.bfloat16):
    T, D = x.shape
    FF = up.shape[1]
    C = min(C, T)
    f32, bf16 = jnp.float32, jnp.bfloat16
    whole = lambda f: (0, 0)
    return pl.pallas_call(
        functools.partial(ffn_kernel, C),
        grid=(FF // F,),
        in_specs=[
            pl.BlockSpec((T, D), whole, pipeline_mode=pl.Buffered(1)),
            pl.BlockSpec((T, D), whole, pipeline_mode=pl.Buffered(1)),
            pl.BlockSpec((D, F), lambda f: (0, f)),
            pl.BlockSpec((F, D), lambda f: (f, 0)),
        ],
        out_specs=[
            pl.BlockSpec((T, D), whole, pipeline_mode=pl.Buffered(1)),
            pl.BlockSpec((T, D), whole, pipeline_mode=pl.Buffered(1)),
            pl.BlockSpec((D, F), lambda f: (0, f)),
            pl.BlockSpec((F, D), lambda f: (f, 0)),
        ],
        out_shape=[
            jax.ShapeDtypeStruct((T, D), f32),
            jax.ShapeDtypeStruct((T, D), f32),
            jax.ShapeDtypeStruct((D, FF), wire),
            jax.ShapeDtypeStruct((FF, D), wire),
        ],
        scratch_shapes=[pltpu.VMEM((T, F), bf16), pltpu.VMEM((T, F), bf16)],
        compiler_params=pltpu.CompilerParams(vmem_limit_bytes=56 << 20),
        cost_estimate=pl.CostEstimate(flops=12 * T * D * FF, bytes_accessed=32 << 20, transcendentals=T * FF),
        name="feedforward",
    )(x, b, up, down)


def ffn_packed_kernel(
    C, bits, M, order, moved,
    x_ref, b_ref, up_ref, down_ref, kv_ref, q_ref, g_ref,
    out_ref, dx_ref, grads_ref, all_kv, others,
    act_s, ug_s, wide, ups, own_sem, kv_send, kv_recv, tile_send, tile_recv,
):
    f = pl.program_id(0)
    T, D = x_ref.shape
    groups, each, _, count, _ = up_ref.shape
    tiles = ups.shape[0]
    n = groups * each
    owned = D // n
    f32, bf16 = jnp.float32, jnp.bfloat16
    stages = len(bits)
    me = place(bits)
    block = lax.axis_index("seq")
    n_seq = len(moved)
    local = kv_ref.shape[1]

    def kv_copies(stage):
        copies = []
        for half in (0, 1):
            route = list(range(stages)) if half == 0 else [stages - 1] + list(range(stages - 1))
            at = tuple(slice(None) if i in route[:stage] else me[i] for i in range(stages))
            piece = all_kv.at[at + (slice(None), pl.ds(half * (local // 2), local // 2))]
            copies.append(pltpu.make_async_remote_copy(
                src_ref=piece, dst_ref=piece, send_sem=kv_send.at[half, stage], recv_sem=kv_recv.at[half, stage],
                device_id=partner(bits[route[stage]]), device_id_type=MESH))
        return copies

    def tile_copies(k):
        r = pl.ds(order[k] * M, M)
        return [pltpu.make_async_remote_copy(
            src_ref=ref.at[r], dst_ref=others.at[k, i], send_sem=tile_send.at[k, i], recv_sem=tile_recv.at[k, i],
            device_id={"seq": n_seq - 1 - block}, device_id_type=MESH) for i, ref in enumerate((q_ref, g_ref))]

    def among(devices):
        return functools.reduce(jnp.logical_or, [block == i for i in devices])

    @pl.when(f == 0)
    def _():
        pltpu.make_async_copy(kv_ref, all_kv.at[tuple(me)], own_sem).start()
        barrier = pltpu.get_barrier_semaphore()
        for bit in bits:
            pl.semaphore_signal(barrier, inc=1, device_id=partner(bit), device_id_type=MESH)
        pl.semaphore_signal(barrier, inc=1, device_id={"seq": n_seq - 1 - block}, device_id_type=MESH)

    end = 2 * tiles - 1
    when = [min(max(2, 2 * k + 1), end) for k in range(stages)]
    after = when[-1]

    def progress(point):
        if point == when[0]:
            pl.semaphore_wait(pltpu.get_barrier_semaphore(), stages + 1)
            pltpu.make_async_copy(kv_ref, all_kv.at[tuple(me)], own_sem).wait()
        for stage in range(stages):
            if when[stage] == point:
                for copy in kv_copies(stage - 1) if stage else []:
                    copy.wait()
                for copy in kv_copies(stage):
                    copy.start()
        if after == point:
            for k in range(len(order)):
                @pl.when(among([i for i in range(n_seq) if moved[i] > k]))
                def _(k=k):
                    for copy in tile_copies(k):
                        copy.start()

    def progress_at(parity):
        for point in sorted(set(when + [after])):
            if point % 2 == parity:
                @pl.when(f == point // 2)
                def _(point=point):
                    progress(point)

    progress_at(0)

    @pl.when(f == 0)
    def _():
        out_ref[...] = jnp.zeros_like(out_ref)
        dx_ref[...] = jnp.zeros_like(dx_ref)

        def unpack(d, _):
            part = up_ref[d // each, lax.rem(d, each), 0].astype(f32)
            for j in range(tiles):
                at = pl.ds(pl.multiple_of(d * owned, 8), owned)
                wide[j, at, :] = part[j * owned:(j + 1) * owned]
            return 0

        lax.fori_loop(0, n, unpack, 0)
        for j in range(tiles):
            ups[j] = wide[j].astype(bf16)

    up = ups[f]
    down = down_ref[...].reshape(D, D)
    for c in range(T // C):
        if c == T // C // 2:
            progress_at(1)
        r = slice(c * C, (c + 1) * C)
        u = dot(x_ref[r, :], up, 1, 0)
        a = dot(b_ref[r, :], down, 1, 1)
        act, slope = gelu_both(u)
        act = act.astype(bf16)
        ug = (a * slope).astype(bf16)
        act_s[r, :] = act
        ug_s[r, :] = ug
        out_ref[r, :] += dot(act, down, 1, 0)
        dx_ref[r, :] += dot(ug, up, 1, 1)
    wide[f] = dot(x_ref[...], ug_s[...], 0, 0)
    grad_down = dot(act_s[...], b_ref[...], 0, 0).astype(bf16)
    for k in range(each):
        at = f * each + k
        grads_ref[at, count:] = grad_down[k * count:(k + 1) * count]

    @pl.when(f == tiles - 1)
    def _():
        def pack(d, _):
            at = pl.ds(pl.multiple_of(d * owned, 8), owned)
            part = jnp.concatenate([wide[j, at, :] for j in range(tiles)], axis=0)
            grads_ref[d, :count] = part.astype(bf16)
            return 0

        lax.fori_loop(0, n, pack, 0)
        for copy in kv_copies(stages - 1):
            copy.wait()
        for k in range(len(order)):
            @pl.when(among([i for i in range(n_seq) if moved[i] > k]))
            def _(k=k):
                for copy in tile_copies(k):
                    copy.wait_send()

            @pl.when(among([n_seq - 1 - i for i in range(n_seq) if moved[i] > k]))
            def _(k=k):
                for copy in tile_copies(k):
                    copy.wait_recv()


def ffn_packed(x, b, packed, kv, q, g, order, moved, M, n_seq, collective_id, C=256):
    T, D = x.shape
    n, count = packed.shape[0], packed.shape[1] // 2
    FF = n * count
    tiles = FF // D
    each = n // tiles
    packed = packed.reshape(tiles, each, 2, count, D)
    f32, bf16 = jnp.float32, jnp.bfloat16
    once = pl.Buffered(1)
    whole = lambda f: (0, 0)
    bits = bits_of(n_seq, 1)
    anywhere = pl.BlockSpec(memory_space=pl.ANY)
    out, dx, grads, all_kv, others = pl.pallas_call(
        functools.partial(ffn_packed_kernel, C, bits, M, tuple(order), tuple(moved)),
        grid=(tiles,),
        in_specs=[
            pl.BlockSpec((T, D), whole, pipeline_mode=once),
            pl.BlockSpec((T, D), whole, pipeline_mode=once),
            pl.BlockSpec((tiles, each, 1, count, D), lambda f: (0, 0, 0, 0, 0), pipeline_mode=once),
            pl.BlockSpec((1, each, 1, count, D), lambda f: (f, 0, 1, 0, 0)),
            anywhere, anywhere, anywhere,
        ],
        out_specs=[
            pl.BlockSpec((T, D), whole, pipeline_mode=once),
            pl.BlockSpec((T, D), whole, pipeline_mode=once),
            pl.BlockSpec((n, 2 * count, D), lambda f: (0, 0, 0), pipeline_mode=once),
            anywhere, anywhere,
        ],
        out_shape=[
            jax.ShapeDtypeStruct((T, D), f32),
            jax.ShapeDtypeStruct((T, D), f32),
            jax.ShapeDtypeStruct((n, 2 * count, D), bf16),
            jax.ShapeDtypeStruct((2,) * len(bits) + kv.shape, bf16),
            jax.ShapeDtypeStruct((len(order), 2, M, D), bf16),
        ],
        scratch_shapes=[
            pltpu.VMEM((T, D), bf16), pltpu.VMEM((T, D), bf16),
            pltpu.VMEM((tiles, D, D), f32), pltpu.VMEM((tiles, D, D), bf16),
            pltpu.SemaphoreType.DMA,
            pltpu.SemaphoreType.DMA((2, len(bits))), pltpu.SemaphoreType.DMA((2, len(bits))),
            pltpu.SemaphoreType.DMA((len(order), 2)), pltpu.SemaphoreType.DMA((len(order), 2)),
        ],
        compiler_params=pltpu.CompilerParams(
            collective_id=collective_id, has_side_effects=True, vmem_limit_bytes=60 << 20),
        cost_estimate=pl.CostEstimate(flops=1 << 20, bytes_accessed=1 << 16, transcendentals=0),
        name="feedforward",
    )(x, b, packed, packed, kv, q, g)
    return out, dx, grads, all_kv.reshape((n_seq,) + kv.shape), others


def streams_of(bits, squares, hidden):
    n = len(bits)
    one, other = routes(bits)
    near = max(i for i in range(n) if bits[i][0] == "seq")
    last = [i for i in (near, near + 1) if i < n - 1]
    last += [i for i in range(n - 1) if i not in last] + [n - 1]
    early, late = list(range(n)), list(range(2, n + 2))
    split = list(range(2)) + list(range(4, n + 2))
    unit = squares // 48 * 16
    head = hidden // 12 // 16 * 16
    tail = hidden // 6 // 16 * 16
    rest = (hidden - 2 * head - tail) // 2
    return [
        (0, 0, 16, one, early), (0, 16, 16, other, early),
        (1, 0, unit, one, early), (1, unit, squares - unit, other, early),
        (2, 0, head, one, early), (2, head, head, other, early),
        (2, 2 * head, rest, one, late), (2, 2 * head + rest, rest, other, late),
        (2, 2 * head + 2 * rest, tail, last, split),
    ]


def front_kernel(
    bits, here, M, chunk, streams,
    x_ref, c_ref, weight_ref, subset_ref, ga_ref, sa_ref, gf_ref, sf_ref, near_ref, far_ref, query_ref, pair_ref, output_ref, up_ref, down_ref,
    q_ref, g_ref, kv_ref, xa_ref, xf_ref, b_ref, wide_ref, wp, hidden_ref,
    pr_all, sq_all, hidden_own, stage_q, stage_o, stage_p,
    own_sem, send_sem, recv_sem,
):
    f32, bf16 = jnp.float32, jnp.bfloat16
    T, D = x_ref.shape
    n = len(bits)
    me = place(bits)
    owned = query_ref.shape[0]
    tiles = up_ref.shape[1] // D
    rows = hidden_own.shape[0] // 2
    up = up_ref[...].astype(f32)
    hidden_own[:rows, :] = jnp.concatenate([up[:, j * D:(j + 1) * D] for j in range(tiles)], axis=0).astype(bf16)
    hidden_own[rows:, :] = down_ref[...]
    own = pltpu.make_async_copy(hidden_own, hidden_ref.at[tuple(me)], own_sem)
    own.start()
    squares = jnp.concatenate([query_ref[...].astype(f32), output_ref[...].astype(f32)], axis=0)
    sq_all[tuple(me)] = squares.astype(bf16)
    pairs = jnp.concatenate([pair_ref[...].astype(f32), jnp.zeros((pr_all.shape[-2] - owned, 128), f32)], axis=0)
    pr_all[tuple(me)] = pairs.astype(bf16)
    greet(bits)
    own.wait()

    gains = [ref[...].reshape(1, D) for ref in (ga_ref, sa_ref, gf_ref, sf_ref)]

    def normalize(i):
        r = slice(i * chunk, (i + 1) * chunk)
        x = x_ref[r, :].astype(f32)
        x = x - jnp.mean(x, axis=1, keepdims=True)
        unit = x * lax.rsqrt(jnp.mean(x * x, axis=1, keepdims=True) + 1e-05)
        xa_ref[r, :] = (unit * gains[0] + gains[1]).astype(bf16)
        xf_ref[r, :] = (unit * gains[2] + gains[3]).astype(bf16)
        part = i * chunk // (T // here)
        b_ref[r, :] = (c_ref[r, :].astype(f32) * weight_ref[subset_ref[part]]).astype(bf16)

    def unpack():
        for d in range(1 << n):
            at = tuple((d >> (n - 1 - i)) & 1 for i in range(n))
            r = slice(d * owned, (d + 1) * owned)
            both = sq_all[at].astype(f32)
            stage_q[r, :] = both[:owned]
            stage_o[r, :] = both[owned:2 * owned]
            stage_p[r, :] = pr_all[at].astype(f32)[:owned]
        wp[...] = stage_p[...].astype(bf16)
        wide_ref[0] = stage_q[...].astype(bf16)
        wide_ref[1] = stage_o[...].astype(bf16)

    block = lax.axis_index("seq")
    per = T // here // M
    tables = []
    for j in range(per):
        tables.append(turn_factors(near_ref[...], far_ref[pl.ds(block * per + j, 1), :]))
    first = lax.broadcasted_iota(jnp.int32, (M, 128), 1) < HD

    def keys(i):
        r = slice(i * chunk, (i + 1) * chunk)
        kv = dot(xa_ref[r, :], wp[...], 1, 0)
        for j in range(chunk // M):
            part = kv[j * M:(j + 1) * M]
            turned = turn(part, *tables[(i * chunk // M + j) % per])
            kv_ref[i * chunk + j * M:i * chunk + (j + 1) * M, :] = jnp.where(first, turned, part).astype(bf16)

    def queries(i):
        r = slice(i * chunk, (i + 1) * chunk)
        z = dot(xa_ref[r, :], wide_ref[0], 1, 0)
        for j in range(chunk // M):
            tab = tables[(i * chunk // M + j) % per]
            for p in range(D // 128):
                c = slice(p * 128, (p + 1) * 128)
                part = turn(z[j * M:(j + 1) * M, c], *tab) * (HD ** -0.5 / LN2)
                q_ref[i * chunk + j * M:i * chunk + (j + 1) * M, c] = part.astype(bf16)

    def gradients(i):
        r = slice(i * chunk, (i + 1) * chunk)
        g_ref[r, :] = dot(b_ref[r, :], wide_ref[1], 1, 1).astype(bf16)

    chunks = T // chunk
    rounds = max(s[4][-1] for s in streams) + 1
    jobs = [[] for _ in range(rounds)]
    for i in range(chunks):
        jobs[min(i, n - 1)].append(functools.partial(normalize, i))
    jobs[min(n, rounds - 1)] += [unpack] + [functools.partial(f, i) for f in (keys, queries, gradients) for i in range(chunks)]
    arrays = (pr_all, sq_all, hidden_ref)
    held = [set() for _ in streams]
    for now in range(rounds):
        copies = []
        for i, (a, start, size, order, when) in enumerate(streams):
            if now not in when:
                continue
            stage = when.index(now)
            where = tuple(slice(None) if b in held[i] else me[b] for b in range(n))
            piece = arrays[a].at[where + (pl.ds(start, size),)]
            copy = pltpu.make_async_remote_copy(
                src_ref=piece, dst_ref=piece, send_sem=send_sem.at[i, stage], recv_sem=recv_sem.at[i, stage],
                device_id=partner(bits[order[stage]]), device_id_type=MESH)
            copy.start()
            copies.append(copy)
            held[i].add(order[stage])
        for job in jobs[now]:
            job()
        for copy in copies:
            copy.wait()


def front(x, c, weights, subsets, norms, query, pair, output, up, down, here, length, M, n_seq, n_rows, collective_id, chunk=256):
    bits = bits_of(n_seq, n_rows)
    n = len(bits)
    T, D = x.shape
    owned, hidden = query.shape[0], 2 * down.shape[0]
    f32, bf16 = jnp.float32, jnp.bfloat16
    near, far = turn_tables(length, M)
    vmem = pl.BlockSpec(memory_space=pltpu.VMEM)
    smem = pl.BlockSpec(memory_space=pltpu.SMEM)
    token = jax.ShapeDtypeStruct((T, D), bf16)
    streams = streams_of(bits, 2 * owned, hidden)
    q, g, kv, xa, xf, b, wide, wp, packed = pl.pallas_call(
        functools.partial(front_kernel, bits, here, M, chunk, streams),
        out_shape=[token, token, jax.ShapeDtypeStruct((T, 128), bf16), token, token, token,
                   jax.ShapeDtypeStruct((2, D, D), bf16), jax.ShapeDtypeStruct((D, 128), bf16),
                   jax.ShapeDtypeStruct((2,) * n + (hidden, D), bf16)],
        in_specs=[vmem] * 2 + [smem] * 2 + [vmem] * 11,
        out_specs=[vmem] * 8 + [pl.BlockSpec(memory_space=pl.ANY)],
        scratch_shapes=[
            pltpu.VMEM((2,) * n + (32, 128), bf16),
            pltpu.VMEM((2,) * n + (2 * owned, D), bf16),
            pltpu.VMEM((hidden, D), bf16),
            pltpu.VMEM((D, D), f32),
            pltpu.VMEM((D, D), f32),
            pltpu.VMEM((D, 128), f32),
            pltpu.SemaphoreType.DMA,
            pltpu.SemaphoreType.DMA((len(streams), n)),
            pltpu.SemaphoreType.DMA((len(streams), n)),
        ],
        compiler_params=pltpu.CompilerParams(
            collective_id=collective_id, has_side_effects=True, vmem_limit_bytes=56 << 20),
        name="front",
    )(x, c, weights, subsets, *norms, near, far, query, pair, output, up, down)
    return q, g, kv, xa, xf, b, wide, wp, packed.reshape(1 << n, hidden, D)


class Halving:
    def __init__(self, bits, order, me, first, send, recv, acc, send_sem, recv_sem):
        self.bits, self.order, self.me, self.first = bits, order, me, first
        self.send, self.recv, self.acc = send, recv, acc
        self.send_sem, self.recv_sem = send_sem, recv_sem
        self.copy = None

    def spot(self, stage, j, own):
        left = sorted(self.order[stage:])
        b = self.order[stage]
        rest = [i for i in left if i != b]
        index = 0
        for i in left:
            if i == b:
                bit = self.me[b] if own else 1 - self.me[b]
            else:
                bit = lax.rem(j // (1 << (len(rest) - 1 - rest.index(i))), 2)
            index = index * 2 + bit
        return index

    def block(self, stage, at):
        return self.first(at) if stage == 0 else self.acc[stage - 1][at]

    def start(self, stage):
        def fill(j, _):
            self.send[stage][j] = self.block(stage, self.spot(stage, j, False)).astype(jnp.bfloat16)
            return 0

        lax.fori_loop(0, 1 << (len(self.order) - 1 - stage), fill, 0)
        self.copy = pltpu.make_async_remote_copy(
            src_ref=self.send[stage], dst_ref=self.recv[stage],
            send_sem=self.send_sem.at[stage], recv_sem=self.recv_sem.at[stage],
            device_id=partner(self.bits[self.order[stage]]), device_id_type=MESH)
        self.copy.start()

    def finish(self, stage):
        self.copy.wait()

        def add(j, _):
            own = self.block(stage, self.spot(stage, j, True))
            self.acc[stage][j] = own + self.recv[stage][j].astype(jnp.float32)
            return 0

        lax.fori_loop(0, 1 << (len(self.order) - 1 - stage), add, 0)


def halving_shapes(stages, rows, columns):
    sizes = [(1 << (stages - 1 - s), rows, columns) for s in range(stages)]
    half = [pltpu.VMEM(s, jnp.bfloat16) for s in sizes]
    return half + half + [pltpu.VMEM(s, jnp.float32) for s in sizes] + [
        pltpu.SemaphoreType.DMA((stages,)), pltpu.SemaphoreType.DMA((stages,))]


def post_kernel(bits, here, M, order, moved, counts, chunk, *refs):
    (sums_ref, o_hbm, dq_hbm, *refs) = refs
    backs, refs = refs[:len(counts)], refs[len(counts):]
    backs = [ref.at[k] for ref, count in zip(backs, counts) for k in range(count)]
    (xa_ref, b_ref, x_hbm, c_hbm, out_hbm, dx_hbm, wide_ref, wp_ref, ga_ref, gf_ref, weight_ref, subset_ref, near_ref, far_ref,
     layer_ref, states_ref, square_ref, small_ref, *refs) = refs
    f32, bf16 = jnp.float32, jnp.bfloat16
    T, D = xa_ref.shape
    n = len(bits)
    seq_bits = [i for i in range(n) if bits[i][0] == "seq"]
    n_s = len(seq_bits)
    me = place(bits)
    o_ref, dq_ref, x_ref, c_ref, out_ref, dx_ref, ai_ref, gq, go, gs, inv_ref, load_sem, *refs = refs

    def take(stages):
        nonlocal refs
        mine, refs = refs[:3 * stages + 2], refs[3 * stages + 2:]
        return mine[:stages], mine[stages:2 * stages], mine[2 * stages:3 * stages], mine[-2], mine[-1]

    loads = [pltpu.make_async_copy(s, d, load_sem.at[i])
             for i, (s, d) in enumerate((
                 (dq_hbm.at[:T], dq_ref), (o_hbm.at[:T], o_ref), (out_hbm, out_ref),
                 (x_hbm, x_ref), (dx_hbm, dx_ref), (c_hbm, c_ref)))]
    for load in loads:
        load.start()
    greet(bits)

    owned = D >> n
    local = T // here
    per = local // M
    wide = sums_ref.shape[2] >> n_s

    def keys_first(s):
        return lambda at: sums_ref[s, :, pl.ds(pl.multiple_of(at * wide, 128), wide)]

    def square_first(ref):
        def get(at):
            r = pl.ds(pl.multiple_of(at * owned, 8), owned)
            return jnp.concatenate([ref[r, :D // 2], ref[r, D // 2:]], axis=0)
        return get

    def small_first(at):
        r = pl.ds(pl.multiple_of(at * owned, 8), owned)
        return jnp.concatenate([gs[r, :128], gs[r, 128:]], axis=0)

    x_first = seq_bits[::-1]
    z_first = x_first[1:] + x_first[:1]
    kv = [Halving(bits, z_first if s % 2 else x_first, me, keys_first(s), *take(n_s)) for s in range(here)]
    routes_back = [list(reversed(o)) for o in routes(bits)]
    squares = [Halving(bits, routes_back[i], me, square_first(ref), *take(n)) for i, ref in enumerate((gq, go))]
    small = Halving(bits, routes_back[0], me, small_first, *take(n))

    for h in kv:
        h.start(0)

    block = lax.axis_index("seq")
    loads[0].wait()
    loads[1].wait()
    for k, at in enumerate(order):
        r = slice(at * M, (at + 1) * M)
        away = functools.reduce(jnp.logical_or, [block == i for i in range(len(moved)) if moved[i] > k])
        o_ref[r, :] = jnp.where(away, backs[k][0], o_ref[r, :])
        dq_ref[r, :] = jnp.where(away, backs[k][1], dq_ref[r, :])

    gq[...] = dot(xa_ref[...], dq_ref[...], 0, 0)
    squares[0].start(0)
    go[...] = dot(o_ref[...], b_ref[...], 0, 0)
    squares[1].start(0)
    chunks = T // chunk

    def backward(i):
        r = slice(i * chunk, (i + 1) * chunk)
        ai_ref[r, :] = dot(dq_ref[r, :], wide_ref[0], 1, 1)

    def forward(i):
        r = slice(i * chunk, (i + 1) * chunk)
        total = x_ref[r, :].astype(f32) + (dot(o_ref[r, :], wide_ref[1], 1, 0) + out_ref[r, :])
        layer_ref[r, :] = total.astype(bf16)

    totals = [jnp.zeros((1, D), f32) for _ in range(4)]

    def hidden(i):
        r = slice(i * chunk, (i + 1) * chunk)
        x = x_ref[r, :].astype(f32)
        x = x - jnp.mean(x, axis=1, keepdims=True)
        inverse = lax.rsqrt(jnp.mean(x * x, axis=1, keepdims=True) + 1e-05)
        unit = x * inverse
        fi = dx_ref[r, :]
        totals[2] = totals[2] + jnp.sum(fi * unit, axis=0, keepdims=True)
        totals[3] = totals[3] + jnp.sum(fi, axis=0, keepdims=True)
        dx_ref[r, :] = fi * gf_ref[...].reshape(1, D)
        out_ref[r, :] = unit
        inv_ref[r, :] = inverse

    moved_on = [0]

    def advance():
        stage = moved_on[0]
        moved_on[0] += 1
        for h in squares:
            h.finish(stage)
            if stage + 1 < n:
                h.start(stage + 1)

    for i in range(chunks):
        backward(i)
    advance()
    for load in loads[2:5]:
        load.wait()
    for i in range(chunks):
        forward(i)
        hidden(i)
    for stage in range(n_s):
        for h in kv:
            h.finish(stage)
            if stage + 1 < n_s:
                h.start(stage + 1)
        if moved_on[0] < n - 1:
            advance()

    first = lax.broadcasted_iota(jnp.int32, (M, 128), 1) < HD
    grads = []
    for s in range(here):
        home = kv[s].acc[n_s - 1][0].T
        for j in range(per):
            factors = turn_factors(near_ref[...], far_ref[pl.ds(block * per + j, 1), :])
            part = home[j * M:(j + 1) * M]
            turned = turn_back(part, *factors) * LN2
            grads.append(jnp.where(first, turned, part).astype(bf16))
    pairs = jnp.concatenate(grads, axis=0)
    gs[:, :128] = dot(xa_ref[...], pairs, 0, 0)
    loads[5].wait()
    for i in range(chunks):
        r = slice(i * chunk, (i + 1) * chunk)
        unit = out_ref[r, :]
        ai = ai_ref[r, :] + dot(pairs[r], wp_ref[...], 1, 1)
        totals[0] = totals[0] + jnp.sum(ai * unit, axis=0, keepdims=True)
        totals[1] = totals[1] + jnp.sum(ai, axis=0, keepdims=True)
        both = ai * ga_ref[...].reshape(1, D) + dx_ref[r, :]
        middle = jnp.mean(both, axis=1, keepdims=True)
        slope = jnp.mean(both * unit, axis=1, keepdims=True)
        up = c_ref[r, :].astype(f32) * weight_ref[subset_ref[i * chunk // local]]
        states_ref[r, :] = (up + inv_ref[r, :] * (both - middle - unit * slope)).astype(bf16)
    rows = jnp.concatenate(totals + [jnp.zeros((124, D), f32)], axis=0)
    gs[:, 128:] = rows.T
    small.start(0)
    while moved_on[0] < n:
        advance()
    for i, h in enumerate(squares):
        total = h.acc[n - 1][0]
        square_ref[i, :, :D // 2] = total[:owned]
        square_ref[i, :, D // 2:] = total[owned:]
    for stage in range(n):
        small.finish(stage)
        if stage + 1 < n:
            small.start(stage + 1)
    total = small.acc[n - 1][0]
    small_ref[:, :128] = total[:owned]
    small_ref[:, 128:] = total[owned:]


def post(sums, o, dq, backs, order, moved, xa, b, x, c, out, dx, wide, wp, norms, weights, subsets,
         here, length, M, n_seq, n_rows, collective_id, chunk=256):
    bits = bits_of(n_seq, n_rows)
    n, n_s = len(bits), n_seq.bit_length() - 1
    T, D = xa.shape
    owned = D >> n
    f32, bf16 = jnp.float32, jnp.bfloat16
    near, far = turn_tables(length, M)
    vmem, anywhere = pl.BlockSpec(memory_space=pltpu.VMEM), pl.BlockSpec(memory_space=pl.ANY)
    smem = pl.BlockSpec(memory_space=pltpu.SMEM)
    token = jax.ShapeDtypeStruct((T, D), bf16)
    scratch = [
        *[pltpu.VMEM((T, D), bf16)] * 4, *[pltpu.VMEM((T, D), f32)] * 3,
        pltpu.VMEM((D, D), f32), pltpu.VMEM((D, D), f32), pltpu.VMEM((D, 256), f32),
        pltpu.VMEM((T, 1), f32), pltpu.SemaphoreType.DMA((6,)),
    ]
    for _ in range(here):
        scratch += halving_shapes(n_s, 128, length // n_seq)
    for _ in range(2):
        scratch += halving_shapes(n, 2 * owned, D // 2)
    scratch += halving_shapes(n, 2 * owned, 128)
    return pl.pallas_call(
        functools.partial(post_kernel, bits, here, M, tuple(order), tuple(moved), tuple(b.shape[0] for b in backs), chunk),
        out_shape=[token, token, jax.ShapeDtypeStruct((2, owned, D), f32), jax.ShapeDtypeStruct((owned, 256), f32)],
        in_specs=[vmem, anywhere, anywhere] + [vmem] * len(backs) + [vmem] * 2 + [anywhere] * 4 + [vmem] * 4 + [smem] * 2 + [vmem] * 2,
        out_specs=[vmem] * 4,
        scratch_shapes=scratch,
        compiler_params=pltpu.CompilerParams(
            collective_id=collective_id, has_side_effects=True, vmem_limit_bytes=60 << 20),
        name="post",
    )(sums, o, dq, *backs, xa, b, x, c, out, dx, wide, wp, norms[0], norms[2], weights, subsets, near, far)


def layer_norm(values):
    center = values - jnp.mean(values, axis=-1, keepdims=True)
    inverse = lax.rsqrt(jnp.mean(center * center, axis=-1, keepdims=True) + 1e-05)
    return center * inverse, inverse


def norm_back(incoming, normed, inverse, gain):
    scaled = incoming * gain
    return inverse * (
        scaled
        - jnp.mean(scaled, axis=-1, keepdims=True)
        - normed * jnp.mean(scaled * normed, axis=-1, keepdims=True)
    )


def rotary_tables(positions):
    half_rot = ROT // 2
    frequency = 10000.0 ** (-2.0 * jnp.arange(half_rot, dtype=jnp.float32) / ROT)
    angles = positions[:, None] * frequency[None, :]
    cosine = jnp.concatenate([jnp.cos(angles), jnp.cos(angles)], axis=-1)
    sine_vals = jnp.concatenate([jnp.sin(angles), jnp.sin(angles)], axis=-1)
    return (cosine, sine_vals)


def rotate(vector, cosine, sine_vals):
    half_rot = ROT // 2
    rotary_part = vector[..., :ROT]
    turned = jnp.concatenate([-rotary_part[..., half_rot:], rotary_part[..., :half_rot]], axis=-1)
    return jnp.concatenate([rotary_part * cosine + turned * sine_vals, vector[..., ROT:]], axis=-1)


def plan(n, here, per, M, tk):
    order = [(s, j) for j in reversed(range(per)) for s in range(here)]
    row = lambda i, j: (i * per + j) * M
    price = lambda first: first // tk + (0.5 if first % tk + M <= tk // 2 else 1.0) + 1.1
    moved = [0] * n
    for i in range(n // 2, n):
        load = lambda k: max(
            sum(price(row(i, j)) for _, j in order[k:]),
            sum(price(row(n - 1 - i, j)) for _, j in order) + sum(price(row(i, j)) for _, j in order[:k]))
        moved[i] = min(range(len(order)), key=load)
    most = max(moved)
    takes = [[(here * per + k, s, row(n - 1 - i, j)) for k, (s, j) in enumerate(order[:moved[n - 1 - i]])] if i < n // 2 else []
             for i in range(n)]
    keeps = [[(s * per + j, s, row(i, j)) for s, j in order[moved[i]:]] for i in range(n)]
    cost = lambda steps: sum(price(x[2]) for x in steps)
    mean = sum(cost(t) + cost(k) for t, k in zip(takes, keeps)) / n
    lists = ([], [], [])
    for take, keep in zip(takes, keeps):
        ahead, between = (0.32, 0.42) if take else (0.24, 0.40)
        keep, head, middle = list(keep), list(take[:1]), list(take[1:])
        while len(keep) > 1 and cost(head) + price(keep[0][2]) / 2 < ahead * mean:
            head.append(keep.pop(0))
        while len(keep) > 1 and cost(middle) + price(keep[0][2]) / 2 < between * mean and cost(keep) > 0.24 * mean:
            middle.append(keep.pop(0))
        for part, steps in zip(lists, (head, middle, keep)):
            part.append(steps)
    tables = []
    for part in lists:
        size = max(1, max(len(w) for w in part))
        full = [[x + (1,) for x in w] + [(w[-1] if w else (0, 0, 0)) + (0,)] * (size - len(w)) for w in part]
        tables.append(np.array(full, np.int32))
    return order, moved, most, tables


def local(
    mesh, states, cotangent, subsets, subset_weight, gain_attn, shift_attn, gain_ffn, shift_ffn,
    query_projection, pair_projection, output_projection, up_projection, down_projection,
):
    f32, bf16 = jnp.float32, jnp.bfloat16
    both = ("seq", "rows")
    here, length_here, D = states.shape
    T = here * length_here
    n_seq, n_rows = mesh.shape["seq"], mesh.shape["rows"]
    n = n_seq * n_rows
    length = length_here * n_seq
    block = lax.axis_index("seq")
    offset = block * length_here
    M = min(128, length_here)
    per = length_here // M
    tk = min(512, length)
    FF = up_projection.shape[1]
    P = 2 * HD
    scale = HD ** -0.5
    own_rows = query_projection.shape[0]
    aligned = own_rows % 8 == 0 and here % 2 == 0

    rows_here = offset + jnp.arange(length_here, dtype=jnp.int32)
    cosine, sine_vals = rotary_tables(rows_here.astype(f32))
    if aligned:
        norms = (gain_attn, shift_attn, gain_ffn, shift_ffn)
        queries, out_grad, own_kv, attention_input, feedforward_input, branch_grad, wide, full_pair, packed = front(
            states.reshape(T, D), cotangent.reshape(T, D), subset_weight, subsets, norms, query_projection, pair_projection,
            output_projection, up_projection, down_projection, here, length, M, n_seq, n_rows, 1)
    else:
        table_rows = jnp.arange(subset_weight.shape[0], dtype=jnp.int32)
        row_scale = jnp.sum(
            jnp.where(table_rows[None, :] == subsets[:, None], subset_weight[None, :], 0.0), axis=1
        )
        source = states.astype(f32).reshape(T, D)
        unit, inverse = layer_norm(source)
        upstream = (cotangent.astype(f32) * row_scale[:, None, None]).reshape(T, D)
        big = jnp.stack([up_projection, down_projection.reshape(up_projection.shape)])
        big = lax.all_gather(big, both, axis=1, tiled=True)
        full_up, full_down = big[0], big[1].reshape(FF, D)
        small = jnp.concatenate([query_projection, pair_projection, output_projection], axis=1)
        small = lax.all_gather(small, both, axis=0, tiled=True)
        full_query, full_pair, full_output = small[:, :D], small[:, D:D + P], small[:, D + P:]
        attention_input = (unit * gain_attn + shift_attn).astype(bf16)
        feedforward_input = (unit * gain_ffn + shift_ffn).astype(bf16)
        branch_grad = upstream.astype(bf16)
        pair_pre = jnp.dot(attention_input, full_pair, preferred_element_type=f32)
        pair_pre = pair_pre.reshape(here, length_here, P)
        key_values = jnp.concatenate(
            [rotate(pair_pre[..., :HD], cosine[None], sine_vals[None]), pair_pre[..., HD:]], axis=2
        ).astype(bf16)
        query_pre = jnp.dot(attention_input, full_query, preferred_element_type=f32)
        queries = rotate(
            query_pre.reshape(here, length_here, H, HD) * (scale / LN2),
            cosine[None, :, None, :], sine_vals[None, :, None, :],
        ).astype(bf16).reshape(T, D)
        out_grad = lax.dot_general(
            branch_grad, full_output, (((1,), (1,)), ((), ())), preferred_element_type=f32
        ).astype(bf16)
        all_kv = lax.all_gather(key_values, "seq", axis=0)

    order, moved, most, tables = plan(n_seq, here, per, M, tk)
    own = here * per
    at_slots = [s * per + j for s, j in order[:most]]
    steps = []
    for table in tables:
        mine = jnp.asarray(table)[block]
        steps.append(tuple(mine[:, c] for c in range(4)))
    q_tiles, g_tiles = queries.reshape(own, M, D), out_grad.reshape(own, M, D)

    def send(tiles):
        pairs_of = [(i, n_seq - 1 - i) for i in range(n_seq) if moved[i] > tiles[0]]
        return lax.ppermute(
            jnp.stack([jnp.stack([q_tiles[at_slots[k]], g_tiles[at_slots[k]]]) for k in tiles]), "seq", pairs_of)

    def send_back(given, first):
        return lax.ppermute(given, "seq", [(n_seq - 1 - i, i) for i in range(n_seq) if moved[i] > first])

    if aligned:
        ffn_out, ffn_input_grad, ffn_grads, all_kv, first_taken = ffn_packed(
            feedforward_input, branch_grad, packed, own_kv.reshape(here, length_here, P), queries, out_grad,
            at_slots[:1], moved, M, n_seq, 3)
    else:
        first_taken = send([0])
        ffn_out, ffn_input_grad, grad_up, grad_down = ffn(feedforward_input, branch_grad, full_up, full_down)
        ffn_grads = jnp.concatenate([grad_up.reshape(n, -1, D), grad_down.reshape(n, -1, D)], axis=1)
    ffn_grads = lax.psum_scatter(ffn_grads, both, scatter_dimension=0, tiled=True)[0]
    *done, given = attention(steps[0], queries, out_grad, first_taken, 0, all_kv, M, tk)
    backs = [send_back(given, 0)]
    if most > 1:
        *done, given = attention(
            steps[1], queries, out_grad, send(list(range(1, most))), 1, all_kv, M, tk, done)
        backs.append(send_back(given, 1))
    else:
        done = attention(steps[1], queries, out_grad, None, 0, all_kv, M, tk, done)
    half = ffn_grads.shape[0] // 2
    final_up = ffn_grads[:half]
    if aligned:
        final_up = jnp.swapaxes(final_up.reshape(FF // D, own_rows, D), 0, 1)
    final_up = final_up.reshape(-1, FF).astype(f32)
    final_down = ffn_grads[half:].astype(f32)
    attended, query_pre_grad, pair_terms = attention(steps[2], queries, out_grad, None, 0, all_kv, M, tk, done)
    if aligned:
        layer_out, grad_states, squares, small = post(
            pair_terms, attended, query_pre_grad, backs, at_slots, moved, attention_input, branch_grad,
            states.reshape(T, D), cotangent.reshape(T, D), ffn_out, ffn_input_grad, wide, full_pair, norms, subset_weight, subsets,
            here, length, M, n_seq, n_rows, 2)
        vectors = small[:, P:]
        return (
            layer_out.reshape(states.shape), grad_states.reshape(states.shape),
            vectors[:, 0], vectors[:, 1], vectors[:, 2], vectors[:, 3],
            squares[0], small[:, :P], squares[1], final_up, final_down,
        )

    a_own, d_own = list(attended.reshape(-1, M, D)[:own]), list(query_pre_grad.reshape(-1, M, D)[:own])
    count = jnp.asarray(np.array(moved, np.int32))[block]
    for k, back in enumerate(tile for part in backs for tile in part):
        a_own[at_slots[k]] = jnp.where(count > k, back[0], a_own[at_slots[k]])
        d_own[at_slots[k]] = jnp.where(count > k, back[1], d_own[at_slots[k]])
    attended, query_pre_grad = jnp.concatenate(a_own), jnp.concatenate(d_own)

    pair_terms = pair_terms.astype(bf16).reshape(here, P, n_seq, length_here)
    pair_terms = jnp.moveaxis(pair_terms, 2, 0)
    arrived = lax.all_to_all(pair_terms, "seq", split_axis=0, concat_axis=0, tiled=True)
    pair_grad = jnp.swapaxes(arrived.astype(f32).sum(axis=0), 1, 2)

    residual = jnp.dot(attended, full_output, preferred_element_type=f32) + ffn_out
    layer_out = (source + residual).astype(bf16).reshape(here, length_here, D)
    grad_output = lax.dot_general(
        attended, branch_grad, (((0,), (0,)), ((), ())), preferred_element_type=f32)
    grad_query = lax.dot_general(
        attention_input, query_pre_grad, (((0,), (0,)), ((), ())), preferred_element_type=f32)
    attn_input_grad = lax.dot_general(
        query_pre_grad, full_query, (((1,), (1,)), ((), ())), preferred_element_type=f32)

    pair_pre_grad = jnp.concatenate(
        [rotate(pair_grad[..., :HD] * LN2, cosine[None], -sine_vals[None]), pair_grad[..., HD:]], axis=2
    ).reshape(T, P).astype(bf16)
    grad_pair = lax.dot_general(
        attention_input, pair_pre_grad, (((0,), (0,)), ((), ())), preferred_element_type=f32)
    attn_input_grad = attn_input_grad + lax.dot_general(
        pair_pre_grad, full_pair, (((1,), (1,)), ((), ())), preferred_element_type=f32)

    sums = jnp.stack([
        jnp.sum(attn_input_grad * unit, axis=0), jnp.sum(attn_input_grad, axis=0),
        jnp.sum(ffn_input_grad * unit, axis=0), jnp.sum(ffn_input_grad, axis=0)], axis=1)
    grad_states = upstream + norm_back(attn_input_grad, unit, inverse, gain_attn)
    grad_states = grad_states + norm_back(ffn_input_grad, unit, inverse, gain_ffn)
    grad_states = grad_states.astype(bf16).reshape(here, length_here, D)

    last = jnp.concatenate([grad_query, grad_pair, jnp.pad(sums, ((0, 0), (0, 124))), grad_output], axis=1)
    last = lax.psum_scatter(last.astype(bf16), both, scatter_dimension=0, tiled=True).astype(f32)
    vectors = last[:, D + P:]
    at = D + P + 128
    return (
        layer_out, grad_states,
        vectors[:, 0], vectors[:, 1], vectors[:, 2], vectors[:, 3],
        last[:, :D], last[:, D:D + P], last[:, at:at + D], final_up, final_down,
    )


def solution(mesh):
    from jax.sharding import PartitionSpec as P

    blocks, owned = P("rows", "seq", None), P(("seq", "rows"), None)
    vector = P(("seq", "rows"))
    return jax.shard_map(
        functools.partial(local, mesh),
        mesh=mesh,
        in_specs=(blocks, blocks, P("rows"), P(), P(), P(), P(), P()) + (owned,) * 5,
        out_specs=(blocks, blocks) + (vector,) * 4 + (owned,) * 5,
        check_vma=False,
    )
```

```python
import functools
import jax
import jax.numpy as jnp
import numpy as np
from jax import lax
from jax.experimental import pallas as pl
from jax.experimental.pallas import tpu as pltpu

H = 12
HD = 64
LN2 = 0.6931471805599453


def dot(a, b, ca, cb):
    return lax.dot_general(a, b, (((ca,), (cb,)), ((), ())), preferred_element_type=jnp.float32)


def three_parts(x):
    hi = x.astype(jnp.bfloat16)
    rest = x - hi.astype(jnp.float32)
    mid = rest.astype(jnp.bfloat16)
    low = (rest - mid.astype(jnp.float32)).astype(jnp.bfloat16)
    return hi, mid, low


ROT = 16


def turn_tables(length, M):
    frequency = 10000.0 ** (-2.0 * np.arange(ROT // 2) / ROT)
    lanes = np.zeros(HD)
    lanes[:ROT] = np.concatenate([frequency, frequency])
    lanes = np.concatenate([lanes, lanes])

    def table(places):
        angles = places[:, None] * lanes[None, :]
        return np.concatenate([np.cos(angles), np.sin(angles)], axis=1).astype(np.float32)

    return table(np.arange(M)), table(np.arange(0, length, M))


def turn_factors(near, far):
    cn, sn, cf, sf = near[:, :128], near[:, 128:], far[:, :128], far[:, 128:]
    sine = sf * cn + cf * sn
    lane = lax.broadcasted_iota(jnp.int32, sine.shape, 1) & (HD - 1)
    low = jnp.where(lane < ROT // 2, sine, 0.0)
    high = jnp.where((lane >= ROT // 2) & (lane < ROT), sine, 0.0)
    return cf * cn - sf * sn, low, high


def turn(z, cosine, low, high):
    return z * cosine - pltpu.roll(z, 120, 1) * low + pltpu.roll(z, 8, 1) * high


def turn_back(z, cosine, low, high):
    return z * cosine + pltpu.roll(z, 120, 1) * low - pltpu.roll(z, 8, 1) * high


def attn_kernel(
    M, tk, own, first_call,
    slot_ref, seq_ref, row_ref, on_ref,
    q_ref, g_ref, other_ref, near_ref, far_ref, kv_ref, *refs,
):
    if not first_call:
        before_ref, refs = refs[2], refs[3:]
    o_ref, dq_ref, sums_ref, *refs = refs
    given_ref = None
    if other_ref is not None:
        given_ref, *refs = refs
    ka, va, qs, gs, qt, gt, stash, oacc, dqacc, top, delta, dkv_ref, limit, sum_sem = refs
    t = pl.program_id(0)
    seq = seq_ref[t]
    row0 = row_ref[t]
    G = 4 * M
    groups = [slice(g * G, (g + 1) * G) for g in range(H // 4)]
    heads = [slice(h * M, (h + 1) * M) for h in range(H)]
    f32, bf16 = jnp.float32, jnp.bfloat16
    parts_, count, block, _ = kv_ref.shape

    row_head = lax.broadcasted_iota(jnp.int32, (128, 128), 0) // HD
    spread = (row_head == lax.broadcasted_iota(jnp.int32, (128, 128), 1) // HD).astype(bf16)
    only_keys = (row_head == 0).astype(bf16)

    @pl.when(t == 0)
    def _():
        if first_call:
            dkv_ref[...] = jnp.zeros_like(dkv_ref)
        else:
            pltpu.make_async_copy(before_ref, dkv_ref, sum_sem).start()
        lower = lax.broadcasted_iota(jnp.int32, (block, 128), 1) < HD
        one = jnp.ones((block, 128), bf16)

        def arrange(i, most):
            for s in range(count):
                kv = kv_ref[i, s]
                rows = pl.ds(pl.multiple_of(i * block, block), block)
                ka[s, rows, :] = jnp.where(lower, kv, one)
                va[s, rows, :] = jnp.where(lower, one, kv)
                most = jnp.maximum(most, dot(kv * kv, only_keys, 1, 0))
            return most

        limit[0] = jnp.max(lax.fori_loop(0, parts_, arrange, jnp.zeros((block, 128), f32)))

    @pl.when(on_ref[t] != 0)
    def _():
        taken = slot_ref[t] >= own
        q_in = q_ref[...] if other_ref is None else jnp.where(taken, other_ref[0, 0], q_ref[...])
        g_in = g_ref[...] if other_ref is None else jnp.where(taken, other_ref[0, 1], g_ref[...])
        lane = lax.broadcasted_iota(jnp.int32, (M, 128), 1)
        low_half = lane < HD
        most = jnp.zeros((M, 128), f32)
        for p in range(H // 2):
            pair = q_in[:, p * 128:(p + 1) * 128]
            most = jnp.maximum(most, dot(pair * pair, spread, 1, 0))
            pair = pair.astype(f32)
            qs[heads[2 * p], :] = jnp.where(low_half, pair, 0.0).astype(bf16)
            qs[heads[2 * p + 1], :] = jnp.where(low_half, pltpu.roll(pair, HD, 1), 0.0).astype(bf16)
        oacc[...] = jnp.zeros_like(oacc)
        dqacc[...] = jnp.zeros_like(dqacc)
        n_full = row0 // tk

        def keys(ref, kt, size=tk):
            return ref[seq, pl.ds(pl.multiple_of(kt * tk, tk), size), :]

        def allowed(kt, size):
            row = row0 + (lax.broadcasted_iota(jnp.int32, (G, size), 0) & (M - 1))
            col = kt * tk + lax.broadcasted_iota(jnp.int32, (G, size), 1)
            return col <= row

        def scores(kt, r, masked, size=tk):
            s = dot(qs[r, :], keys(ka, kt, size), 1, 1)
            if masked:
                s = jnp.where(allowed(kt, size), s, -1e30)
            return s

        short = row0 + M - n_full * tk <= tk // 2

        def last(step):
            @pl.when(short)
            def _():
                step(tk // 2)

            @pl.when(jnp.logical_not(short))
            def _():
                step(tk)

        @pl.when(jnp.max(most) * limit[0] > 3600.0)
        def _():
            top[...] = jnp.full_like(top, -1e30)

            def peak(kt, masked):
                for r in groups:
                    s = scores(kt, r, masked)
                    part = s[:, :128]
                    for j in range(1, tk // 128):
                        part = jnp.maximum(part, s[:, j * 128:(j + 1) * 128])
                    top[r, :] = jnp.maximum(top[r, :], part)

            lax.fori_loop(0, n_full, lambda kt, _: (peak(kt, False), 0)[1], 0)
            peak(n_full, True)
            for r in heads:
                best = -jnp.max(top[r, :], axis=1, keepdims=True)
                for j, part in enumerate(three_parts(best)):
                    qs[r, HD + j:HD + j + 1] = part

        def first(kt, masked, size=tk):
            v = keys(va, kt, size)
            for r in groups:
                e = jnp.exp2(scores(kt, r, masked, size)).astype(bf16)
                stash[kt, r, :size] = e
                oacc[r, :] += dot(e, v, 1, 0)

        lax.fori_loop(0, n_full, lambda kt, _: (first(kt, False), 0)[1], 0)
        last(lambda size: first(n_full, True, size))

        ones = jnp.ones((3 * 128, 128), bf16)
        for p in range(H // 2):
            grads = g_in[:, p * 128:(p + 1) * 128].astype(f32)
            outs = []
            for h in (2 * p, 2 * p + 1):
                r = heads[h]
                acc = oacc[r, :]
                inverse = pltpu.roll(1.0 / acc, HD, 1)
                out = acc * inverse
                outs.append(out)
                grad = grads if h % 2 == 1 else pltpu.roll(grads, HD, 1)
                low = jnp.where(low_half, 0.0, grad * inverse).astype(bf16).astype(f32)
                delta[r, :] = dot(jnp.concatenate(three_parts(low * out), axis=1), ones, 1, 0)
                gs[r, :] = low.astype(bf16)
            out = jnp.where(low_half, pltpu.roll(outs[0], HD, 1), outs[1]).astype(bf16)
            o_ref[:, p * 128:(p + 1) * 128] = out
            if given_ref is not None:
                @pl.when(taken)
                def _(p=p, out=out):
                    given_ref[0, 0, :, p * 128:(p + 1) * 128] = out
        qt[...] = qs[...].T
        gt[...] = gs[...].T

        if not first_call:
            @pl.when(t == 0)
            def _():
                pltpu.make_async_copy(before_ref, dkv_ref, sum_sem).wait()

        def second(kt, size=tk):
            k = keys(ka, kt, size)
            v = keys(va, kt, size)
            dk = jnp.zeros((HD, size), f32)
            dv = jnp.zeros((HD, size), f32)
            for r in groups:
                e = stash[kt, r, :size]
                slope = e.astype(f32) * (dot(gs[r, :], v, 1, 1) - jnp.tile(delta[r, :], (1, size // 128)))
                slope = slope.astype(bf16)
                dqacc[r, :] += dot(slope, k, 1, 0)
                dk = dk + dot(qt[:HD, r], slope, 1, 0)
                dv = dv + dot(gt[HD:, r], e, 1, 0)
            c = pl.ds(pl.multiple_of(kt * tk, tk), size)
            dkv_ref[seq, :HD, c] += dk
            dkv_ref[seq, HD:, c] += dv

        lax.fori_loop(0, n_full, lambda kt, _: (second(kt), 0)[1], 0)
        last(lambda size: second(n_full, size))
        factors = turn_factors(near_ref[...], far_ref[pl.ds(row0 // M, 1), :])
        for p in range(H // 2):
            z = jnp.where(low_half, dqacc[heads[2 * p], :], pltpu.roll(dqacc[heads[2 * p + 1], :], HD, 1))
            z = (turn_back(z, *factors) * HD ** -0.5).astype(bf16)
            dq_ref[:, p * 128:(p + 1) * 128] = z
            if given_ref is not None:
                @pl.when(taken)
                def _(p=p, z=z):
                    given_ref[0, 1, :, p * 128:(p + 1) * 128] = z

    @pl.when(t == pl.num_programs(0) - 1)
    def _():
        copy = pltpu.make_async_copy(dkv_ref, sums_ref, sum_sem)
        copy.start()
        copy.wait()


def attention(tables, q, g, others, skip, kv, M, tk, before=None):
    width = H * HD
    steps = tables[0].shape[0]
    own = q.shape[0] // M
    parts, S, block, _ = kv.shape
    L = parts * block
    near, far = turn_tables(L, M)
    whole = pl.Buffered(1)
    tile = pl.BlockSpec((M, width), lambda t, slot, *_: (jnp.minimum(slot[t], own), 0))
    near_spec = pl.BlockSpec(near.shape, lambda t, *_: (0, 0), pipeline_mode=whole)
    far_spec = pl.BlockSpec(far.shape, lambda t, *_: (0, 0), pipeline_mode=whole)
    mine = pl.BlockSpec((M, width), lambda t, slot, *_: (jnp.minimum(slot[t], own - 1), 0))
    taken = pl.BlockSpec((1, 2, M, width), lambda t, slot, *_: (jnp.maximum(slot[t] - own - skip, 0), 0, 0, 0))
    anywhere = pl.BlockSpec(memory_space=pl.ANY)
    bf16, f32 = jnp.bfloat16, jnp.float32
    pairs = steps * M * H * L // 3
    kernel = functools.partial(attn_kernel, M, tk, own, before is None)
    operands, specs = [q, g], [mine, mine]
    if others is None:
        inner = kernel
        kernel = lambda a, b, c, d, q_ref, g_ref, *refs: inner(a, b, c, d, q_ref, g_ref, None, *refs)
    else:
        operands, specs = operands + [others], specs + [taken]
    operands += [near, far, kv]
    specs += [near_spec, far_spec, pl.BlockSpec(kv.shape, lambda t, *_: (0, 0, 0, 0), pipeline_mode=whole)]
    aliases = {}
    if before is not None:
        aliases = {4 + len(operands) + i: i for i in range(3)}
        operands, specs = operands + list(before), specs + [anywhere] * 3
    slots = jax.ShapeDtypeStruct(((own + 1) * M, width), bf16)
    out_shape, out_specs = [slots, slots, jax.ShapeDtypeStruct((S, 128, L), f32)], [tile, tile, anywhere]
    if others is not None:
        count = others.shape[0]
        out_shape.append(jax.ShapeDtypeStruct(others.shape, bf16))
        out_specs.append(pl.BlockSpec(
            (1, 2, M, width),
            lambda t, slot, *_: (jnp.where(slot[t] < own, count - 1, jnp.minimum(slot[t] - own - skip, count - 1)), 0, 0, 0)))
    return pl.pallas_call(
        kernel,
        grid_spec=pltpu.PrefetchScalarGridSpec(
            num_scalar_prefetch=4,
            grid=(steps,),
            in_specs=specs,
            out_specs=out_specs,
            scratch_shapes=[
                pltpu.VMEM((S, L, 128), bf16),
                pltpu.VMEM((S, L, 128), bf16),
                pltpu.VMEM((H * M, 128), bf16),
                pltpu.VMEM((H * M, 128), bf16),
                pltpu.VMEM((128, H * M), bf16),
                pltpu.VMEM((128, H * M), bf16),
                pltpu.VMEM((L // tk, H * M, tk), bf16),
                pltpu.VMEM((H * M, 128), f32),
                pltpu.VMEM((H * M, 128), f32),
                pltpu.VMEM((H * M, 128), f32),
                pltpu.VMEM((H * M, 128), f32),
                pltpu.VMEM((S, 128, L), f32),
                pltpu.SMEM((1,), f32),
                pltpu.SemaphoreType.DMA,
            ],
        ),
        out_shape=out_shape,
        input_output_aliases=aliases,
        compiler_params=pltpu.CompilerParams(vmem_limit_bytes=58 << 20),
        cost_estimate=pl.CostEstimate(flops=1 << 20, bytes_accessed=1 << 16, transcendentals=0),
        name="attention",
    )(*tables, *operands)


MESH = pl.DeviceIdType.MESH


def bits_of(n_seq, n_rows):
    high = [("seq", 1 << b) for b in reversed(range(n_seq.bit_length() - 1))]
    return high + [("rows", 1 << b) for b in reversed(range(n_rows.bit_length() - 1))]


def place(bits):
    return [lax.rem(lax.axis_index(axis) // weight, 2) for axis, weight in bits]


def partner(bit):
    axis, weight = bit
    mine = lax.axis_index(axis)
    return {axis: mine + weight - 2 * weight * lax.rem(mine // weight, 2)}


def greet(bits):
    barrier = pltpu.get_barrier_semaphore()
    for bit in bits:
        pl.semaphore_signal(barrier, inc=1, device_id=partner(bit), device_id_type=MESH)
    pl.semaphore_wait(barrier, len(bits))


def routes(bits):
    n = len(bits)
    one = list(range(n))
    other = list(range(n))
    near = max(i for i in range(n) if bits[i][0] == "seq")
    if near + 1 < n - 1:
        other[near], other[near + 1] = other[near + 1], other[near]
    return one, other


def gelu_both(x):
    z = jnp.abs(x) * 0.7071067811865476
    s = 1.0 / (1.0 + 0.3275911 * z)
    poly = s * (0.127414796 + s * (-0.142248368 + s * (0.710706871 + s * (-0.7265760135 + s * 0.5307027145))))
    bell = jnp.exp(-z * z)
    tail = poly * bell
    phi = jnp.where(x >= 0.0, 1.0 - tail, tail)
    return x * phi, phi + x * (bell * 0.3989422804014327)


def ffn_kernel(C, x_ref, b_ref, up_ref, down_ref, out_ref, dx_ref, gup_ref, gdown_ref, act_s, ug_s):
    f = pl.program_id(0)
    T = x_ref.shape[0]

    @pl.when(f == 0)
    def _():
        out_ref[...] = jnp.zeros_like(out_ref)
        dx_ref[...] = jnp.zeros_like(dx_ref)

    up = up_ref[...]
    down = down_ref[...]
    for c in range(T // C):
        r = slice(c * C, (c + 1) * C)
        u = dot(x_ref[r, :], up, 1, 0)
        a = dot(b_ref[r, :], down, 1, 1)
        act, slope = gelu_both(u)
        act = act.astype(jnp.bfloat16)
        ug = (a * slope).astype(jnp.bfloat16)
        act_s[r, :] = act
        ug_s[r, :] = ug
        out_ref[r, :] += dot(act, down, 1, 0)
        dx_ref[r, :] += dot(ug, up, 1, 1)
    gup_ref[...] = dot(x_ref[...], ug_s[...], 0, 0).astype(gup_ref.dtype)
    gdown_ref[...] = dot(act_s[...], b_ref[...], 0, 0).astype(gdown_ref.dtype)


def ffn(x, b, up, down, F=512, C=256, wire=jnp.bfloat16):
    T, D = x.shape
    FF = up.shape[1]
    C = min(C, T)
    f32, bf16 = jnp.float32, jnp.bfloat16
    whole = lambda f: (0, 0)
    return pl.pallas_call(
        functools.partial(ffn_kernel, C),
        grid=(FF // F,),
        in_specs=[
            pl.BlockSpec((T, D), whole, pipeline_mode=pl.Buffered(1)),
            pl.BlockSpec((T, D), whole, pipeline_mode=pl.Buffered(1)),
            pl.BlockSpec((D, F), lambda f: (0, f)),
            pl.BlockSpec((F, D), lambda f: (f, 0)),
        ],
        out_specs=[
            pl.BlockSpec((T, D), whole, pipeline_mode=pl.Buffered(1)),
            pl.BlockSpec((T, D), whole, pipeline_mode=pl.Buffered(1)),
            pl.BlockSpec((D, F), lambda f: (0, f)),
            pl.BlockSpec((F, D), lambda f: (f, 0)),
        ],
        out_shape=[
            jax.ShapeDtypeStruct((T, D), f32),
            jax.ShapeDtypeStruct((T, D), f32),
            jax.ShapeDtypeStruct((D, FF), wire),
            jax.ShapeDtypeStruct((FF, D), wire),
        ],
        scratch_shapes=[pltpu.VMEM((T, F), bf16), pltpu.VMEM((T, F), bf16)],
        compiler_params=pltpu.CompilerParams(vmem_limit_bytes=56 << 20),
        cost_estimate=pl.CostEstimate(flops=12 * T * D * FF, bytes_accessed=32 << 20, transcendentals=T * FF),
        name="feedforward",
    )(x, b, up, down)


def ffn_packed_kernel(
    C, bits, M, order, moved,
    x_ref, b_ref, up_ref, down_ref, kv_ref, q_ref, g_ref,
    out_ref, dx_ref, grads_ref, all_kv, others,
    act_s, ug_s, wide, ups, own_sem, kv_send, kv_recv, tile_send, tile_recv,
):
    f = pl.program_id(0)
    T, D = x_ref.shape
    groups, each, _, count, _ = up_ref.shape
    tiles = ups.shape[0]
    n = groups * each
    owned = D // n
    f32, bf16 = jnp.float32, jnp.bfloat16
    stages = len(bits)
    me = place(bits)
    block = lax.axis_index("seq")
    n_seq = len(moved)
    local = kv_ref.shape[1]

    def kv_copies(stage):
        copies = []
        for half in (0, 1):
            route = list(range(stages)) if half == 0 else [stages - 1] + list(range(stages - 1))
            at = tuple(slice(None) if i in route[:stage] else me[i] for i in range(stages))
            piece = all_kv.at[at + (slice(None), pl.ds(half * (local // 2), local // 2))]
            copies.append(pltpu.make_async_remote_copy(
                src_ref=piece, dst_ref=piece, send_sem=kv_send.at[half, stage], recv_sem=kv_recv.at[half, stage],
                device_id=partner(bits[route[stage]]), device_id_type=MESH))
        return copies

    def tile_copies(k):
        r = pl.ds(order[k] * M, M)
        return [pltpu.make_async_remote_copy(
            src_ref=ref.at[r], dst_ref=others.at[k, i], send_sem=tile_send.at[k, i], recv_sem=tile_recv.at[k, i],
            device_id={"seq": n_seq - 1 - block}, device_id_type=MESH) for i, ref in enumerate((q_ref, g_ref))]

    def among(devices):
        return functools.reduce(jnp.logical_or, [block == i for i in devices])

    @pl.when(f == 0)
    def _():
        own = pltpu.make_async_copy(kv_ref, all_kv.at[tuple(me)], own_sem)
        own.start()
        barrier = pltpu.get_barrier_semaphore()
        for bit in bits:
            pl.semaphore_signal(barrier, inc=1, device_id=partner(bit), device_id_type=MESH)
        pl.semaphore_signal(barrier, inc=1, device_id={"seq": n_seq - 1 - block}, device_id_type=MESH)
        pl.semaphore_wait(barrier, stages + 1)
        own.wait()

    end = 2 * tiles - 1
    when = [min(2 * k - 1, end) if k else 0 for k in range(stages)]
    after = when[-1]

    def progress(point):
        for stage in range(stages):
            if when[stage] == point:
                for copy in kv_copies(stage - 1) if stage else []:
                    copy.wait()
                for copy in kv_copies(stage):
                    copy.start()
        if after == point:
            for k in range(len(order)):
                @pl.when(among([i for i in range(n_seq) if moved[i] > k]))
                def _(k=k):
                    for copy in tile_copies(k):
                        copy.start()

    def progress_at(parity):
        for point in sorted(set(when + [after])):
            if point % 2 == parity:
                @pl.when(f == point // 2)
                def _(point=point):
                    progress(point)

    progress_at(0)

    @pl.when(f == 0)
    def _():
        out_ref[...] = jnp.zeros_like(out_ref)
        dx_ref[...] = jnp.zeros_like(dx_ref)

        def unpack(d, _):
            part = up_ref[d // each, lax.rem(d, each), 0].astype(f32)
            for j in range(tiles):
                at = pl.ds(pl.multiple_of(d * owned, 8), owned)
                wide[j, at, :] = part[j * owned:(j + 1) * owned]
            return 0

        lax.fori_loop(0, n, unpack, 0)
        for j in range(tiles):
            ups[j] = wide[j].astype(bf16)

    up = ups[f]
    down = down_ref[...].reshape(D, D)
    for c in range(T // C):
        if c == T // C // 2:
            progress_at(1)
        r = slice(c * C, (c + 1) * C)
        u = dot(x_ref[r, :], up, 1, 0)
        a = dot(b_ref[r, :], down, 1, 1)
        act, slope = gelu_both(u)
        act = act.astype(bf16)
        ug = (a * slope).astype(bf16)
        act_s[r, :] = act
        ug_s[r, :] = ug
        out_ref[r, :] += dot(act, down, 1, 0)
        dx_ref[r, :] += dot(ug, up, 1, 1)
    wide[f] = dot(x_ref[...], ug_s[...], 0, 0)
    grad_down = dot(act_s[...], b_ref[...], 0, 0).astype(bf16)
    for k in range(each):
        at = f * each + k
        grads_ref[at, count:] = grad_down[k * count:(k + 1) * count]

    @pl.when(f == tiles - 1)
    def _():
        def pack(d, _):
            at = pl.ds(pl.multiple_of(d * owned, 8), owned)
            part = jnp.concatenate([wide[j, at, :] for j in range(tiles)], axis=0)
            grads_ref[d, :count] = part.astype(bf16)
            return 0

        lax.fori_loop(0, n, pack, 0)
        for copy in kv_copies(stages - 1):
            copy.wait()
        for k in range(len(order)):
            @pl.when(among([i for i in range(n_seq) if moved[i] > k]))
            def _(k=k):
                for copy in tile_copies(k):
                    copy.wait_send()

            @pl.when(among([n_seq - 1 - i for i in range(n_seq) if moved[i] > k]))
            def _(k=k):
                for copy in tile_copies(k):
                    copy.wait_recv()


def ffn_packed(x, b, packed, kv, q, g, order, moved, M, n_seq, collective_id, C=256):
    T, D = x.shape
    n, count = packed.shape[0], packed.shape[1] // 2
    FF = n * count
    tiles = FF // D
    each = n // tiles
    packed = packed.reshape(tiles, each, 2, count, D)
    f32, bf16 = jnp.float32, jnp.bfloat16
    once = pl.Buffered(1)
    whole = lambda f: (0, 0)
    bits = bits_of(n_seq, 1)
    anywhere = pl.BlockSpec(memory_space=pl.ANY)
    out, dx, grads, all_kv, others = pl.pallas_call(
        functools.partial(ffn_packed_kernel, C, bits, M, tuple(order), tuple(moved)),
        grid=(tiles,),
        in_specs=[
            pl.BlockSpec((T, D), whole, pipeline_mode=once),
            pl.BlockSpec((T, D), whole, pipeline_mode=once),
            pl.BlockSpec((tiles, each, 1, count, D), lambda f: (0, 0, 0, 0, 0), pipeline_mode=once),
            pl.BlockSpec((1, each, 1, count, D), lambda f: (f, 0, 1, 0, 0)),
            anywhere, anywhere, anywhere,
        ],
        out_specs=[
            pl.BlockSpec((T, D), whole, pipeline_mode=once),
            pl.BlockSpec((T, D), whole, pipeline_mode=once),
            pl.BlockSpec((n, 2 * count, D), lambda f: (0, 0, 0), pipeline_mode=once),
            anywhere, anywhere,
        ],
        out_shape=[
            jax.ShapeDtypeStruct((T, D), f32),
            jax.ShapeDtypeStruct((T, D), f32),
            jax.ShapeDtypeStruct((n, 2 * count, D), bf16),
            jax.ShapeDtypeStruct((2,) * len(bits) + kv.shape, bf16),
            jax.ShapeDtypeStruct((len(order), 2, M, D), bf16),
        ],
        scratch_shapes=[
            pltpu.VMEM((T, D), bf16), pltpu.VMEM((T, D), bf16),
            pltpu.VMEM((tiles, D, D), f32), pltpu.VMEM((tiles, D, D), bf16),
            pltpu.SemaphoreType.DMA,
            pltpu.SemaphoreType.DMA((2, len(bits))), pltpu.SemaphoreType.DMA((2, len(bits))),
            pltpu.SemaphoreType.DMA((len(order), 2)), pltpu.SemaphoreType.DMA((len(order), 2)),
        ],
        compiler_params=pltpu.CompilerParams(
            collective_id=collective_id, has_side_effects=True, vmem_limit_bytes=60 << 20),
        cost_estimate=pl.CostEstimate(flops=1 << 20, bytes_accessed=1 << 16, transcendentals=0),
        name="feedforward",
    )(x, b, packed, packed, kv, q, g)
    return out, dx, grads, all_kv.reshape((n_seq,) + kv.shape), others


def streams_of(bits, squares, hidden):
    n = len(bits)
    one, other = routes(bits)
    near = max(i for i in range(n) if bits[i][0] == "seq")
    last = [i for i in (near, near + 1) if i < n - 1]
    last += [i for i in range(n - 1) if i not in last] + [n - 1]
    early, late = list(range(n)), list(range(2, n + 2))
    split = list(range(2)) + list(range(4, n + 2))
    unit = squares // 48 * 16
    head = hidden // 12 // 16 * 16
    tail = hidden // 6 // 16 * 16
    rest = (hidden - 2 * head - tail) // 2
    return [
        (0, 0, 16, one, early), (0, 16, 16, other, early),
        (1, 0, unit, one, early), (1, unit, squares - unit, other, early),
        (2, 0, head, one, early), (2, head, head, other, early),
        (2, 2 * head, rest, one, late), (2, 2 * head + rest, rest, other, late),
        (2, 2 * head + 2 * rest, tail, last, split),
    ]


def front_kernel(
    bits, here, M, chunk, streams,
    x_ref, c_ref, weight_ref, subset_ref, ga_ref, sa_ref, gf_ref, sf_ref, near_ref, far_ref, query_ref, pair_ref, output_ref, up_ref, down_ref,
    q_ref, g_ref, kv_ref, xa_ref, xf_ref, b_ref, wide_ref, wp, hidden_ref,
    pr_all, sq_all, hidden_own, stage_q, stage_o, stage_p,
    own_sem, send_sem, recv_sem,
):
    f32, bf16 = jnp.float32, jnp.bfloat16
    T, D = x_ref.shape
    n = len(bits)
    me = place(bits)
    owned = query_ref.shape[0]
    tiles = up_ref.shape[1] // D
    rows = hidden_own.shape[0] // 2
    up = up_ref[...].astype(f32)
    hidden_own[:rows, :] = jnp.concatenate([up[:, j * D:(j + 1) * D] for j in range(tiles)], axis=0).astype(bf16)
    hidden_own[rows:, :] = down_ref[...]
    own = pltpu.make_async_copy(hidden_own, hidden_ref.at[tuple(me)], own_sem)
    own.start()
    squares = jnp.concatenate([query_ref[...].astype(f32), output_ref[...].astype(f32)], axis=0)
    sq_all[tuple(me)] = squares.astype(bf16)
    pairs = jnp.concatenate([pair_ref[...].astype(f32), jnp.zeros((pr_all.shape[-2] - owned, 128), f32)], axis=0)
    pr_all[tuple(me)] = pairs.astype(bf16)
    greet(bits)
    own.wait()

    gains = [ref[...].reshape(1, D) for ref in (ga_ref, sa_ref, gf_ref, sf_ref)]

    def normalize(i):
        r = slice(i * chunk, (i + 1) * chunk)
        x = x_ref[r, :].astype(f32)
        x = x - jnp.mean(x, axis=1, keepdims=True)
        unit = x * lax.rsqrt(jnp.mean(x * x, axis=1, keepdims=True) + 1e-05)
        xa_ref[r, :] = (unit * gains[0] + gains[1]).astype(bf16)
        xf_ref[r, :] = (unit * gains[2] + gains[3]).astype(bf16)
        part = i * chunk // (T // here)
        b_ref[r, :] = (c_ref[r, :].astype(f32) * weight_ref[subset_ref[part]]).astype(bf16)

    def unpack():
        for d in range(1 << n):
            at = tuple((d >> (n - 1 - i)) & 1 for i in range(n))
            r = slice(d * owned, (d + 1) * owned)
            both = sq_all[at].astype(f32)
            stage_q[r, :] = both[:owned]
            stage_o[r, :] = both[owned:2 * owned]
            stage_p[r, :] = pr_all[at].astype(f32)[:owned]
        wp[...] = stage_p[...].astype(bf16)
        wide_ref[0] = stage_q[...].astype(bf16)
        wide_ref[1] = stage_o[...].astype(bf16)

    block = lax.axis_index("seq")
    per = T // here // M
    tables = []
    for j in range(per):
        tables.append(turn_factors(near_ref[...], far_ref[pl.ds(block * per + j, 1), :]))
    first = lax.broadcasted_iota(jnp.int32, (M, 128), 1) < HD

    def keys(i):
        r = slice(i * chunk, (i + 1) * chunk)
        kv = dot(xa_ref[r, :], wp[...], 1, 0)
        for j in range(chunk // M):
            part = kv[j * M:(j + 1) * M]
            turned = turn(part, *tables[(i * chunk // M + j) % per])
            kv_ref[i * chunk + j * M:i * chunk + (j + 1) * M, :] = jnp.where(first, turned, part).astype(bf16)

    def queries(i):
        r = slice(i * chunk, (i + 1) * chunk)
        z = dot(xa_ref[r, :], wide_ref[0], 1, 0)
        for j in range(chunk // M):
            tab = tables[(i * chunk // M + j) % per]
            for p in range(D // 128):
                c = slice(p * 128, (p + 1) * 128)
                part = turn(z[j * M:(j + 1) * M, c], *tab) * (HD ** -0.5 / LN2)
                q_ref[i * chunk + j * M:i * chunk + (j + 1) * M, c] = part.astype(bf16)

    def gradients(i):
        r = slice(i * chunk, (i + 1) * chunk)
        g_ref[r, :] = dot(b_ref[r, :], wide_ref[1], 1, 1).astype(bf16)

    chunks = T // chunk
    rounds = max(s[4][-1] for s in streams) + 1
    jobs = [[] for _ in range(rounds)]
    for i in range(chunks):
        jobs[min(i, n - 1)].append(functools.partial(normalize, i))
    jobs[min(n, rounds - 1)] += [unpack] + [functools.partial(f, i) for f in (keys, queries, gradients) for i in range(chunks)]
    arrays = (pr_all, sq_all, hidden_ref)
    held = [set() for _ in streams]
    for now in range(rounds):
        copies = []
        for i, (a, start, size, order, when) in enumerate(streams):
            if now not in when:
                continue
            stage = when.index(now)
            where = tuple(slice(None) if b in held[i] else me[b] for b in range(n))
            piece = arrays[a].at[where + (pl.ds(start, size),)]
            copy = pltpu.make_async_remote_copy(
                src_ref=piece, dst_ref=piece, send_sem=send_sem.at[i, stage], recv_sem=recv_sem.at[i, stage],
                device_id=partner(bits[order[stage]]), device_id_type=MESH)
            copy.start()
            copies.append(copy)
            held[i].add(order[stage])
        for job in jobs[now]:
            job()
        for copy in copies:
            copy.wait()


def front(x, c, weights, subsets, norms, query, pair, output, up, down, here, length, M, n_seq, n_rows, collective_id, chunk=256):
    bits = bits_of(n_seq, n_rows)
    n = len(bits)
    T, D = x.shape
    owned, hidden = query.shape[0], 2 * down.shape[0]
    f32, bf16 = jnp.float32, jnp.bfloat16
    near, far = turn_tables(length, M)
    vmem = pl.BlockSpec(memory_space=pltpu.VMEM)
    smem = pl.BlockSpec(memory_space=pltpu.SMEM)
    token = jax.ShapeDtypeStruct((T, D), bf16)
    streams = streams_of(bits, 2 * owned, hidden)
    q, g, kv, xa, xf, b, wide, wp, packed = pl.pallas_call(
        functools.partial(front_kernel, bits, here, M, chunk, streams),
        out_shape=[token, token, jax.ShapeDtypeStruct((T, 128), bf16), token, token, token,
                   jax.ShapeDtypeStruct((2, D, D), bf16), jax.ShapeDtypeStruct((D, 128), bf16),
                   jax.ShapeDtypeStruct((2,) * n + (hidden, D), bf16)],
        in_specs=[vmem] * 2 + [smem] * 2 + [vmem] * 11,
        out_specs=[vmem] * 8 + [pl.BlockSpec(memory_space=pl.ANY)],
        scratch_shapes=[
            pltpu.VMEM((2,) * n + (32, 128), bf16),
            pltpu.VMEM((2,) * n + (2 * owned, D), bf16),
            pltpu.VMEM((hidden, D), bf16),
            pltpu.VMEM((D, D), f32),
            pltpu.VMEM((D, D), f32),
            pltpu.VMEM((D, 128), f32),
            pltpu.SemaphoreType.DMA,
            pltpu.SemaphoreType.DMA((len(streams), n)),
            pltpu.SemaphoreType.DMA((len(streams), n)),
        ],
        compiler_params=pltpu.CompilerParams(
            collective_id=collective_id, has_side_effects=True, vmem_limit_bytes=56 << 20),
        name="front",
    )(x, c, weights, subsets, *norms, near, far, query, pair, output, up, down)
    return q, g, kv, xa, xf, b, wide, wp, packed.reshape(1 << n, hidden, D)


class Halving:
    def __init__(self, bits, order, me, first, send, recv, acc, send_sem, recv_sem):
        self.bits, self.order, self.me, self.first = bits, order, me, first
        self.send, self.recv, self.acc = send, recv, acc
        self.send_sem, self.recv_sem = send_sem, recv_sem
        self.copy = None

    def spot(self, stage, j, own):
        left = sorted(self.order[stage:])
        b = self.order[stage]
        rest = [i for i in left if i != b]
        index = 0
        for i in left:
            if i == b:
                bit = self.me[b] if own else 1 - self.me[b]
            else:
                bit = lax.rem(j // (1 << (len(rest) - 1 - rest.index(i))), 2)
            index = index * 2 + bit
        return index

    def block(self, stage, at):
        return self.first(at) if stage == 0 else self.acc[stage - 1][at]

    def start(self, stage):
        def fill(j, _):
            self.send[stage][j] = self.block(stage, self.spot(stage, j, False)).astype(jnp.bfloat16)
            return 0

        lax.fori_loop(0, 1 << (len(self.order) - 1 - stage), fill, 0)
        self.copy = pltpu.make_async_remote_copy(
            src_ref=self.send[stage], dst_ref=self.recv[stage],
            send_sem=self.send_sem.at[stage], recv_sem=self.recv_sem.at[stage],
            device_id=partner(self.bits[self.order[stage]]), device_id_type=MESH)
        self.copy.start()

    def finish(self, stage):
        self.copy.wait()

        def add(j, _):
            own = self.block(stage, self.spot(stage, j, True))
            self.acc[stage][j] = own + self.recv[stage][j].astype(jnp.float32)
            return 0

        lax.fori_loop(0, 1 << (len(self.order) - 1 - stage), add, 0)


def halving_shapes(stages, rows, columns):
    sizes = [(1 << (stages - 1 - s), rows, columns) for s in range(stages)]
    half = [pltpu.VMEM(s, jnp.bfloat16) for s in sizes]
    return half + half + [pltpu.VMEM(s, jnp.float32) for s in sizes] + [
        pltpu.SemaphoreType.DMA((stages,)), pltpu.SemaphoreType.DMA((stages,))]


def post_kernel(bits, here, M, order, moved, counts, chunk, *refs):
    (sums_ref, o_hbm, dq_hbm, *refs) = refs
    backs, refs = refs[:len(counts)], refs[len(counts):]
    backs = [ref.at[k] for ref, count in zip(backs, counts) for k in range(count)]
    (xa_hbm, b_hbm, x_hbm, c_hbm, out_hbm, dx_hbm, wide_hbm, wp_ref, ga_ref, gf_ref, weight_ref, subset_ref, near_ref, far_ref,
     layer_ref, states_ref, square_ref, small_ref, *refs) = refs
    f32, bf16 = jnp.float32, jnp.bfloat16
    T, D = xa_hbm.shape
    n = len(bits)
    seq_bits = [i for i in range(n) if bits[i][0] == "seq"]
    n_s = len(seq_bits)
    me = place(bits)
    o_ref, dq_ref, xa_ref, b_ref, wide_ref, x_ref, c_ref, out_ref, dx_ref, ai_ref, gq, go, gs, inv_ref, load_sem, *refs = refs

    def take(stages):
        nonlocal refs
        mine, refs = refs[:3 * stages + 2], refs[3 * stages + 2:]
        return mine[:stages], mine[stages:2 * stages], mine[2 * stages:3 * stages], mine[-2], mine[-1]

    loads = [pltpu.make_async_copy(s, d, load_sem.at[i])
             for i, (s, d) in enumerate((
                 (dq_hbm.at[:T], dq_ref), (xa_hbm, xa_ref), (o_hbm.at[:T], o_ref), (b_hbm, b_ref), (wide_hbm, wide_ref),
                 (out_hbm, out_ref), (x_hbm, x_ref), (dx_hbm, dx_ref), (c_hbm, c_ref)))]
    for load in loads:
        load.start()
    greet(bits)

    owned = D >> n
    local = T // here
    per = local // M
    wide = sums_ref.shape[2] >> n_s

    def keys_first(s):
        return lambda at: sums_ref[s, :, pl.ds(pl.multiple_of(at * wide, 128), wide)]

    def square_first(ref):
        def get(at):
            r = pl.ds(pl.multiple_of(at * owned, 8), owned)
            return jnp.concatenate([ref[r, :D // 2], ref[r, D // 2:]], axis=0)
        return get

    def small_first(at):
        r = pl.ds(pl.multiple_of(at * owned, 8), owned)
        return jnp.concatenate([gs[r, :128], gs[r, 128:]], axis=0)

    x_first = seq_bits[::-1]
    z_first = x_first[1:] + x_first[:1]
    kv = [Halving(bits, z_first if s % 2 else x_first, me, keys_first(s), *take(n_s)) for s in range(here)]
    routes_back = [list(reversed(o)) for o in routes(bits)]
    squares = [Halving(bits, routes_back[i], me, square_first(ref), *take(n)) for i, ref in enumerate((gq, go))]
    small = Halving(bits, routes_back[0], me, small_first, *take(n))

    for h in kv:
        h.start(0)

    block = lax.axis_index("seq")
    for load in loads[:4]:
        load.wait()
    for k, at in enumerate(order):
        r = slice(at * M, (at + 1) * M)
        away = functools.reduce(jnp.logical_or, [block == i for i in range(len(moved)) if moved[i] > k])
        o_ref[r, :] = jnp.where(away, backs[k][0], o_ref[r, :])
        dq_ref[r, :] = jnp.where(away, backs[k][1], dq_ref[r, :])

    gq[...] = dot(xa_ref[...], dq_ref[...], 0, 0)
    squares[0].start(0)
    go[...] = dot(o_ref[...], b_ref[...], 0, 0)
    squares[1].start(0)
    chunks = T // chunk

    def backward(i):
        r = slice(i * chunk, (i + 1) * chunk)
        ai_ref[r, :] = dot(dq_ref[r, :], wide_ref[0], 1, 1)

    def forward(i):
        r = slice(i * chunk, (i + 1) * chunk)
        total = x_ref[r, :].astype(f32) + (dot(o_ref[r, :], wide_ref[1], 1, 0) + out_ref[r, :])
        layer_ref[r, :] = total.astype(bf16)

    totals = [jnp.zeros((1, D), f32) for _ in range(4)]

    def hidden(i):
        r = slice(i * chunk, (i + 1) * chunk)
        x = x_ref[r, :].astype(f32)
        x = x - jnp.mean(x, axis=1, keepdims=True)
        inverse = lax.rsqrt(jnp.mean(x * x, axis=1, keepdims=True) + 1e-05)
        unit = x * inverse
        fi = dx_ref[r, :]
        totals[2] = totals[2] + jnp.sum(fi * unit, axis=0, keepdims=True)
        totals[3] = totals[3] + jnp.sum(fi, axis=0, keepdims=True)
        dx_ref[r, :] = fi * gf_ref[...].reshape(1, D)
        out_ref[r, :] = unit
        inv_ref[r, :] = inverse

    moved_on = [0]

    def advance():
        stage = moved_on[0]
        moved_on[0] += 1
        for h in squares:
            h.finish(stage)
            if stage + 1 < n:
                h.start(stage + 1)

    loads[4].wait()
    for i in range(chunks):
        backward(i)
    advance()
    for load in loads[5:8]:
        load.wait()
    for i in range(chunks):
        forward(i)
        hidden(i)
    for stage in range(n_s):
        for h in kv:
            h.finish(stage)
            if stage + 1 < n_s:
                h.start(stage + 1)
        if moved_on[0] < n - 1:
            advance()

    first = lax.broadcasted_iota(jnp.int32, (M, 128), 1) < HD
    grads = []
    for s in range(here):
        home = kv[s].acc[n_s - 1][0].T
        for j in range(per):
            factors = turn_factors(near_ref[...], far_ref[pl.ds(block * per + j, 1), :])
            part = home[j * M:(j + 1) * M]
            turned = turn_back(part, *factors) * LN2
            grads.append(jnp.where(first, turned, part).astype(bf16))
    pairs = jnp.concatenate(grads, axis=0)
    gs[:, :128] = dot(xa_ref[...], pairs, 0, 0)
    loads[8].wait()
    for i in range(chunks):
        r = slice(i * chunk, (i + 1) * chunk)
        unit = out_ref[r, :]
        ai = ai_ref[r, :] + dot(pairs[r], wp_ref[...], 1, 1)
        totals[0] = totals[0] + jnp.sum(ai * unit, axis=0, keepdims=True)
        totals[1] = totals[1] + jnp.sum(ai, axis=0, keepdims=True)
        both = ai * ga_ref[...].reshape(1, D) + dx_ref[r, :]
        middle = jnp.mean(both, axis=1, keepdims=True)
        slope = jnp.mean(both * unit, axis=1, keepdims=True)
        up = c_ref[r, :].astype(f32) * weight_ref[subset_ref[i * chunk // local]]
        states_ref[r, :] = (up + inv_ref[r, :] * (both - middle - unit * slope)).astype(bf16)
    rows = jnp.concatenate(totals + [jnp.zeros((124, D), f32)], axis=0)
    gs[:, 128:] = rows.T
    small.start(0)
    while moved_on[0] < n:
        advance()
    for i, h in enumerate(squares):
        total = h.acc[n - 1][0]
        square_ref[i, :, :D // 2] = total[:owned]
        square_ref[i, :, D // 2:] = total[owned:]
    for stage in range(n):
        small.finish(stage)
        if stage + 1 < n:
            small.start(stage + 1)
    total = small.acc[n - 1][0]
    small_ref[:, :128] = total[:owned]
    small_ref[:, 128:] = total[owned:]


def post(sums, o, dq, backs, order, moved, xa, b, x, c, out, dx, wide, wp, norms, weights, subsets,
         here, length, M, n_seq, n_rows, collective_id, chunk=256):
    bits = bits_of(n_seq, n_rows)
    n, n_s = len(bits), n_seq.bit_length() - 1
    T, D = xa.shape
    owned = D >> n
    f32, bf16 = jnp.float32, jnp.bfloat16
    near, far = turn_tables(length, M)
    vmem, anywhere = pl.BlockSpec(memory_space=pltpu.VMEM), pl.BlockSpec(memory_space=pl.ANY)
    smem = pl.BlockSpec(memory_space=pltpu.SMEM)
    token = jax.ShapeDtypeStruct((T, D), bf16)
    scratch = [
        *[pltpu.VMEM((T, D), bf16)] * 4, pltpu.VMEM((2, D, D), bf16), *[pltpu.VMEM((T, D), bf16)] * 2,
        *[pltpu.VMEM((T, D), f32)] * 3,
        pltpu.VMEM((D, D), f32), pltpu.VMEM((D, D), f32), pltpu.VMEM((D, 256), f32),
        pltpu.VMEM((T, 1), f32), pltpu.SemaphoreType.DMA((9,)),
    ]
    for _ in range(here):
        scratch += halving_shapes(n_s, 128, length // n_seq)
    for _ in range(2):
        scratch += halving_shapes(n, 2 * owned, D // 2)
    scratch += halving_shapes(n, 2 * owned, 128)
    return pl.pallas_call(
        functools.partial(post_kernel, bits, here, M, tuple(order), tuple(moved), tuple(b.shape[0] for b in backs), chunk),
        out_shape=[token, token, jax.ShapeDtypeStruct((2, owned, D), f32), jax.ShapeDtypeStruct((owned, 256), f32)],
        in_specs=[vmem, anywhere, anywhere] + [vmem] * len(backs) + [anywhere] * 7 + [vmem] * 3 + [smem] * 2 + [vmem] * 2,
        out_specs=[vmem] * 4,
        scratch_shapes=scratch,
        compiler_params=pltpu.CompilerParams(
            collective_id=collective_id, has_side_effects=True, vmem_limit_bytes=60 << 20),
        name="post",
    )(sums, o, dq, *backs, xa, b, x, c, out, dx, wide, wp, norms[0], norms[2], weights, subsets, near, far)


def layer_norm(values):
    center = values - jnp.mean(values, axis=-1, keepdims=True)
    inverse = lax.rsqrt(jnp.mean(center * center, axis=-1, keepdims=True) + 1e-05)
    return center * inverse, inverse


def norm_back(incoming, normed, inverse, gain):
    scaled = incoming * gain
    return inverse * (
        scaled
        - jnp.mean(scaled, axis=-1, keepdims=True)
        - normed * jnp.mean(scaled * normed, axis=-1, keepdims=True)
    )


def rotary_tables(positions):
    half_rot = ROT // 2
    frequency = 10000.0 ** (-2.0 * jnp.arange(half_rot, dtype=jnp.float32) / ROT)
    angles = positions[:, None] * frequency[None, :]
    cosine = jnp.concatenate([jnp.cos(angles), jnp.cos(angles)], axis=-1)
    sine_vals = jnp.concatenate([jnp.sin(angles), jnp.sin(angles)], axis=-1)
    return (cosine, sine_vals)


def rotate(vector, cosine, sine_vals):
    half_rot = ROT // 2
    rotary_part = vector[..., :ROT]
    turned = jnp.concatenate([-rotary_part[..., half_rot:], rotary_part[..., :half_rot]], axis=-1)
    return jnp.concatenate([rotary_part * cosine + turned * sine_vals, vector[..., ROT:]], axis=-1)


def plan(n, here, per, M, tk):
    order = [(s, j) for j in reversed(range(per)) for s in range(here)]
    row = lambda i, j: (i * per + j) * M
    price = lambda first: first // tk + (0.5 if first % tk + M <= tk // 2 else 1.0) + 1.1
    moved = [0] * n
    for i in range(n // 2, n):
        load = lambda k: max(
            sum(price(row(i, j)) for _, j in order[k:]),
            sum(price(row(n - 1 - i, j)) for _, j in order) + sum(price(row(i, j)) for _, j in order[:k]))
        moved[i] = min(range(len(order)), key=load)
    most = max(moved)
    takes = [[(here * per + k, s, row(n - 1 - i, j)) for k, (s, j) in enumerate(order[:moved[n - 1 - i]])] if i < n // 2 else []
             for i in range(n)]
    keeps = [[(s * per + j, s, row(i, j)) for s, j in order[moved[i]:]] for i in range(n)]
    cost = lambda steps: sum(price(x[2]) for x in steps)
    mean = sum(cost(t) + cost(k) for t, k in zip(takes, keeps)) / n
    lists = ([], [], [])
    for take, keep in zip(takes, keeps):
        ahead = 0.32 if take else 0.24
        keep, head, middle = list(keep), list(take[:1]), list(take[1:])
        while len(keep) > 1 and cost(head) + price(keep[0][2]) / 2 < ahead * mean:
            head.append(keep.pop(0))
        while len(keep) > 1 and cost(middle) + price(keep[0][2]) / 2 < 0.2 * mean:
            middle.append(keep.pop(0))
        for part, steps in zip(lists, (head, middle, keep)):
            part.append(steps)
    tables = []
    for part in lists:
        size = max(1, max(len(w) for w in part))
        full = [[x + (1,) for x in w] + [(w[-1] if w else (0, 0, 0)) + (0,)] * (size - len(w)) for w in part]
        tables.append(np.array(full, np.int32))
    return order, moved, most, tables


def local(
    mesh, states, cotangent, subsets, subset_weight, gain_attn, shift_attn, gain_ffn, shift_ffn,
    query_projection, pair_projection, output_projection, up_projection, down_projection,
):
    f32, bf16 = jnp.float32, jnp.bfloat16
    both = ("seq", "rows")
    here, length_here, D = states.shape
    T = here * length_here
    n_seq, n_rows = mesh.shape["seq"], mesh.shape["rows"]
    n = n_seq * n_rows
    length = length_here * n_seq
    block = lax.axis_index("seq")
    offset = block * length_here
    M = min(128, length_here)
    per = length_here // M
    tk = min(512, length)
    FF = up_projection.shape[1]
    P = 2 * HD
    scale = HD ** -0.5
    own_rows = query_projection.shape[0]
    aligned = own_rows % 8 == 0 and here % 2 == 0

    rows_here = offset + jnp.arange(length_here, dtype=jnp.int32)
    cosine, sine_vals = rotary_tables(rows_here.astype(f32))
    if aligned:
        norms = (gain_attn, shift_attn, gain_ffn, shift_ffn)
        queries, out_grad, own_kv, attention_input, feedforward_input, branch_grad, wide, full_pair, packed = front(
            states.reshape(T, D), cotangent.reshape(T, D), subset_weight, subsets, norms, query_projection, pair_projection,
            output_projection, up_projection, down_projection, here, length, M, n_seq, n_rows, 1)
    else:
        table_rows = jnp.arange(subset_weight.shape[0], dtype=jnp.int32)
        row_scale = jnp.sum(
            jnp.where(table_rows[None, :] == subsets[:, None], subset_weight[None, :], 0.0), axis=1
        )
        source = states.astype(f32).reshape(T, D)
        unit, inverse = layer_norm(source)
        upstream = (cotangent.astype(f32) * row_scale[:, None, None]).reshape(T, D)
        big = jnp.stack([up_projection, down_projection.reshape(up_projection.shape)])
        big = lax.all_gather(big, both, axis=1, tiled=True)
        full_up, full_down = big[0], big[1].reshape(FF, D)
        small = jnp.concatenate([query_projection, pair_projection, output_projection], axis=1)
        small = lax.all_gather(small, both, axis=0, tiled=True)
        full_query, full_pair, full_output = small[:, :D], small[:, D:D + P], small[:, D + P:]
        attention_input = (unit * gain_attn + shift_attn).astype(bf16)
        feedforward_input = (unit * gain_ffn + shift_ffn).astype(bf16)
        branch_grad = upstream.astype(bf16)
        pair_pre = jnp.dot(attention_input, full_pair, preferred_element_type=f32)
        pair_pre = pair_pre.reshape(here, length_here, P)
        key_values = jnp.concatenate(
            [rotate(pair_pre[..., :HD], cosine[None], sine_vals[None]), pair_pre[..., HD:]], axis=2
        ).astype(bf16)
        query_pre = jnp.dot(attention_input, full_query, preferred_element_type=f32)
        queries = rotate(
            query_pre.reshape(here, length_here, H, HD) * (scale / LN2),
            cosine[None, :, None, :], sine_vals[None, :, None, :],
        ).astype(bf16).reshape(T, D)
        out_grad = lax.dot_general(
            branch_grad, full_output, (((1,), (1,)), ((), ())), preferred_element_type=f32
        ).astype(bf16)
        all_kv = lax.all_gather(key_values, "seq", axis=0)

    order, moved, most, tables = plan(n_seq, here, per, M, tk)
    own = here * per
    at_slots = [s * per + j for s, j in order[:most]]
    steps = []
    for table in tables:
        mine = jnp.asarray(table)[block]
        steps.append(tuple(mine[:, c] for c in range(4)))
    q_tiles, g_tiles = queries.reshape(own, M, D), out_grad.reshape(own, M, D)

    def send(tiles):
        pairs_of = [(i, n_seq - 1 - i) for i in range(n_seq) if moved[i] > tiles[0]]
        return lax.ppermute(
            jnp.stack([jnp.stack([q_tiles[at_slots[k]], g_tiles[at_slots[k]]]) for k in tiles]), "seq", pairs_of)

    def send_back(given, first):
        return lax.ppermute(given, "seq", [(n_seq - 1 - i, i) for i in range(n_seq) if moved[i] > first])

    if aligned:
        ffn_out, ffn_input_grad, ffn_grads, all_kv, first_taken = ffn_packed(
            feedforward_input, branch_grad, packed, own_kv.reshape(here, length_here, P), queries, out_grad,
            at_slots[:1], moved, M, n_seq, 3)
    else:
        first_taken = send([0])
        ffn_out, ffn_input_grad, grad_up, grad_down = ffn(feedforward_input, branch_grad, full_up, full_down)
        ffn_grads = jnp.concatenate([grad_up.reshape(n, -1, D), grad_down.reshape(n, -1, D)], axis=1)
    ffn_grads = lax.psum_scatter(ffn_grads, both, scatter_dimension=0, tiled=True)[0]
    *done, given = attention(steps[0], queries, out_grad, first_taken, 0, all_kv, M, tk)
    backs = [send_back(given, 0)]
    if most > 1:
        *done, given = attention(
            steps[1], queries, out_grad, send(list(range(1, most))), 1, all_kv, M, tk, done)
        backs.append(send_back(given, 1))
    else:
        done = attention(steps[1], queries, out_grad, None, 0, all_kv, M, tk, done)
    half = ffn_grads.shape[0] // 2
    final_up = ffn_grads[:half]
    if aligned:
        final_up = jnp.swapaxes(final_up.reshape(FF // D, own_rows, D), 0, 1)
    final_up = final_up.reshape(-1, FF).astype(f32)
    final_down = ffn_grads[half:].astype(f32)
    attended, query_pre_grad, pair_terms = attention(steps[2], queries, out_grad, None, 0, all_kv, M, tk, done)
    if aligned:
        layer_out, grad_states, squares, small = post(
            pair_terms, attended, query_pre_grad, backs, at_slots, moved, attention_input, branch_grad,
            states.reshape(T, D), cotangent.reshape(T, D), ffn_out, ffn_input_grad, wide, full_pair, norms, subset_weight, subsets,
            here, length, M, n_seq, n_rows, 2)
        vectors = small[:, P:]
        return (
            layer_out.reshape(states.shape), grad_states.reshape(states.shape),
            vectors[:, 0], vectors[:, 1], vectors[:, 2], vectors[:, 3],
            squares[0], small[:, :P], squares[1], final_up, final_down,
        )

    a_own, d_own = list(attended.reshape(-1, M, D)[:own]), list(query_pre_grad.reshape(-1, M, D)[:own])
    count = jnp.asarray(np.array(moved, np.int32))[block]
    for k, back in enumerate(tile for part in backs for tile in part):
        a_own[at_slots[k]] = jnp.where(count > k, back[0], a_own[at_slots[k]])
        d_own[at_slots[k]] = jnp.where(count > k, back[1], d_own[at_slots[k]])
    attended, query_pre_grad = jnp.concatenate(a_own), jnp.concatenate(d_own)

    pair_terms = pair_terms.astype(bf16).reshape(here, P, n_seq, length_here)
    pair_terms = jnp.moveaxis(pair_terms, 2, 0)
    arrived = lax.all_to_all(pair_terms, "seq", split_axis=0, concat_axis=0, tiled=True)
    pair_grad = jnp.swapaxes(arrived.astype(f32).sum(axis=0), 1, 2)

    residual = jnp.dot(attended, full_output, preferred_element_type=f32) + ffn_out
    layer_out = (source + residual).astype(bf16).reshape(here, length_here, D)
    grad_output = lax.dot_general(
        attended, branch_grad, (((0,), (0,)), ((), ())), preferred_element_type=f32)
    grad_query = lax.dot_general(
        attention_input, query_pre_grad, (((0,), (0,)), ((), ())), preferred_element_type=f32)
    attn_input_grad = lax.dot_general(
        query_pre_grad, full_query, (((1,), (1,)), ((), ())), preferred_element_type=f32)

    pair_pre_grad = jnp.concatenate(
        [rotate(pair_grad[..., :HD] * LN2, cosine[None], -sine_vals[None]), pair_grad[..., HD:]], axis=2
    ).reshape(T, P).astype(bf16)
    grad_pair = lax.dot_general(
        attention_input, pair_pre_grad, (((0,), (0,)), ((), ())), preferred_element_type=f32)
    attn_input_grad = attn_input_grad + lax.dot_general(
        pair_pre_grad, full_pair, (((1,), (1,)), ((), ())), preferred_element_type=f32)

    sums = jnp.stack([
        jnp.sum(attn_input_grad * unit, axis=0), jnp.sum(attn_input_grad, axis=0),
        jnp.sum(ffn_input_grad * unit, axis=0), jnp.sum(ffn_input_grad, axis=0)], axis=1)
    grad_states = upstream + norm_back(attn_input_grad, unit, inverse, gain_attn)
    grad_states = grad_states + norm_back(ffn_input_grad, unit, inverse, gain_ffn)
    grad_states = grad_states.astype(bf16).reshape(here, length_here, D)

    last = jnp.concatenate([grad_query, grad_pair, jnp.pad(sums, ((0, 0), (0, 124))), grad_output], axis=1)
    last = lax.psum_scatter(last.astype(bf16), both, scatter_dimension=0, tiled=True).astype(f32)
    vectors = last[:, D + P:]
    at = D + P + 128
    return (
        layer_out, grad_states,
        vectors[:, 0], vectors[:, 1], vectors[:, 2], vectors[:, 3],
        last[:, :D], last[:, D:D + P], last[:, at:at + D], final_up, final_down,
    )


def solution(mesh):
    from jax.sharding import PartitionSpec as P

    blocks, owned = P("rows", "seq", None), P(("seq", "rows"), None)
    vector = P(("seq", "rows"))
    return jax.shard_map(
        functools.partial(local, mesh),
        mesh=mesh,
        in_specs=(blocks, blocks, P("rows"), P(), P(), P(), P(), P()) + (owned,) * 5,
        out_specs=(blocks, blocks) + (vector,) * 4 + (owned,) * 5,
        check_vma=False,
    )
```

```python
import functools
import jax
import jax.numpy as jnp
import numpy as np
from jax import lax
from jax.experimental import pallas as pl
from jax.experimental.pallas import tpu as pltpu

H = 12
HD = 64
LN2 = 0.6931471805599453


def dot(a, b, ca, cb):
    return lax.dot_general(a, b, (((ca,), (cb,)), ((), ())), preferred_element_type=jnp.float32)


def three_parts(x):
    hi = x.astype(jnp.bfloat16)
    rest = x - hi.astype(jnp.float32)
    mid = rest.astype(jnp.bfloat16)
    low = (rest - mid.astype(jnp.float32)).astype(jnp.bfloat16)
    return hi, mid, low


ROT = 16


def turn_tables(length, M):
    frequency = 10000.0 ** (-2.0 * np.arange(ROT // 2) / ROT)
    lanes = np.zeros(HD)
    lanes[:ROT] = np.concatenate([frequency, frequency])
    lanes = np.concatenate([lanes, lanes])

    def table(places):
        angles = places[:, None] * lanes[None, :]
        return np.concatenate([np.cos(angles), np.sin(angles)], axis=1).astype(np.float32)

    return table(np.arange(M)), table(np.arange(0, length, M))


def turn_factors(near, far):
    cn, sn, cf, sf = near[:, :128], near[:, 128:], far[:, :128], far[:, 128:]
    sine = sf * cn + cf * sn
    lane = lax.broadcasted_iota(jnp.int32, sine.shape, 1) & (HD - 1)
    low = jnp.where(lane < ROT // 2, sine, 0.0)
    high = jnp.where((lane >= ROT // 2) & (lane < ROT), sine, 0.0)
    return cf * cn - sf * sn, low, high


def turn(z, cosine, low, high):
    return z * cosine - pltpu.roll(z, 120, 1) * low + pltpu.roll(z, 8, 1) * high


def turn_back(z, cosine, low, high):
    return z * cosine + pltpu.roll(z, 120, 1) * low - pltpu.roll(z, 8, 1) * high


def attn_kernel(
    M, tk, own, first_call,
    block_ref, table_ref,
    q_ref, g_ref, other_ref, near_ref, far_ref, kv_ref, *refs,
):
    if not first_call:
        before_ref, refs = refs[2], refs[3:]
    o_ref, dq_ref, sums_ref, *refs = refs
    given_ref = None
    if other_ref is not None:
        given_ref, *refs = refs
    ka, va, qs, gs, qt, gt, stash, oacc, dqacc, top, delta, dkv_ref, limit, sum_sem, other_sem = refs
    t = pl.program_id(0)
    at = (block_ref[0] * pl.num_programs(0) + t) * 4
    slot, seq, row0, on = (table_ref[at + i] for i in range(4))
    G = 4 * M
    groups = [slice(g * G, (g + 1) * G) for g in range(H // 4)]
    heads = [slice(h * M, (h + 1) * M) for h in range(H)]
    f32, bf16 = jnp.float32, jnp.bfloat16
    parts_, count, block, _ = kv_ref.shape

    row_head = lax.broadcasted_iota(jnp.int32, (128, 128), 0) // HD
    spread = (row_head == lax.broadcasted_iota(jnp.int32, (128, 128), 1) // HD).astype(bf16)
    only_keys = (row_head == 0).astype(bf16)

    @pl.when(t == 0)
    def _():
        if first_call:
            dkv_ref[...] = jnp.zeros_like(dkv_ref)
        else:
            pltpu.make_async_copy(before_ref, dkv_ref, sum_sem).start()
        lower = lax.broadcasted_iota(jnp.int32, (block, 128), 1) < HD
        one = jnp.ones((block, 128), bf16)

        def arrange(i, most):
            for s in range(count):
                kv = kv_ref[i, s]
                rows = pl.ds(pl.multiple_of(i * block, block), block)
                ka[s, rows, :] = jnp.where(lower, kv, one)
                va[s, rows, :] = jnp.where(lower, one, kv)
                most = jnp.maximum(most, dot(kv * kv, only_keys, 1, 0))
            return most

        limit[0] = jnp.max(lax.fori_loop(0, parts_, arrange, jnp.zeros((block, 128), f32)))

    def ready():
        for s in range(count):
            @pl.when(s != seq)
            def _(s=s):
                pltpu.make_async_copy(dkv_ref.at[s], sums_ref.at[s], other_sem.at[s]).start()

    @pl.when((on == 0) & (t == pl.num_programs(0) - 1))
    def _():
        ready()

    @pl.when(on != 0)
    def _():
        taken = slot >= own
        q_in = q_ref[...] if other_ref is None else jnp.where(taken, other_ref[0, 0], q_ref[...])
        g_in = g_ref[...] if other_ref is None else jnp.where(taken, other_ref[0, 1], g_ref[...])
        lane = lax.broadcasted_iota(jnp.int32, (M, 128), 1)
        low_half = lane < HD
        most = jnp.zeros((M, 128), f32)
        for p in range(H // 2):
            pair = q_in[:, p * 128:(p + 1) * 128]
            most = jnp.maximum(most, dot(pair * pair, spread, 1, 0))
            pair = pair.astype(f32)
            qs[heads[2 * p], :] = jnp.where(low_half, pair, 0.0).astype(bf16)
            qs[heads[2 * p + 1], :] = jnp.where(low_half, pltpu.roll(pair, HD, 1), 0.0).astype(bf16)
        oacc[...] = jnp.zeros_like(oacc)
        dqacc[...] = jnp.zeros_like(dqacc)
        n_full = row0 // tk

        def keys(ref, kt, size=tk):
            return ref[seq, pl.ds(pl.multiple_of(kt * tk, tk), size), :]

        def allowed(kt, size):
            row = row0 + (lax.broadcasted_iota(jnp.int32, (G, size), 0) & (M - 1))
            col = kt * tk + lax.broadcasted_iota(jnp.int32, (G, size), 1)
            return col <= row

        def scores(kt, r, masked, size=tk):
            s = dot(qs[r, :], keys(ka, kt, size), 1, 1)
            if masked:
                s = jnp.where(allowed(kt, size), s, -1e30)
            return s

        short = row0 + M - n_full * tk <= tk // 2

        def last(step):
            @pl.when(short)
            def _():
                step(tk // 2)

            @pl.when(jnp.logical_not(short))
            def _():
                step(tk)

        @pl.when(jnp.max(most) * limit[0] > 3600.0)
        def _():
            top[...] = jnp.full_like(top, -1e30)

            def peak(kt, masked):
                for r in groups:
                    s = scores(kt, r, masked)
                    part = s[:, :128]
                    for j in range(1, tk // 128):
                        part = jnp.maximum(part, s[:, j * 128:(j + 1) * 128])
                    top[r, :] = jnp.maximum(top[r, :], part)

            lax.fori_loop(0, n_full, lambda kt, _: (peak(kt, False), 0)[1], 0)
            peak(n_full, True)
            for r in heads:
                best = -jnp.max(top[r, :], axis=1, keepdims=True)
                for j, part in enumerate(three_parts(best)):
                    qs[r, HD + j:HD + j + 1] = part

        def first(kt, masked, size=tk):
            v = keys(va, kt, size)
            for r in groups:
                e = jnp.exp2(scores(kt, r, masked, size)).astype(bf16)
                stash[kt, r, :size] = e
                oacc[r, :] += dot(e, v, 1, 0)

        lax.fori_loop(0, n_full, lambda kt, _: (first(kt, False), 0)[1], 0)
        last(lambda size: first(n_full, True, size))

        ones = jnp.ones((3 * 128, 128), bf16)
        for p in range(H // 2):
            grads = g_in[:, p * 128:(p + 1) * 128].astype(f32)
            outs = []
            for h in (2 * p, 2 * p + 1):
                r = heads[h]
                acc = oacc[r, :]
                inverse = pltpu.roll(1.0 / acc, HD, 1)
                out = acc * inverse
                outs.append(out)
                grad = grads if h % 2 == 1 else pltpu.roll(grads, HD, 1)
                low = jnp.where(low_half, 0.0, grad * inverse).astype(bf16).astype(f32)
                delta[r, :] = dot(jnp.concatenate(three_parts(low * out), axis=1), ones, 1, 0)
                gs[r, :] = low.astype(bf16)
            out = jnp.where(low_half, pltpu.roll(outs[0], HD, 1), outs[1]).astype(bf16)
            o_ref[:, p * 128:(p + 1) * 128] = out
            if given_ref is not None:
                @pl.when(taken)
                def _(p=p, out=out):
                    given_ref[0, 0, :, p * 128:(p + 1) * 128] = out
        qt[...] = qs[...].T
        gt[...] = gs[...].T

        if not first_call:
            @pl.when(t == 0)
            def _():
                pltpu.make_async_copy(before_ref, dkv_ref, sum_sem).wait()

        @pl.when(t == pl.num_programs(0) - 1)
        def _():
            ready()

        def second(kt, size=tk):
            k = keys(ka, kt, size)
            v = keys(va, kt, size)
            dk = jnp.zeros((HD, size), f32)
            dv = jnp.zeros((HD, size), f32)
            for r in groups:
                e = stash[kt, r, :size]
                slope = e.astype(f32) * (dot(gs[r, :], v, 1, 1) - jnp.tile(delta[r, :], (1, size // 128)))
                slope = slope.astype(bf16)
                dqacc[r, :] += dot(slope, k, 1, 0)
                dk = dk + dot(qt[:HD, r], slope, 1, 0)
                dv = dv + dot(gt[HD:, r], e, 1, 0)
            c = pl.ds(pl.multiple_of(kt * tk, tk), size)
            dkv_ref[seq, :HD, c] += dk
            dkv_ref[seq, HD:, c] += dv

        lax.fori_loop(0, n_full, lambda kt, _: (second(kt), 0)[1], 0)
        last(lambda size: second(n_full, size))
        factors = turn_factors(near_ref[...], far_ref[pl.ds(row0 // M, 1), :])
        for p in range(H // 2):
            z = jnp.where(low_half, dqacc[heads[2 * p], :], pltpu.roll(dqacc[heads[2 * p + 1], :], HD, 1))
            z = (turn_back(z, *factors) * HD ** -0.5).astype(bf16)
            dq_ref[:, p * 128:(p + 1) * 128] = z
            if given_ref is not None:
                @pl.when(taken)
                def _(p=p, z=z):
                    given_ref[0, 1, :, p * 128:(p + 1) * 128] = z

    @pl.when(t == pl.num_programs(0) - 1)
    def _():
        copy = pltpu.make_async_copy(dkv_ref.at[seq], sums_ref.at[seq], sum_sem)
        copy.start()
        copy.wait()
        for s in range(count):
            @pl.when(s != seq)
            def _(s=s):
                pltpu.make_async_copy(dkv_ref.at[s], sums_ref.at[s], other_sem.at[s]).wait()


def attention(place_of, table, q, g, others, skip, kv, M, tk, before=None):
    width = H * HD
    steps = table.shape[1]
    slot_of = lambda t, block, table: table[(block[0] * steps + t) * 4]
    own = q.shape[0] // M
    parts, S, block, _ = kv.shape
    L = parts * block
    near, far = turn_tables(L, M)
    whole = pl.Buffered(1)
    tile = pl.BlockSpec((M, width), lambda t, *s: (jnp.minimum(slot_of(t, *s), own), 0))
    near_spec = pl.BlockSpec(near.shape, lambda t, *_: (0, 0), pipeline_mode=whole)
    far_spec = pl.BlockSpec(far.shape, lambda t, *_: (0, 0), pipeline_mode=whole)
    mine = pl.BlockSpec((M, width), lambda t, *s: (jnp.minimum(slot_of(t, *s), own - 1), 0))
    taken = pl.BlockSpec((1, 2, M, width), lambda t, *s: (jnp.maximum(slot_of(t, *s) - own - skip, 0), 0, 0, 0))
    anywhere = pl.BlockSpec(memory_space=pl.ANY)
    bf16, f32 = jnp.bfloat16, jnp.float32
    pairs = steps * M * H * L // 3
    kernel = functools.partial(attn_kernel, M, tk, own, before is None)
    operands, specs = [q, g], [mine, mine]
    if others is None:
        inner = kernel
        kernel = lambda a, b, q_ref, g_ref, *refs: inner(a, b, q_ref, g_ref, None, *refs)
    else:
        operands, specs = operands + [others], specs + [taken]
    operands += [near, far, kv]
    specs += [near_spec, far_spec, pl.BlockSpec(kv.shape, lambda t, *_: (0, 0, 0, 0), pipeline_mode=whole)]
    aliases = {}
    if before is not None:
        aliases = {2 + len(operands) + i: i for i in range(3)}
        operands, specs = operands + list(before), specs + [anywhere] * 3
    slots = jax.ShapeDtypeStruct(((own + 1) * M, width), bf16)
    out_shape, out_specs = [slots, slots, jax.ShapeDtypeStruct((S, 128, L), f32)], [tile, tile, anywhere]
    if others is not None:
        count = others.shape[0]
        out_shape.append(jax.ShapeDtypeStruct(others.shape, bf16))
        out_specs.append(pl.BlockSpec(
            (1, 2, M, width),
            lambda t, *s: (jnp.where(
                slot_of(t, *s) < own, count - 1, jnp.minimum(slot_of(t, *s) - own - skip, count - 1)), 0, 0, 0)))
    return pl.pallas_call(
        kernel,
        grid_spec=pltpu.PrefetchScalarGridSpec(
            num_scalar_prefetch=2,
            grid=(steps,),
            in_specs=specs,
            out_specs=out_specs,
            scratch_shapes=[
                pltpu.VMEM((S, L, 128), bf16),
                pltpu.VMEM((S, L, 128), bf16),
                pltpu.VMEM((H * M, 128), bf16),
                pltpu.VMEM((H * M, 128), bf16),
                pltpu.VMEM((128, H * M), bf16),
                pltpu.VMEM((128, H * M), bf16),
                pltpu.VMEM((L // tk, H * M, tk), bf16),
                pltpu.VMEM((H * M, 128), f32),
                pltpu.VMEM((H * M, 128), f32),
                pltpu.VMEM((H * M, 128), f32),
                pltpu.VMEM((H * M, 128), f32),
                pltpu.VMEM((S, 128, L), f32),
                pltpu.SMEM((1,), f32),
                pltpu.SemaphoreType.DMA,
                pltpu.SemaphoreType.DMA((S,)),
            ],
        ),
        out_shape=out_shape,
        input_output_aliases=aliases,
        compiler_params=pltpu.CompilerParams(vmem_limit_bytes=58 << 20),
        cost_estimate=pl.CostEstimate(flops=1 << 20, bytes_accessed=1 << 16, transcendentals=0),
        name="attention",
    )(place_of, jnp.asarray(table.reshape(-1)), *operands)


MESH = pl.DeviceIdType.MESH


def bits_of(n_seq, n_rows):
    high = [("seq", 1 << b) for b in reversed(range(n_seq.bit_length() - 1))]
    return high + [("rows", 1 << b) for b in reversed(range(n_rows.bit_length() - 1))]


def place(bits):
    return [lax.rem(lax.axis_index(axis) // weight, 2) for axis, weight in bits]


def partner(bit):
    axis, weight = bit
    mine = lax.axis_index(axis)
    return {axis: mine + weight - 2 * weight * lax.rem(mine // weight, 2)}


def greet(bits):
    barrier = pltpu.get_barrier_semaphore()
    for bit in bits:
        pl.semaphore_signal(barrier, inc=1, device_id=partner(bit), device_id_type=MESH)
    pl.semaphore_wait(barrier, len(bits))


def routes(bits):
    n = len(bits)
    one = list(range(n))
    other = list(range(n))
    near = max(i for i in range(n) if bits[i][0] == "seq")
    if near + 1 < n - 1:
        other[near], other[near + 1] = other[near + 1], other[near]
    return one, other


def gelu_both(x):
    z = jnp.abs(x) * 0.7071067811865476
    s = 1.0 / (1.0 + 0.3275911 * z)
    poly = s * (0.127414796 + s * (-0.142248368 + s * (0.710706871 + s * (-0.7265760135 + s * 0.5307027145))))
    bell = jnp.exp(-z * z)
    tail = poly * bell
    phi = jnp.where(x >= 0.0, 1.0 - tail, tail)
    return x * phi, phi + x * (bell * 0.3989422804014327)


def ffn_kernel(C, x_ref, b_ref, up_ref, down_ref, out_ref, dx_ref, gup_ref, gdown_ref, act_s, ug_s):
    f = pl.program_id(0)
    T = x_ref.shape[0]

    @pl.when(f == 0)
    def _():
        out_ref[...] = jnp.zeros_like(out_ref)
        dx_ref[...] = jnp.zeros_like(dx_ref)

    up = up_ref[...]
    down = down_ref[...]
    for c in range(T // C):
        r = slice(c * C, (c + 1) * C)
        u = dot(x_ref[r, :], up, 1, 0)
        a = dot(b_ref[r, :], down, 1, 1)
        act, slope = gelu_both(u)
        act = act.astype(jnp.bfloat16)
        ug = (a * slope).astype(jnp.bfloat16)
        act_s[r, :] = act
        ug_s[r, :] = ug
        out_ref[r, :] += dot(act, down, 1, 0)
        dx_ref[r, :] += dot(ug, up, 1, 1)
    gup_ref[...] = dot(x_ref[...], ug_s[...], 0, 0).astype(gup_ref.dtype)
    gdown_ref[...] = dot(act_s[...], b_ref[...], 0, 0).astype(gdown_ref.dtype)


def ffn(x, b, up, down, F=512, C=256, wire=jnp.bfloat16):
    T, D = x.shape
    FF = up.shape[1]
    C = min(C, T)
    f32, bf16 = jnp.float32, jnp.bfloat16
    whole = lambda f: (0, 0)
    return pl.pallas_call(
        functools.partial(ffn_kernel, C),
        grid=(FF // F,),
        in_specs=[
            pl.BlockSpec((T, D), whole, pipeline_mode=pl.Buffered(1)),
            pl.BlockSpec((T, D), whole, pipeline_mode=pl.Buffered(1)),
            pl.BlockSpec((D, F), lambda f: (0, f)),
            pl.BlockSpec((F, D), lambda f: (f, 0)),
        ],
        out_specs=[
            pl.BlockSpec((T, D), whole, pipeline_mode=pl.Buffered(1)),
            pl.BlockSpec((T, D), whole, pipeline_mode=pl.Buffered(1)),
            pl.BlockSpec((D, F), lambda f: (0, f)),
            pl.BlockSpec((F, D), lambda f: (f, 0)),
        ],
        out_shape=[
            jax.ShapeDtypeStruct((T, D), f32),
            jax.ShapeDtypeStruct((T, D), f32),
            jax.ShapeDtypeStruct((D, FF), wire),
            jax.ShapeDtypeStruct((FF, D), wire),
        ],
        scratch_shapes=[pltpu.VMEM((T, F), bf16), pltpu.VMEM((T, F), bf16)],
        compiler_params=pltpu.CompilerParams(vmem_limit_bytes=56 << 20),
        cost_estimate=pl.CostEstimate(flops=12 * T * D * FF, bytes_accessed=32 << 20, transcendentals=T * FF),
        name="feedforward",
    )(x, b, up, down)


def ffn_packed_kernel(
    C, bits, M, order, moved,
    x_ref, b_ref, up_ref, down_ref, kv_ref, q_ref, g_ref,
    out_ref, dx_ref, grads_ref, all_kv, others,
    act_s, ug_s, wide, ups, own_sem, kv_send, kv_recv, tile_send, tile_recv,
):
    f = pl.program_id(0)
    T, D = x_ref.shape
    groups, each, _, count, _ = up_ref.shape
    tiles = ups.shape[0]
    n = groups * each
    owned = D // n
    f32, bf16 = jnp.float32, jnp.bfloat16
    stages = len(bits)
    me = place(bits)
    block = lax.axis_index("seq")
    n_seq = len(moved)
    local = kv_ref.shape[1]

    def kv_copies(stage):
        copies = []
        for half in (0, 1):
            route = list(range(stages)) if half == 0 else [stages - 1] + list(range(stages - 1))
            at = tuple(slice(None) if i in route[:stage] else me[i] for i in range(stages))
            piece = all_kv.at[at + (slice(None), pl.ds(half * (local // 2), local // 2))]
            copies.append(pltpu.make_async_remote_copy(
                src_ref=piece, dst_ref=piece, send_sem=kv_send.at[half, stage], recv_sem=kv_recv.at[half, stage],
                device_id=partner(bits[route[stage]]), device_id_type=MESH))
        return copies

    def tile_copies(k):
        r = pl.ds(order[k] * M, M)
        return [pltpu.make_async_remote_copy(
            src_ref=ref.at[r], dst_ref=others.at[k, i], send_sem=tile_send.at[k, i], recv_sem=tile_recv.at[k, i],
            device_id={"seq": n_seq - 1 - block}, device_id_type=MESH) for i, ref in enumerate((q_ref, g_ref))]

    def among(devices):
        return functools.reduce(jnp.logical_or, [block == i for i in devices])

    @pl.when(f == 0)
    def _():
        own = pltpu.make_async_copy(kv_ref, all_kv.at[tuple(me)], own_sem)
        own.start()
        barrier = pltpu.get_barrier_semaphore()
        for bit in bits:
            pl.semaphore_signal(barrier, inc=1, device_id=partner(bit), device_id_type=MESH)
        pl.semaphore_signal(barrier, inc=1, device_id={"seq": n_seq - 1 - block}, device_id_type=MESH)
        pl.semaphore_wait(barrier, stages + 1)
        own.wait()

    end = 2 * tiles - 1
    when = [min(2 * k - 1, end) if k else 0 for k in range(stages)]
    after = when[-1]

    def progress(point):
        for stage in range(stages):
            if when[stage] == point:
                for copy in kv_copies(stage - 1) if stage else []:
                    copy.wait()
                for copy in kv_copies(stage):
                    copy.start()
        if after == point:
            for k in range(len(order)):
                @pl.when(among([i for i in range(n_seq) if moved[i] > k]))
                def _(k=k):
                    for copy in tile_copies(k):
                        copy.start()

    def progress_at(parity):
        for point in sorted(set(when + [after])):
            if point % 2 == parity:
                @pl.when(f == point // 2)
                def _(point=point):
                    progress(point)

    progress_at(0)

    @pl.when(f == 0)
    def _():
        out_ref[...] = jnp.zeros_like(out_ref)
        dx_ref[...] = jnp.zeros_like(dx_ref)

        def unpack(d, _):
            part = up_ref[d // each, lax.rem(d, each), 0].astype(f32)
            for j in range(tiles):
                at = pl.ds(pl.multiple_of(d * owned, 8), owned)
                wide[j, at, :] = part[j * owned:(j + 1) * owned]
            return 0

        lax.fori_loop(0, n, unpack, 0)
        for j in range(tiles):
            ups[j] = wide[j].astype(bf16)

    up = ups[f]
    down = down_ref[...].reshape(D, D)
    for c in range(T // C):
        if c == T // C // 2:
            progress_at(1)
        r = slice(c * C, (c + 1) * C)
        u = dot(x_ref[r, :], up, 1, 0)
        a = dot(b_ref[r, :], down, 1, 1)
        act, slope = gelu_both(u)
        act = act.astype(bf16)
        ug = (a * slope).astype(bf16)
        act_s[r, :] = act
        ug_s[r, :] = ug
        out_ref[r, :] += dot(act, down, 1, 0)
        dx_ref[r, :] += dot(ug, up, 1, 1)
    wide[f] = dot(x_ref[...], ug_s[...], 0, 0)
    grad_down = dot(act_s[...], b_ref[...], 0, 0).astype(bf16)
    for k in range(each):
        at = f * each + k
        grads_ref[at, count:] = grad_down[k * count:(k + 1) * count]

    @pl.when(f == tiles - 1)
    def _():
        def pack(d, _):
            at = pl.ds(pl.multiple_of(d * owned, 8), owned)
            part = jnp.concatenate([wide[j, at, :] for j in range(tiles)], axis=0)
            grads_ref[d, :count] = part.astype(bf16)
            return 0

        lax.fori_loop(0, n, pack, 0)
        for copy in kv_copies(stages - 1):
            copy.wait()
        for k in range(len(order)):
            @pl.when(among([i for i in range(n_seq) if moved[i] > k]))
            def _(k=k):
                for copy in tile_copies(k):
                    copy.wait_send()

            @pl.when(among([n_seq - 1 - i for i in range(n_seq) if moved[i] > k]))
            def _(k=k):
                for copy in tile_copies(k):
                    copy.wait_recv()


def ffn_packed(x, b, packed, kv, q, g, order, moved, M, n_seq, collective_id, C=256):
    T, D = x.shape
    n, count = packed.shape[0], packed.shape[1] // 2
    FF = n * count
    tiles = FF // D
    each = n // tiles
    packed = packed.reshape(tiles, each, 2, count, D)
    f32, bf16 = jnp.float32, jnp.bfloat16
    once = pl.Buffered(1)
    whole = lambda f: (0, 0)
    bits = bits_of(n_seq, 1)
    anywhere = pl.BlockSpec(memory_space=pl.ANY)
    out, dx, grads, all_kv, others = pl.pallas_call(
        functools.partial(ffn_packed_kernel, C, bits, M, tuple(order), tuple(moved)),
        grid=(tiles,),
        in_specs=[
            pl.BlockSpec((T, D), whole, pipeline_mode=once),
            pl.BlockSpec((T, D), whole, pipeline_mode=once),
            pl.BlockSpec((tiles, each, 1, count, D), lambda f: (0, 0, 0, 0, 0), pipeline_mode=once),
            pl.BlockSpec((1, each, 1, count, D), lambda f: (f, 0, 1, 0, 0)),
            anywhere, anywhere, anywhere,
        ],
        out_specs=[
            pl.BlockSpec((T, D), whole, pipeline_mode=once),
            pl.BlockSpec((T, D), whole, pipeline_mode=once),
            pl.BlockSpec((n, 2 * count, D), lambda f: (0, 0, 0), pipeline_mode=once),
            anywhere, anywhere,
        ],
        out_shape=[
            jax.ShapeDtypeStruct((T, D), f32),
            jax.ShapeDtypeStruct((T, D), f32),
            jax.ShapeDtypeStruct((n, 2 * count, D), bf16),
            jax.ShapeDtypeStruct((2,) * len(bits) + kv.shape, bf16),
            jax.ShapeDtypeStruct((len(order), 2, M, D), bf16),
        ],
        scratch_shapes=[
            pltpu.VMEM((T, D), bf16), pltpu.VMEM((T, D), bf16),
            pltpu.VMEM((tiles, D, D), f32), pltpu.VMEM((tiles, D, D), bf16),
            pltpu.SemaphoreType.DMA,
            pltpu.SemaphoreType.DMA((2, len(bits))), pltpu.SemaphoreType.DMA((2, len(bits))),
            pltpu.SemaphoreType.DMA((len(order), 2)), pltpu.SemaphoreType.DMA((len(order), 2)),
        ],
        compiler_params=pltpu.CompilerParams(
            collective_id=collective_id, has_side_effects=True, vmem_limit_bytes=60 << 20),
        cost_estimate=pl.CostEstimate(flops=1 << 20, bytes_accessed=1 << 16, transcendentals=0),
        name="feedforward",
    )(x, b, packed, packed, kv, q, g)
    return out, dx, grads, all_kv.reshape((n_seq,) + kv.shape), others


def streams_of(bits, squares, hidden):
    n = len(bits)
    one, other = routes(bits)
    near = max(i for i in range(n) if bits[i][0] == "seq")
    last = [i for i in (near, near + 1) if i < n - 1]
    last += [i for i in range(n - 1) if i not in last] + [n - 1]
    early, late = list(range(n)), list(range(2, n + 2))
    split = list(range(2)) + list(range(4, n + 2))
    unit = squares // 48 * 16
    head = hidden // 12 // 16 * 16
    tail = hidden // 6 // 16 * 16
    rest = (hidden - 2 * head - tail) // 2
    return [
        (0, 0, 16, one, early), (0, 16, 16, other, early),
        (1, 0, unit, one, early), (1, unit, squares - unit, other, early),
        (2, 0, head, one, early), (2, head, head, other, early),
        (2, 2 * head, rest, one, late), (2, 2 * head + rest, rest, other, late),
        (2, 2 * head + 2 * rest, tail, last, split),
    ]


def front_kernel(
    bits, here, M, chunk, streams,
    x_ref, c_ref, weight_ref, subset_ref, ga_ref, sa_ref, gf_ref, sf_ref, near_ref, far_ref, query_ref, pair_ref, output_ref, up_ref, down_ref,
    q_ref, g_ref, kv_ref, xa_ref, xf_ref, b_ref, wide_ref, wp, hidden_ref,
    pr_all, sq_all, hidden_own, stage_q, stage_o, stage_p,
    own_sem, send_sem, recv_sem,
):
    f32, bf16 = jnp.float32, jnp.bfloat16
    T, D = x_ref.shape
    n = len(bits)
    me = place(bits)
    owned = query_ref.shape[0]
    tiles = up_ref.shape[1] // D
    rows = hidden_own.shape[0] // 2
    up = up_ref[...].astype(f32)
    hidden_own[:rows, :] = jnp.concatenate([up[:, j * D:(j + 1) * D] for j in range(tiles)], axis=0).astype(bf16)
    hidden_own[rows:, :] = down_ref[...]
    own = pltpu.make_async_copy(hidden_own, hidden_ref.at[tuple(me)], own_sem)
    own.start()
    squares = jnp.concatenate([query_ref[...].astype(f32), output_ref[...].astype(f32)], axis=0)
    sq_all[tuple(me)] = squares.astype(bf16)
    pairs = jnp.concatenate([pair_ref[...].astype(f32), jnp.zeros((pr_all.shape[-2] - owned, 128), f32)], axis=0)
    pr_all[tuple(me)] = pairs.astype(bf16)
    greet(bits)
    own.wait()

    gains = [ref[...].reshape(1, D) for ref in (ga_ref, sa_ref, gf_ref, sf_ref)]

    def normalize(i):
        r = slice(i * chunk, (i + 1) * chunk)
        x = x_ref[r, :].astype(f32)
        x = x - jnp.mean(x, axis=1, keepdims=True)
        unit = x * lax.rsqrt(jnp.mean(x * x, axis=1, keepdims=True) + 1e-05)
        xa_ref[r, :] = (unit * gains[0] + gains[1]).astype(bf16)
        xf_ref[r, :] = (unit * gains[2] + gains[3]).astype(bf16)
        part = i * chunk // (T // here)
        b_ref[r, :] = (c_ref[r, :].astype(f32) * weight_ref[subset_ref[part]]).astype(bf16)

    def unpack():
        for d in range(1 << n):
            at = tuple((d >> (n - 1 - i)) & 1 for i in range(n))
            r = slice(d * owned, (d + 1) * owned)
            both = sq_all[at].astype(f32)
            stage_q[r, :] = both[:owned]
            stage_o[r, :] = both[owned:2 * owned]
            stage_p[r, :] = pr_all[at].astype(f32)[:owned]
        wp[...] = stage_p[...].astype(bf16)
        wide_ref[0] = stage_q[...].astype(bf16)
        wide_ref[1] = stage_o[...].astype(bf16)

    block = lax.axis_index("seq")
    per = T // here // M
    tables = []
    for j in range(per):
        tables.append(turn_factors(near_ref[...], far_ref[pl.ds(block * per + j, 1), :]))
    first = lax.broadcasted_iota(jnp.int32, (M, 128), 1) < HD

    def keys(i):
        r = slice(i * chunk, (i + 1) * chunk)
        kv = dot(xa_ref[r, :], wp[...], 1, 0)
        for j in range(chunk // M):
            part = kv[j * M:(j + 1) * M]
            turned = turn(part, *tables[(i * chunk // M + j) % per])
            kv_ref[i * chunk + j * M:i * chunk + (j + 1) * M, :] = jnp.where(first, turned, part).astype(bf16)

    def queries(i):
        r = slice(i * chunk, (i + 1) * chunk)
        z = dot(xa_ref[r, :], wide_ref[0], 1, 0)
        for j in range(chunk // M):
            tab = tables[(i * chunk // M + j) % per]
            for p in range(D // 128):
                c = slice(p * 128, (p + 1) * 128)
                part = turn(z[j * M:(j + 1) * M, c], *tab) * (HD ** -0.5 / LN2)
                q_ref[i * chunk + j * M:i * chunk + (j + 1) * M, c] = part.astype(bf16)

    def gradients(i):
        r = slice(i * chunk, (i + 1) * chunk)
        g_ref[r, :] = dot(b_ref[r, :], wide_ref[1], 1, 1).astype(bf16)

    chunks = T // chunk
    rounds = max(s[4][-1] for s in streams) + 1
    jobs = [[] for _ in range(rounds)]
    for i in range(chunks):
        jobs[min(i, n - 1)].append(functools.partial(normalize, i))
    jobs[min(n, rounds - 1)] += [unpack] + [functools.partial(f, i) for f in (keys, queries, gradients) for i in range(chunks)]
    arrays = (pr_all, sq_all, hidden_ref)
    held = [set() for _ in streams]
    for now in range(rounds):
        copies = []
        for i, (a, start, size, order, when) in enumerate(streams):
            if now not in when:
                continue
            stage = when.index(now)
            where = tuple(slice(None) if b in held[i] else me[b] for b in range(n))
            piece = arrays[a].at[where + (pl.ds(start, size),)]
            copy = pltpu.make_async_remote_copy(
                src_ref=piece, dst_ref=piece, send_sem=send_sem.at[i, stage], recv_sem=recv_sem.at[i, stage],
                device_id=partner(bits[order[stage]]), device_id_type=MESH)
            copy.start()
            copies.append(copy)
            held[i].add(order[stage])
        for job in jobs[now]:
            job()
        for copy in copies:
            copy.wait()


def front(x, c, weights, subsets, norms, query, pair, output, up, down, here, length, M, n_seq, n_rows, collective_id, chunk=256):
    bits = bits_of(n_seq, n_rows)
    n = len(bits)
    T, D = x.shape
    owned, hidden = query.shape[0], 2 * down.shape[0]
    f32, bf16 = jnp.float32, jnp.bfloat16
    near, far = turn_tables(length, M)
    vmem = pl.BlockSpec(memory_space=pltpu.VMEM)
    smem = pl.BlockSpec(memory_space=pltpu.SMEM)
    token = jax.ShapeDtypeStruct((T, D), bf16)
    streams = streams_of(bits, 2 * owned, hidden)
    q, g, kv, xa, xf, b, wide, wp, packed = pl.pallas_call(
        functools.partial(front_kernel, bits, here, M, chunk, streams),
        out_shape=[token, token, jax.ShapeDtypeStruct((T, 128), bf16), token, token, token,
                   jax.ShapeDtypeStruct((2, D, D), bf16), jax.ShapeDtypeStruct((D, 128), bf16),
                   jax.ShapeDtypeStruct((2,) * n + (hidden, D), bf16)],
        in_specs=[vmem] * 2 + [smem] * 2 + [vmem] * 11,
        out_specs=[vmem] * 8 + [pl.BlockSpec(memory_space=pl.ANY)],
        scratch_shapes=[
            pltpu.VMEM((2,) * n + (32, 128), bf16),
            pltpu.VMEM((2,) * n + (2 * owned, D), bf16),
            pltpu.VMEM((hidden, D), bf16),
            pltpu.VMEM((D, D), f32),
            pltpu.VMEM((D, D), f32),
            pltpu.VMEM((D, 128), f32),
            pltpu.SemaphoreType.DMA,
            pltpu.SemaphoreType.DMA((len(streams), n)),
            pltpu.SemaphoreType.DMA((len(streams), n)),
        ],
        compiler_params=pltpu.CompilerParams(
            collective_id=collective_id, has_side_effects=True, vmem_limit_bytes=56 << 20),
        name="front",
    )(x, c, weights, subsets, *norms, near, far, query, pair, output, up, down)
    return q, g, kv, xa, xf, b, wide, wp, packed.reshape(1 << n, hidden, D)


class Halving:
    def __init__(self, bits, order, me, first, send, recv, acc, send_sem, recv_sem):
        self.bits, self.order, self.me, self.first = bits, order, me, first
        self.send, self.recv, self.acc = send, recv, acc
        self.send_sem, self.recv_sem = send_sem, recv_sem
        self.copy = None

    def spot(self, stage, j, own):
        left = sorted(self.order[stage:])
        b = self.order[stage]
        rest = [i for i in left if i != b]
        index = 0
        for i in left:
            if i == b:
                bit = self.me[b] if own else 1 - self.me[b]
            else:
                bit = lax.rem(j // (1 << (len(rest) - 1 - rest.index(i))), 2)
            index = index * 2 + bit
        return index

    def block(self, stage, at):
        return self.first(at) if stage == 0 else self.acc[stage - 1][at]

    def start(self, stage):
        def fill(j, _):
            self.send[stage][j] = self.block(stage, self.spot(stage, j, False)).astype(jnp.bfloat16)
            return 0

        lax.fori_loop(0, 1 << (len(self.order) - 1 - stage), fill, 0)
        self.copy = pltpu.make_async_remote_copy(
            src_ref=self.send[stage], dst_ref=self.recv[stage],
            send_sem=self.send_sem.at[stage], recv_sem=self.recv_sem.at[stage],
            device_id=partner(self.bits[self.order[stage]]), device_id_type=MESH)
        self.copy.start()

    def finish(self, stage):
        self.copy.wait()

        def add(j, _):
            own = self.block(stage, self.spot(stage, j, True))
            self.acc[stage][j] = own + self.recv[stage][j].astype(jnp.float32)
            return 0

        lax.fori_loop(0, 1 << (len(self.order) - 1 - stage), add, 0)


def halving_shapes(stages, rows, columns):
    sizes = [(1 << (stages - 1 - s), rows, columns) for s in range(stages)]
    half = [pltpu.VMEM(s, jnp.bfloat16) for s in sizes]
    return half + half + [pltpu.VMEM(s, jnp.float32) for s in sizes] + [
        pltpu.SemaphoreType.DMA((stages,)), pltpu.SemaphoreType.DMA((stages,))]


def post_kernel(bits, here, M, order, moved, counts, chunk, *refs):
    (sums_ref, o_hbm, dq_hbm, *refs) = refs
    backs, refs = refs[:len(counts)], refs[len(counts):]
    backs = [ref.at[k] for ref, count in zip(backs, counts) for k in range(count)]
    (xa_hbm, b_hbm, x_hbm, c_hbm, out_hbm, dx_hbm, wide_hbm, wp_ref, ga_ref, gf_ref, weight_ref, subset_ref, near_ref, far_ref,
     layer_ref, states_ref, query_out, output_out, pair_out, vector_out, *refs) = refs
    f32, bf16 = jnp.float32, jnp.bfloat16
    T, D = xa_hbm.shape
    n = len(bits)
    seq_bits = [i for i in range(n) if bits[i][0] == "seq"]
    n_s = len(seq_bits)
    me = place(bits)
    o_ref, dq_ref, xa_ref, b_ref, wide_ref, x_ref, c_ref, out_ref, dx_ref, ai_ref, gq, go, gs, inv_ref, load_sem, *refs = refs

    def take(stages):
        nonlocal refs
        mine, refs = refs[:3 * stages + 2], refs[3 * stages + 2:]
        return mine[:stages], mine[stages:2 * stages], mine[2 * stages:3 * stages], mine[-2], mine[-1]

    loads = [pltpu.make_async_copy(s, d, load_sem.at[i])
             for i, (s, d) in enumerate((
                 (dq_hbm.at[:T], dq_ref), (xa_hbm, xa_ref), (o_hbm.at[:T], o_ref), (b_hbm, b_ref), (wide_hbm, wide_ref),
                 (out_hbm, out_ref), (x_hbm, x_ref), (dx_hbm, dx_ref), (c_hbm, c_ref)))]
    for load in loads:
        load.start()
    greet(bits)

    owned = D >> n
    local = T // here
    per = local // M
    wide = sums_ref.shape[2] >> n_s

    def keys_first(s):
        return lambda at: sums_ref[s, :, pl.ds(pl.multiple_of(at * wide, 128), wide)]

    def square_first(ref):
        def get(at):
            r = pl.ds(pl.multiple_of(at * owned, 8), owned)
            return jnp.concatenate([ref[r, :D // 2], ref[r, D // 2:]], axis=0)
        return get

    def small_first(at):
        r = pl.ds(pl.multiple_of(at * owned, 8), owned)
        return jnp.concatenate([gs[r, :128], gs[r, 128:]], axis=0)

    x_first = seq_bits[::-1]
    z_first = x_first[1:] + x_first[:1]
    kv = [Halving(bits, z_first if s % 2 else x_first, me, keys_first(s), *take(n_s)) for s in range(here)]
    routes_back = [list(reversed(o)) for o in routes(bits)]
    squares = [Halving(bits, routes_back[i], me, square_first(ref), *take(n)) for i, ref in enumerate((gq, go))]
    small = Halving(bits, routes_back[0], me, small_first, *take(n))

    for h in kv:
        h.start(0)

    block = lax.axis_index("seq")
    for load in loads[:4]:
        load.wait()
    for k, at in enumerate(order):
        r = slice(at * M, (at + 1) * M)
        away = functools.reduce(jnp.logical_or, [block == i for i in range(len(moved)) if moved[i] > k])
        o_ref[r, :] = jnp.where(away, backs[k][0], o_ref[r, :])
        dq_ref[r, :] = jnp.where(away, backs[k][1], dq_ref[r, :])

    gq[...] = dot(xa_ref[...], dq_ref[...], 0, 0)
    squares[0].start(0)
    go[...] = dot(o_ref[...], b_ref[...], 0, 0)
    squares[1].start(0)
    chunks = T // chunk

    def backward(i):
        r = slice(i * chunk, (i + 1) * chunk)
        ai_ref[r, :] = dot(dq_ref[r, :], wide_ref[0], 1, 1)

    def forward(i):
        r = slice(i * chunk, (i + 1) * chunk)
        total = x_ref[r, :].astype(f32) + (dot(o_ref[r, :], wide_ref[1], 1, 0) + out_ref[r, :])
        layer_ref[r, :] = total.astype(bf16)

    totals = [jnp.zeros((1, D), f32) for _ in range(4)]

    def hidden(i):
        r = slice(i * chunk, (i + 1) * chunk)
        x = x_ref[r, :].astype(f32)
        x = x - jnp.mean(x, axis=1, keepdims=True)
        inverse = lax.rsqrt(jnp.mean(x * x, axis=1, keepdims=True) + 1e-05)
        unit = x * inverse
        fi = dx_ref[r, :]
        totals[2] = totals[2] + jnp.sum(fi * unit, axis=0, keepdims=True)
        totals[3] = totals[3] + jnp.sum(fi, axis=0, keepdims=True)
        dx_ref[r, :] = fi * gf_ref[...].reshape(1, D)
        out_ref[r, :] = unit
        inv_ref[r, :] = inverse

    moved_on = [0]

    def advance():
        stage = moved_on[0]
        moved_on[0] += 1
        for h in squares:
            h.finish(stage)
            if stage + 1 < n:
                h.start(stage + 1)

    loads[4].wait()
    for i in range(chunks):
        backward(i)
    advance()
    for load in loads[5:8]:
        load.wait()
    for i in range(chunks):
        forward(i)
        hidden(i)
    for stage in range(n_s):
        for h in kv:
            h.finish(stage)
            if stage + 1 < n_s:
                h.start(stage + 1)
        if moved_on[0] < n - 1:
            advance()

    first = lax.broadcasted_iota(jnp.int32, (M, 128), 1) < HD
    grads = []
    for s in range(here):
        home = kv[s].acc[n_s - 1][0].T
        for j in range(per):
            factors = turn_factors(near_ref[...], far_ref[pl.ds(block * per + j, 1), :])
            part = home[j * M:(j + 1) * M]
            turned = turn_back(part, *factors) * LN2
            grads.append(jnp.where(first, turned, part).astype(bf16))
    pairs = jnp.concatenate(grads, axis=0)
    gs[:, :128] = dot(xa_ref[...], pairs, 0, 0)
    loads[8].wait()
    for i in range(chunks):
        r = slice(i * chunk, (i + 1) * chunk)
        unit = out_ref[r, :]
        ai = ai_ref[r, :] + dot(pairs[r], wp_ref[...], 1, 1)
        totals[0] = totals[0] + jnp.sum(ai * unit, axis=0, keepdims=True)
        totals[1] = totals[1] + jnp.sum(ai, axis=0, keepdims=True)
        both = ai * ga_ref[...].reshape(1, D) + dx_ref[r, :]
        middle = jnp.mean(both, axis=1, keepdims=True)
        slope = jnp.mean(both * unit, axis=1, keepdims=True)
        up = c_ref[r, :].astype(f32) * weight_ref[subset_ref[i * chunk // local]]
        states_ref[r, :] = (up + inv_ref[r, :] * (both - middle - unit * slope)).astype(bf16)
    rows = jnp.concatenate(totals + [jnp.zeros((124, D), f32)], axis=0)
    gs[:, 128:] = rows.T
    small.start(0)
    while moved_on[0] < n:
        advance()
    for h, ref in zip(squares, (query_out, output_out)):
        total = h.acc[n - 1][0]
        ref[:, :D // 2] = total[:owned]
        ref[:, D // 2:] = total[owned:]
    for stage in range(n):
        small.finish(stage)
        if stage + 1 < n:
            small.start(stage + 1)
    total = small.acc[n - 1][0]
    pair_out[...] = total[:owned]
    vector_out[...] = total[owned:]


def post(sums, o, dq, backs, order, moved, xa, b, x, c, out, dx, wide, wp, norms, weights, subsets,
         here, length, M, n_seq, n_rows, collective_id, chunk=256):
    bits = bits_of(n_seq, n_rows)
    n, n_s = len(bits), n_seq.bit_length() - 1
    T, D = xa.shape
    owned = D >> n
    f32, bf16 = jnp.float32, jnp.bfloat16
    near, far = turn_tables(length, M)
    vmem, anywhere = pl.BlockSpec(memory_space=pltpu.VMEM), pl.BlockSpec(memory_space=pl.ANY)
    smem = pl.BlockSpec(memory_space=pltpu.SMEM)
    token = jax.ShapeDtypeStruct((T, D), bf16)
    scratch = [
        *[pltpu.VMEM((T, D), bf16)] * 4, pltpu.VMEM((2, D, D), bf16), *[pltpu.VMEM((T, D), bf16)] * 2,
        *[pltpu.VMEM((T, D), f32)] * 3,
        pltpu.VMEM((D, D), f32), pltpu.VMEM((D, D), f32), pltpu.VMEM((D, 256), f32),
        pltpu.VMEM((T, 1), f32), pltpu.SemaphoreType.DMA((9,)),
    ]
    for _ in range(here):
        scratch += halving_shapes(n_s, 128, length // n_seq)
    for _ in range(2):
        scratch += halving_shapes(n, 2 * owned, D // 2)
    scratch += halving_shapes(n, 2 * owned, 128)
    return pl.pallas_call(
        functools.partial(post_kernel, bits, here, M, tuple(order), tuple(moved), tuple(b.shape[0] for b in backs), chunk),
        out_shape=[token, token] + [jax.ShapeDtypeStruct((owned, w), f32) for w in (D, D, 128, 128)],
        in_specs=[vmem, anywhere, anywhere] + [vmem] * len(backs) + [anywhere] * 7 + [vmem] * 3 + [smem] * 2 + [vmem] * 2,
        out_specs=[vmem] * 6,
        scratch_shapes=scratch,
        compiler_params=pltpu.CompilerParams(
            collective_id=collective_id, has_side_effects=True, vmem_limit_bytes=60 << 20),
        name="post",
    )(sums, o, dq, *backs, xa, b, x, c, out, dx, wide, wp, norms[0], norms[2], weights, subsets, near, far)


def layer_norm(values):
    center = values - jnp.mean(values, axis=-1, keepdims=True)
    inverse = lax.rsqrt(jnp.mean(center * center, axis=-1, keepdims=True) + 1e-05)
    return center * inverse, inverse


def norm_back(incoming, normed, inverse, gain):
    scaled = incoming * gain
    return inverse * (
        scaled
        - jnp.mean(scaled, axis=-1, keepdims=True)
        - normed * jnp.mean(scaled * normed, axis=-1, keepdims=True)
    )


def rotary_tables(positions):
    half_rot = ROT // 2
    frequency = 10000.0 ** (-2.0 * jnp.arange(half_rot, dtype=jnp.float32) / ROT)
    angles = positions[:, None] * frequency[None, :]
    cosine = jnp.concatenate([jnp.cos(angles), jnp.cos(angles)], axis=-1)
    sine_vals = jnp.concatenate([jnp.sin(angles), jnp.sin(angles)], axis=-1)
    return (cosine, sine_vals)


def rotate(vector, cosine, sine_vals):
    half_rot = ROT // 2
    rotary_part = vector[..., :ROT]
    turned = jnp.concatenate([-rotary_part[..., half_rot:], rotary_part[..., :half_rot]], axis=-1)
    return jnp.concatenate([rotary_part * cosine + turned * sine_vals, vector[..., ROT:]], axis=-1)


def plan(n, here, per, M, tk):
    order = [(s, j) for j in reversed(range(per)) for s in range(here)]
    row = lambda i, j: (i * per + j) * M
    price = lambda first: first // tk + (0.5 if first % tk + M <= tk // 2 else 1.0) + 1.1
    moved = [0] * n
    for i in range(n // 2, n):
        load = lambda k: max(
            sum(price(row(i, j)) for _, j in order[k:]),
            sum(price(row(n - 1 - i, j)) for _, j in order) + sum(price(row(i, j)) for _, j in order[:k]))
        moved[i] = min(range(len(order)), key=load)
    most = max(moved)
    takes = [[(here * per + k, s, row(n - 1 - i, j)) for k, (s, j) in enumerate(order[:moved[n - 1 - i]])] if i < n // 2 else []
             for i in range(n)]
    keeps = [[(s * per + j, s, row(i, j)) for s, j in order[moved[i]:]] for i in range(n)]
    cost = lambda steps: sum(price(x[2]) for x in steps)
    mean = sum(cost(t) + cost(k) for t, k in zip(takes, keeps)) / n
    lists = ([], [], [])
    for take, keep in zip(takes, keeps):
        ahead = 0.32 if take else 0.24
        keep, head, middle = list(keep), list(take[:1]), list(take[1:])
        while len(keep) > 1 and cost(head) + price(keep[0][2]) / 2 < ahead * mean:
            head.append(keep.pop(0))
        while len(keep) > 1 and cost(middle) + price(keep[0][2]) / 2 < 0.2 * mean:
            middle.append(keep.pop(0))
        for part, steps in zip(lists, (head, middle, keep)):
            part.append(steps)
    tables = []
    for part in lists:
        size = max(1, max(len(w) for w in part))
        full = [[x + (1,) for x in w] + [(w[-1] if w else (0, 0, 0)) + (0,)] * (size - len(w)) for w in part]
        tables.append(np.array(full, np.int32))
    return order, moved, most, tables


def local(
    mesh, states, cotangent, subsets, subset_weight, gain_attn, shift_attn, gain_ffn, shift_ffn,
    query_projection, pair_projection, output_projection, up_projection, down_projection,
):
    f32, bf16 = jnp.float32, jnp.bfloat16
    both = ("seq", "rows")
    here, length_here, D = states.shape
    T = here * length_here
    n_seq, n_rows = mesh.shape["seq"], mesh.shape["rows"]
    n = n_seq * n_rows
    length = length_here * n_seq
    block = lax.axis_index("seq")
    offset = block * length_here
    M = min(128, length_here)
    per = length_here // M
    tk = min(512, length)
    FF = up_projection.shape[1]
    P = 2 * HD
    scale = HD ** -0.5
    own_rows = query_projection.shape[0]
    aligned = own_rows % 8 == 0 and here % 2 == 0

    rows_here = offset + jnp.arange(length_here, dtype=jnp.int32)
    cosine, sine_vals = rotary_tables(rows_here.astype(f32))
    if aligned:
        norms = (gain_attn, shift_attn, gain_ffn, shift_ffn)
        queries, out_grad, own_kv, attention_input, feedforward_input, branch_grad, wide, full_pair, packed = front(
            states.reshape(T, D), cotangent.reshape(T, D), subset_weight, subsets, norms, query_projection, pair_projection,
            output_projection, up_projection, down_projection, here, length, M, n_seq, n_rows, 1)
    else:
        table_rows = jnp.arange(subset_weight.shape[0], dtype=jnp.int32)
        row_scale = jnp.sum(
            jnp.where(table_rows[None, :] == subsets[:, None], subset_weight[None, :], 0.0), axis=1
        )
        source = states.astype(f32).reshape(T, D)
        unit, inverse = layer_norm(source)
        upstream = (cotangent.astype(f32) * row_scale[:, None, None]).reshape(T, D)
        big = jnp.stack([up_projection, down_projection.reshape(up_projection.shape)])
        big = lax.all_gather(big, both, axis=1, tiled=True)
        full_up, full_down = big[0], big[1].reshape(FF, D)
        small = jnp.concatenate([query_projection, pair_projection, output_projection], axis=1)
        small = lax.all_gather(small, both, axis=0, tiled=True)
        full_query, full_pair, full_output = small[:, :D], small[:, D:D + P], small[:, D + P:]
        attention_input = (unit * gain_attn + shift_attn).astype(bf16)
        feedforward_input = (unit * gain_ffn + shift_ffn).astype(bf16)
        branch_grad = upstream.astype(bf16)
        pair_pre = jnp.dot(attention_input, full_pair, preferred_element_type=f32)
        pair_pre = pair_pre.reshape(here, length_here, P)
        key_values = jnp.concatenate(
            [rotate(pair_pre[..., :HD], cosine[None], sine_vals[None]), pair_pre[..., HD:]], axis=2
        ).astype(bf16)
        query_pre = jnp.dot(attention_input, full_query, preferred_element_type=f32)
        queries = rotate(
            query_pre.reshape(here, length_here, H, HD) * (scale / LN2),
            cosine[None, :, None, :], sine_vals[None, :, None, :],
        ).astype(bf16).reshape(T, D)
        out_grad = lax.dot_general(
            branch_grad, full_output, (((1,), (1,)), ((), ())), preferred_element_type=f32
        ).astype(bf16)
        all_kv = lax.all_gather(key_values, "seq", axis=0)

    order, moved, most, tables = plan(n_seq, here, per, M, tk)
    own = here * per
    at_slots = [s * per + j for s, j in order[:most]]
    here_at = block.reshape(1).astype(jnp.int32)
    q_tiles, g_tiles = queries.reshape(own, M, D), out_grad.reshape(own, M, D)

    def send(tiles):
        pairs_of = [(i, n_seq - 1 - i) for i in range(n_seq) if moved[i] > tiles[0]]
        return lax.ppermute(
            jnp.stack([jnp.stack([q_tiles[at_slots[k]], g_tiles[at_slots[k]]]) for k in tiles]), "seq", pairs_of)

    def send_back(given, first):
        return lax.ppermute(given, "seq", [(n_seq - 1 - i, i) for i in range(n_seq) if moved[i] > first])

    if aligned:
        ffn_out, ffn_input_grad, ffn_grads, all_kv, first_taken = ffn_packed(
            feedforward_input, branch_grad, packed, own_kv.reshape(here, length_here, P), queries, out_grad,
            at_slots[:1], moved, M, n_seq, 3)
    else:
        first_taken = send([0])
        ffn_out, ffn_input_grad, grad_up, grad_down = ffn(feedforward_input, branch_grad, full_up, full_down)
        ffn_grads = jnp.concatenate([grad_up.reshape(n, -1, D), grad_down.reshape(n, -1, D)], axis=1)
    ffn_grads = lax.psum_scatter(ffn_grads, both, scatter_dimension=0, tiled=True)[0]
    *done, given = attention(here_at, tables[0], queries, out_grad, first_taken, 0, all_kv, M, tk)
    backs = [send_back(given, 0)]
    if most > 1:
        *done, given = attention(
            here_at, tables[1], queries, out_grad, send(list(range(1, most))), 1, all_kv, M, tk, done)
        backs.append(send_back(given, 1))
    else:
        done = attention(here_at, tables[1], queries, out_grad, None, 0, all_kv, M, tk, done)
    half = ffn_grads.shape[0] // 2
    final_up = ffn_grads[:half]
    if aligned:
        final_up = jnp.swapaxes(final_up.reshape(FF // D, own_rows, D), 0, 1)
    final_up = final_up.reshape(-1, FF).astype(f32)
    final_down = ffn_grads[half:].astype(f32)
    attended, query_pre_grad, pair_terms = attention(here_at, tables[2], queries, out_grad, None, 0, all_kv, M, tk, done)
    if aligned:
        layer_out, grad_states, grad_query, grad_output, grad_pair, vectors = post(
            pair_terms, attended, query_pre_grad, backs, at_slots, moved, attention_input, branch_grad,
            states.reshape(T, D), cotangent.reshape(T, D), ffn_out, ffn_input_grad, wide, full_pair, norms, subset_weight, subsets,
            here, length, M, n_seq, n_rows, 2)
        return (
            layer_out.reshape(states.shape), grad_states.reshape(states.shape),
            vectors[:, 0], vectors[:, 1], vectors[:, 2], vectors[:, 3],
            grad_query, grad_pair, grad_output, final_up, final_down,
        )

    a_own, d_own = list(attended.reshape(-1, M, D)[:own]), list(query_pre_grad.reshape(-1, M, D)[:own])
    count = jnp.asarray(np.array(moved, np.int32))[block]
    for k, back in enumerate(tile for part in backs for tile in part):
        a_own[at_slots[k]] = jnp.where(count > k, back[0], a_own[at_slots[k]])
        d_own[at_slots[k]] = jnp.where(count > k, back[1], d_own[at_slots[k]])
    attended, query_pre_grad = jnp.concatenate(a_own), jnp.concatenate(d_own)

    pair_terms = pair_terms.astype(bf16).reshape(here, P, n_seq, length_here)
    pair_terms = jnp.moveaxis(pair_terms, 2, 0)
    arrived = lax.all_to_all(pair_terms, "seq", split_axis=0, concat_axis=0, tiled=True)
    pair_grad = jnp.swapaxes(arrived.astype(f32).sum(axis=0), 1, 2)

    residual = jnp.dot(attended, full_output, preferred_element_type=f32) + ffn_out
    layer_out = (source + residual).astype(bf16).reshape(here, length_here, D)
    grad_output = lax.dot_general(
        attended, branch_grad, (((0,), (0,)), ((), ())), preferred_element_type=f32)
    grad_query = lax.dot_general(
        attention_input, query_pre_grad, (((0,), (0,)), ((), ())), preferred_element_type=f32)
    attn_input_grad = lax.dot_general(
        query_pre_grad, full_query, (((1,), (1,)), ((), ())), preferred_element_type=f32)

    pair_pre_grad = jnp.concatenate(
        [rotate(pair_grad[..., :HD] * LN2, cosine[None], -sine_vals[None]), pair_grad[..., HD:]], axis=2
    ).reshape(T, P).astype(bf16)
    grad_pair = lax.dot_general(
        attention_input, pair_pre_grad, (((0,), (0,)), ((), ())), preferred_element_type=f32)
    attn_input_grad = attn_input_grad + lax.dot_general(
        pair_pre_grad, full_pair, (((1,), (1,)), ((), ())), preferred_element_type=f32)

    sums = jnp.stack([
        jnp.sum(attn_input_grad * unit, axis=0), jnp.sum(attn_input_grad, axis=0),
        jnp.sum(ffn_input_grad * unit, axis=0), jnp.sum(ffn_input_grad, axis=0)], axis=1)
    grad_states = upstream + norm_back(attn_input_grad, unit, inverse, gain_attn)
    grad_states = grad_states + norm_back(ffn_input_grad, unit, inverse, gain_ffn)
    grad_states = grad_states.astype(bf16).reshape(here, length_here, D)

    last = jnp.concatenate([grad_query, grad_pair, jnp.pad(sums, ((0, 0), (0, 124))), grad_output], axis=1)
    last = lax.psum_scatter(last.astype(bf16), both, scatter_dimension=0, tiled=True).astype(f32)
    vectors = last[:, D + P:]
    at = D + P + 128
    return (
        layer_out, grad_states,
        vectors[:, 0], vectors[:, 1], vectors[:, 2], vectors[:, 3],
        last[:, :D], last[:, D:D + P], last[:, at:at + D], final_up, final_down,
    )


def solution(mesh):
    from jax.sharding import PartitionSpec as P

    blocks, owned = P("rows", "seq", None), P(("seq", "rows"), None)
    vector = P(("seq", "rows"))
    return jax.shard_map(
        functools.partial(local, mesh),
        mesh=mesh,
        in_specs=(blocks, blocks, P("rows"), P(), P(), P(), P(), P()) + (owned,) * 5,
        out_specs=(blocks, blocks) + (vector,) * 4 + (owned,) * 5,
        check_vma=False,
    )
```
